32 devices in a mesh: grp: 4 (over z), gy: 2 (over y), gx: 4 (over x, core).
Axes of the slice: x: 2, y: 2, z: 4, core: 2. Of those that a mesh axis runs over, the one named last changes fastest.
Arguments:
- residual: float32 [64, 32, 512], P('grp', 'gy', 'gx'), may hold values from -6 to 6
- mobility: float32 [64, 32, 512], P('grp', 'gy', 'gx'), may hold values from 0.1 to 10
Outputs:
- correction: float32 [64, 32, 512], P('grp', 'gy', 'gx')
The draws below stay inside these ranges and needn't reach their ends.
All inputs are finite; a program needn't handle non-finite values.
Results may differ from the reference program's by a relative error of at most 0.0001.
Values sent between devices are 32-bit elements; how exact they have to be, the bound alone decides.
No kernel may reach another device: no remote copies, remote signals or barrier semaphores. Data moves between devices by JAX's collectives and lax.ppermute only.
A program may use at most 64 MiB of HBM per device.

```python
import math
import jax
import jax.numpy as jnp

LEVELS = 5
SWEEPS = 2
COARSE = 8
NZ = 64
NY = 32
NX = 512


def block_scale(stream_key, dims, cuts, smallest, top_value):
    loudness = 1.0
    for position, parts in cuts:
        steps = jax.random.uniform(jax.random.fold_in(jax.random.fold_in(stream_key, 6), position), (parts,), jnp.float32, smallest / len(cuts), top_value / len(cuts))
        loudness = loudness * jnp.repeat(jnp.exp(steps), dims[position] // parts).reshape((-1,) + (1,) * (len(dims) - 1 - position))
    return loudness


def normal_values(key, extent, deviation, most, split=(), held_as=jnp.bfloat16):
    array = jax.random.normal(key, extent, jnp.float32) * deviation
    if len(split) > 0:
        array = block_scale(key, extent, split, -0.22, 0.18) * array
    return jnp.clip(array, min=-most, max=most).astype(held_as)


def setup_inputs(seed: int = 0) -> dict:
    keys = jax.random.split(jax.random.key(seed), 3)
    residual = normal_values(keys[0], (NZ, NY, NX), 1.0, 6.0, ((0, 4), (1, 2), (2, 4)), jnp.float32)
    mobility = jnp.clip(jnp.exp(math.log(10.0) - 4.6051702 * jax.random.uniform(keys[1], (NZ, NY, NX), jnp.float32) ** block_scale(keys[1], (NZ, NY, NX), ((0, 4), (1, 2), (2, 4)), -0.2, 0.2)), 0.1, 10.0)
    return dict(residual=residual, mobility=mobility)


RELAX_WEIGHT = 0.8


def interior(values):
    return values[1:-1, 1:-1, 1:-1]


def neighbours(padded):
    return (padded[:-2, 1:-1, 1:-1], padded[1:-1, :-2, 1:-1], padded[1:-1, 1:-1, :-2],
            padded[2:, 1:-1, 1:-1], padded[1:-1, 2:, 1:-1], padded[1:-1, 1:-1, 2:])


def face_coefficients(padded_mobility):
    centre = interior(padded_mobility)
    weights = tuple(0.5 * (centre + neighbour) for neighbour in neighbours(padded_mobility))
    diagonal = weights[0] + weights[1] + weights[2] + weights[3] + weights[4] + weights[5]
    return weights, diagonal


def operate(padded, weights, diagonal, factor):
    summed = diagonal * interior(padded)
    for weight, neighbour in zip(weights, neighbours(padded)):
        summed = summed - weight * neighbour
    return factor * summed


def relaxed(padded, source, weights, diagonal, factor):
    return interior(padded) + RELAX_WEIGHT * (source - operate(padded, weights, diagonal, factor)) / (factor * diagonal)


def restrict(values):
    shaped = values.reshape(values.shape[0] // 2, 2, values.shape[1] // 2, 2, values.shape[2] // 2, 2)
    return jnp.mean(shaped, axis=(1, 3, 5))


def prolong(values):
    widened = jnp.broadcast_to(values[:, None, :, None, :, None],
                               (values.shape[0], 2, values.shape[1], 2, values.shape[2], 2))
    return widened.reshape(2 * values.shape[0], 2 * values.shape[1], 2 * values.shape[2])


def reference(residual, mobility):
    mobilities = [mobility]
    for grid_level in range(LEVELS):
        mobilities.append(restrict(mobilities[-1]))
    sources = [residual]
    iterates = []
    for grid_level in range(LEVELS):
        factor = 0.25 ** grid_level
        weights, diagonal = face_coefficients(jnp.pad(mobilities[grid_level], 1))
        source = sources[grid_level]
        iterate = RELAX_WEIGHT * source / (factor * diagonal)
        for repeat in range(SWEEPS - 1):
            iterate = relaxed(jnp.pad(iterate, 1), source, weights, diagonal, factor)
        leftover = source - operate(jnp.pad(iterate, 1), weights, diagonal, factor)
        iterates.append(iterate)
        sources.append(restrict(leftover))
    factor = 0.25 ** LEVELS
    weights, diagonal = face_coefficients(jnp.pad(mobilities[LEVELS], 1))
    source = sources[LEVELS]
    iterate = RELAX_WEIGHT * source / (factor * diagonal)
    for repeat in range(COARSE - 1):
        iterate = relaxed(jnp.pad(iterate, 1), source, weights, diagonal, factor)
    for grid_level in range(LEVELS - 1, -1, -1):
        factor = 0.25 ** grid_level
        weights, diagonal = face_coefficients(jnp.pad(mobilities[grid_level], 1))
        iterate = iterates[grid_level] + prolong(iterate)
        for repeat in range(SWEEPS):
            iterate = relaxed(jnp.pad(iterate, 1), sources[grid_level], weights, diagonal, factor)
    return iterate
```

```python
import jax
import jax.numpy as jnp
import numpy as np
from jax import lax
from jax.experimental import pallas as pl
from jax.experimental.pallas import tpu as pltpu
from jax.sharding import PartitionSpec as P

LEVELS = 5
COARSE = 8
AXES = ("grp", "gy", "gx")
F32 = jnp.float32

HALO = 3
ZW = 4 + 2 * HALO
XW = 32 + 2 * HALO
LW = 384
EDGE = 4 * HALO
M_DEEP, M_FAR, R_DEEP, R_FAR = 11, 4, 10, 3
M_EDGE, R_EDGE = 11, 10


def lane_iota(rows=8):
    return lax.broadcasted_iota(jnp.int32, (rows, 128), 1)


def gather(source, index):
    return jnp.take_along_axis(source, index, axis=1, mode="promise_in_bounds")


def spread(source, offset, px):
    rows = source.shape[0]
    return gather(source, (4 * lane_iota(rows) + (px - 4 * offset)) & 127)


def between(low, high, rows=8):
    lane = lane_iota(rows)
    return (lane >= low) & (lane < high)


def table(rows):
    return jnp.asarray(np.repeat(np.stack(rows)[:, None, :], 8, axis=1).astype(np.int32))


def edge_send_rows():
    row = np.zeros(128, np.int64)
    base = 0
    for a, width in ((1, M_EDGE), (0, R_EDGE)):
        for side in (0, 1):
            first = EDGE - width if side == 0 else 0
            for z in range(HALO):
                for k in range(width):
                    row[base] = a * 48 + z * 12 + first + k + (1000 if side else 0)
                    base += 1
    return [row]


def edge_own_rows():
    rows = []
    for side, tiles in ((0, (0, 1)), (1, (1, 2))):
        for tile in tiles:
            row = np.full(128, -1, np.int64)
            for lane in range(128):
                z, x = divmod(128 * tile + lane, XW)
                x = x if side == 0 else x - (XW - HALO)
                if HALO <= z < HALO + 4 and 0 <= x < HALO:
                    row[lane] = (z - HALO) * 12 + 4 * x
            rows.append(row)
    return rows


def edge_far_rows():
    rows = []
    base_of = {(1, 0): 0, (1, 1): 33, (0, 0): 66, (0, 1): 96}
    for tile, first in ((0, 0), (2, HALO + 4)):
        for a, width in ((0, R_EDGE), (1, M_EDGE)):
            row = np.full(128, -1000, np.int64)
            for lane in range(128):
                z, x = divmod(128 * tile + lane, XW)
                if not first <= z < first + HALO:
                    continue
                for side in (0, 1):
                    k = 4 * x if side == 0 else 4 * (x - (XW - HALO))
                    if 0 <= k < EDGE:
                        start = base_of[a, side] + (z - first) * width
                        row[lane] = start + k - (EDGE - width if side == 0 else 0)
            rows.append(row)
    return rows


def coordinate_rows(rows):
    cells = np.arange(LW)
    z, x = cells // XW, cells % XW
    z = np.where(cells < ZW * XW, z, -1000000)
    both = np.stack([z, x])[:, None, :]
    return jnp.asarray(np.repeat(both, rows, axis=1).astype(np.int32))


class Plan:
    def __init__(self, mesh):
        self.counts = tuple(mesh.shape[axis] for axis in AXES)
        self.near = 1 if self.counts[1] == 2 else 2
        self.rows = 16 * (1 + self.near)
        self.cells = self.rows // 4
        self.tile = -(-self.cells // 8) * 8
        self.z_rows = 16 + 8 * self.near
        sizes = [
            M_DEEP * self.z_rows,
            M_FAR * 8 * self.near,
            R_DEEP * self.z_rows,
            R_FAR * 8 * self.near,
            4 * self.rows,
        ]
        self.starts = [sum(sizes[:i]) for i in range(len(sizes))]
        self.payload = sum(sizes)
        self.devices = self.counts[0] * self.counts[1] * self.counts[2]
        self.coarse = (4 * self.counts[0], 4 * self.counts[1], 32 * self.counts[2])

    def pairs(self, swaps):
        out = []
        for index in np.ndindex(*self.counts):
            there = []
            for axis, swap in enumerate(swaps):
                i, n = index[axis], self.counts[axis]
                j = i if swap is None else (i + 1 if i % 2 == swap else i - 1)
                if axis == 2:
                    j = j % n
                there.append(j)
            if all(0 <= j < n for j, n in zip(there, self.counts)):
                out.append(
                    (
                        int(np.ravel_multi_index(index, self.counts)),
                        int(np.ravel_multi_index(there, self.counts)),
                    )
                )
        return out

    def y_places(self):
        iy = lax.axis_index("gy")
        if self.near == 1:
            return 16 * iy, [(1 - iy, 16 * (1 - iy))]
        odd = lax.rem(iy, 2)
        return 16, [(1 - odd, 32 * (1 - odd)), (odd, 32 * odd)]


def is_even(axis):
    return lax.rem(lax.axis_index(axis), 2) == 0


def at(start, size):
    if isinstance(start, int):
        return pl.ds(start, size)
    return pl.ds(pl.multiple_of(start, 8), size)


def edges_kernel(r_ref, m_ref, even_ref, odd_ref):
    even = is_even("gx")
    for pz in range(4):
        for half in range(2):
            to_right = jnp.zeros((8, 128), F32)
            to_left = jnp.zeros((8, 128), F32)
            for a, ref in enumerate((r_ref, m_ref)):
                for z in range(4):
                    cells = ref[4 * z + pz, 8 * half : 8 * half + 8, :]
                    base = a * 48 + z * 12
                    here = between(base, base + EDGE)
                    shift = (base - (128 - EDGE)) % 128
                    to_right = jnp.where(here, pltpu.roll(cells, shift, 1), to_right)
                    to_left = jnp.where(here, pltpu.roll(cells, base, 1), to_left)
            rows = slice(8 * half, 8 * half + 8)
            even_ref[pz, rows, :] = jnp.where(even, to_right, to_left)
            odd_ref[pz, rows, :] = jnp.where(even, to_left, to_right)


def z_pack_kernel(plan, *refs):
    near = plan.near
    tab_ref, r_ref, m_ref = refs[:3]
    beside = [refs[3 + 2 * i : 5 + 2 * i] for i in range(near)]
    edges = [refs[3 + 2 * near + 2 * i : 5 + 2 * near + 2 * i] for i in range(1 + near)]
    outs = refs[-2:]
    own_row, places = plan.y_places()
    x_even = is_even("gx")
    z_even = is_even("grp")
    index = tab_ref[0]
    for swap, out in enumerate(outs):
        top = z_even if swap == 0 else jnp.logical_not(z_even)
        for a, ref, deep, far, start, far_start in (
            (1, m_ref, M_DEEP, M_FAR, plan.starts[0], plan.starts[1]),
            (0, r_ref, R_DEEP, R_FAR, plan.starts[2], plan.starts[3]),
        ):
            for d in range(1, deep + 1):
                plane = jnp.where(top, 16 - d, d - 1)
                row = start + (d - 1) * plan.z_rows
                out[row : row + 16, :] = ref[plane]
                for i, (side, _) in enumerate(places):
                    to = row + 16 + 8 * i
                    out[to : to + 8, :] = beside[i][a][plane, at(8 * (1 - side), 8), :]
                    if d <= far:
                        to = far_start + ((d - 1) * near + i) * 8
                        out[to : to + 8, :] = beside[i][a][plane, at(8 * side, 8), :]
        first = jnp.where(top, 12, 0)
        use_right = index >= 1000
        lanes = jnp.where(use_right, index - 1000, index) + first
        for i in range(1 + near):
            base = own_row if i == 0 else places[i - 1][1]
            even_ref, odd_ref = edges[i]
            for pz in range(4):
                for half in range(2):
                    rows = slice(8 * half, 8 * half + 8)
                    even, odd = even_ref[pz, rows, :], odd_ref[pz, rows, :]
                    left = gather(jnp.where(x_even, odd, even), lanes)
                    right = gather(jnp.where(x_even, even, odd), lanes)
                    to = at(plan.starts[4] + pz * plan.rows + base + 8 * half, 8)
                    out[to, :] = jnp.where(use_right, right, left)


def padded_rows(plan, cells):
    if plan.cells == plan.tile:
        return cells
    return jnp.concatenate(
        [cells, jnp.zeros((plan.tile - plan.cells, cells.shape[1]), F32)], axis=0
    )


def every_fourth(plan, ref, lead, py):
    return padded_rows(plan, ref[(*lead, pl.ds(py, plan.cells, 4), slice(None))])


def own_kernel(plan, *refs):
    near = plan.near
    tab_ref, r_ref, m_ref = refs[:3]
    beside = [refs[3 + 2 * i : 5 + 2 * i] for i in range(near)]
    edges = [refs[3 + 2 * near + 2 * i : 5 + 2 * near + 2 * i] for i in range(1 + near)]
    out, planes, sides = refs[-3:]
    tile = plan.tile
    own_row, places = plan.y_places()
    x_even = is_even("gx")
    blocks = [(own_row, (r_ref, m_ref))] + [(place[1], b) for place, b in zip(places, beside)]
    for i, (base, pair) in enumerate(blocks):
        for a in range(2):
            planes[a, :, at(base, 16), :] = pair[a][...]
        even, odd = edges[i][0][...], edges[i][1][...]
        sides[0, :, at(base, 16), :] = jnp.where(x_even, odd, even)
        sides[1, :, at(base, 16), :] = jnp.where(x_even, even, odd)

    def body(pz, carry):
        for a in range(2):
            for py in range(4):
                cells = [every_fourth(plan, planes, (a, 4 * z + pz), py) for z in range(4)]
                side = [every_fourth(plan, sides, (s, pz), py) for s in range(2)]
                for px in range(4):
                    for t in range(3):
                        value = jnp.zeros((tile, 128), F32)
                        for z in range(4):
                            offset = (z + HALO) * XW + HALO - 128 * t
                            low, high = max(offset, 0), min(offset + 32, 128)
                            if low < high:
                                value = jnp.where(
                                    between(low, high, tile),
                                    spread(cells[z], offset % 32, px),
                                    value,
                                )
                        for s in range(2):
                            if t - s in (0, 1):
                                index = tab_ref[2 * s + t - s]
                                index = jnp.concatenate([index] * (tile // 8), axis=0)
                                lanes = jnp.maximum(index, 0) + (48 * a + px)
                                value = jnp.where(index >= 0, gather(side[s], lanes), value)
                        out[a, pz, py, px, :, 128 * t : 128 * t + 128] = value
        return carry

    lax.fori_loop(0, 4, body, 0)


def inside_mask(plan, coord_ref):
    tile = plan.tile
    z = coord_ref[0] + (4 * lax.axis_index("grp") - HALO)
    x = coord_ref[1] + (32 * lax.axis_index("gx") - HALO)
    mask = (z >= 0) & (z < plan.coarse[0]) & (x >= 0) & (x < plan.coarse[2])
    if plan.near == 2:
        row = lax.broadcasted_iota(jnp.int32, (tile, LW), 0)
        y = row + (4 * lax.axis_index("gy") - 4)
        mask = mask & (row < plan.cells) & (y >= 0) & (y < plan.coarse[1])
    return mask


def roll_lanes(value, shift):
    return pltpu.roll(value, shift % LW, 1)


def fill_rim(plan, ref, n):
    tile = plan.tile
    row = lax.broadcasted_iota(jnp.int32, (tile, LW), 0)

    def body(i, carry):
        for j in range(n):
            ref[0, i + 1, j + 1] = roll_lanes(ref[n, i + 1, j + 1], XW)
            ref[n + 1, i + 1, j + 1] = roll_lanes(ref[1, i + 1, j + 1], -XW)
            up = pltpu.roll(ref[i + 1, n, j + 1], 1, 0)
            down = pltpu.roll(ref[i + 1, 1, j + 1], tile - 1, 0)
            ref[i + 1, 0, j + 1] = jnp.where(row == 0, 0.0, up)
            ref[i + 1, n + 1, j + 1] = jnp.where(row == tile - 1, 0.0, down)
            ref[i + 1, j + 1, 0] = roll_lanes(ref[i + 1, j + 1, n], 1)
            ref[i + 1, j + 1, n + 1] = roll_lanes(ref[i + 1, j + 1, 1], -1)
        return carry

    lax.fori_loop(0, n, body, 0)


def around(ref, a, b, c):
    return (
        ref[a, b + 1, c + 1],
        ref[a + 2, b + 1, c + 1],
        ref[a + 1, b, c + 1],
        ref[a + 1, b + 2, c + 1],
        ref[a + 1, b + 1, c],
        ref[a + 1, b + 1, c + 2],
    )


def pull(m_ref, v_ref, h_ref, a, b, c):
    cells = around(v_ref, a, b, c)
    mobility = around(m_ref, a, b, c)
    total = ((cells[0] + cells[1]) + (cells[2] + cells[3])) + (cells[4] + cells[5])
    products = [m * v for m, v in zip(mobility, cells)]
    other = ((products[0] + products[1]) + (products[2] + products[3])) + (
        products[4] + products[5]
    )
    return h_ref[a, b, c] * (m_ref[a + 1, b + 1, c + 1] * total + other)


def over_pairs(n, step):
    def body(i, carry):
        step(lax.div(i, n), lax.rem(i, n))
        return carry

    lax.fori_loop(0, n * n, body, 0)


def descend(plan, n, factor, inside, m_ref, r_ref, v_ref, w_ref, d_ref, h_ref, e_ref, k_ref):
    fill_rim(plan, m_ref, n)

    def first(a, b):
        for c in range(n):
            s = around(m_ref, a, b, c)
            d = 3.0 * m_ref[a + 1, b + 1, c + 1] + 0.5 * (
                ((s[0] + s[1]) + (s[2] + s[3])) + (s[4] + s[5])
            )
            h = jnp.where(inside, 0.4 / d, 0.0)
            e = (2.0 / factor) * h * r_ref[a, b, c]
            d_ref[a, b, c] = d
            h_ref[a, b, c] = h
            e_ref[a, b, c] = e
            v_ref[a + 1, b + 1, c + 1] = e

    over_pairs(n, first)
    fill_rim(plan, v_ref, n)

    def second(a, b):
        for c in range(n):
            value = 1.2 * e_ref[a, b, c] + pull(m_ref, v_ref, h_ref, a, b, c)
            w_ref[a + 1, b + 1, c + 1] = value
            k_ref[a, b, c] = value

    over_pairs(n, second)
    fill_rim(plan, w_ref, n)


def leftover(factor, m_ref, r_ref, w_ref, d_ref, h_ref, a, b, c):
    away = w_ref[a + 1, b + 1, c + 1] - 1.25 * pull(m_ref, w_ref, h_ref, a, b, c)
    return r_ref[a, b, c] - factor * (d_ref[a, b, c] * away)


def down_kernel(plan, *refs):
    (tab_ref, coord_ref, own_ref, even_ref, odd_ref) = refs[:5]
    chunk, m0_out, h0, e0, k0, m1_out, h1, e1, k1 = refs[5:14]
    m0, r0, v0, w0, d0, m1, r1, v1, w1, d1, planes, sides = refs[14:]
    near, tile = plan.near, plan.tile
    own_row, places = plan.y_places()
    z_even = is_even("grp")
    inside = inside_mask(plan, coord_ref)

    for side in range(2):
        use_even = jnp.logical_not(z_even) if side == 0 else z_even

        def read(rows):
            return jnp.where(use_even, even_ref[rows, :], odd_ref[rows, :])

        for a, deep, far, start, far_start in (
            (1, M_DEEP, M_FAR, plan.starts[0], plan.starts[1]),
            (0, R_DEEP, R_FAR, plan.starts[2], plan.starts[3]),
        ):
            for d in range(1, EDGE + 1):
                plane = EDGE - d if side == 0 else d - 1
                if d > far:
                    planes[side, a, plane] = jnp.zeros((plan.rows, 128), F32)
                if d > deep:
                    continue
                row = start + (d - 1) * plan.z_rows
                planes[side, a, plane, at(own_row, 16), :] = read(slice(row, row + 16))
                for i, (y_side, base) in enumerate(places):
                    row_i = row + 16 + 8 * i
                    planes[side, a, plane, at(base + 8 * (1 - y_side), 8), :] = read(
                        slice(row_i, row_i + 8)
                    )
                    if d <= far:
                        row_i = far_start + ((d - 1) * near + i) * 8
                        planes[side, a, plane, at(base + 8 * y_side, 8), :] = read(
                            slice(row_i, row_i + 8)
                        )
        for pz in range(4):
            row = plan.starts[4] + pz * plan.rows
            sides[side, pz] = read(slice(row, row + plan.rows))

    def place(pz, carry):
        for a in range(2):
            for py in range(4):
                for side, t in ((0, 0), (1, 2)):
                    cells = [
                        every_fourth(plan, planes, (side, a, 4 * z + pz), py)
                        for z in range(HALO)
                    ]
                    edge = every_fourth(plan, sides, (side, pz), py)
                    index = tab_ref[2 * side + a]
                    index = jnp.concatenate([index] * (tile // 8), axis=0)
                    lanes = slice(128 * t, 128 * t + 128)
                    for px in range(4):
                        value = own_ref[a, pz, py, px, :, lanes]
                        for z in range(HALO):
                            offset = (z if side == 0 else z + HALO + 4) * XW + HALO - 128 * t
                            value = jnp.where(
                                between(offset, offset + 32, tile),
                                spread(cells[z], offset % 32, px),
                                value,
                            )
                        from_edge = jnp.clip(index + px, 0, 127)
                        value = jnp.where(index > -100, gather(edge, from_edge), value)
                        value = jnp.where(inside[:, lanes], value, 0.0)
                        if a == 1:
                            m0[pz + 1, py + 1, px + 1, :, lanes] = value
                            m0_out[pz, py, px, :, lanes] = value
                        else:
                            r0[pz, py, px, :, lanes] = value
                for px in range(4):
                    lanes = slice(128, 256)
                    value = jnp.where(inside[:, lanes], own_ref[a, pz, py, px, :, lanes], 0.0)
                    if a == 1:
                        m0[pz + 1, py + 1, px + 1, :, lanes] = value
                        m0_out[pz, py, px, :, lanes] = value
                    else:
                        r0[pz, py, px, :, lanes] = value
        return carry

    lax.fori_loop(0, 4, place, 0)

    descend(plan, 4, 1.0, inside, m0, r0, v0, w0, d0, h0, e0, k0)

    def restrict(a, b):
        for c in range(2):
            rest = jnp.zeros((tile, LW), F32)
            mobility = jnp.zeros((tile, LW), F32)
            for da in range(2):
                for db in range(2):
                    for dc in range(2):
                        i, j, k = 2 * a + da, 2 * b + db, 2 * c + dc
                        rest = rest + leftover(1.0, m0, r0, w0, d0, h0, i, j, k)
                        mobility = mobility + m0[i + 1, j + 1, k + 1]
            r1[a, b, c] = 0.125 * rest
            m1[a + 1, b + 1, c + 1] = 0.125 * mobility
            m1_out[a, b, c] = 0.125 * mobility

    over_pairs(2, restrict)
    descend(plan, 2, 0.25, inside, m1, r1, v1, w1, d1, h1, e1, k1)
    rest = jnp.zeros((tile, LW), F32)
    mobility = jnp.zeros((tile, LW), F32)
    for a in range(2):
        for b in range(2):
            for c in range(2):
                rest = rest + leftover(0.25, m1, r1, w1, d1, h1, a, b, c)
                mobility = mobility + m1[a + 1, b + 1, c + 1]
    both = []
    for total in (rest, mobility):
        packed = jnp.zeros((tile, 128), F32)
        for t in range(3):
            part = 0.125 * total[:, 128 * t : 128 * t + 128]
            for z in range(4):
                offset = (z + HALO) * XW + HALO - 128 * t
                low, high = max(offset, 0), min(offset + 32, 128)
                if low < high:
                    move = 32 * z - offset
                    packed = jnp.where(
                        between(low + move, high + move, tile),
                        pltpu.roll(part, move % 128, 1),
                        packed,
                    )
        both.append(own_rows(plan, packed))
    block = jnp.concatenate(both, axis=0)

    def put(i, carry):
        chunk[i] = block
        return carry

    lax.fori_loop(0, plan.devices, put, 0, unroll=8)


def own_rows(plan, cells):
    if plan.near == 1:
        return jnp.where(lax.axis_index("gy") == 0, cells[0:4], cells[4:8])
    return cells[4:8]


class Level:
    def __init__(self, plan, level):
        self.size = tuple(n >> (level - 2) for n in plan.coarse)
        self.tile = max(8, self.size[1])
        self.shape = (self.size[0], self.tile, 128)
        self.factor = 0.25**level

    def shifts(self, v):
        z, y, x = self.size
        if z > 1:
            none = jnp.zeros((1, self.tile, 128), F32)
            yield jnp.concatenate([none, v[:-1]], axis=0)
            yield jnp.concatenate([v[1:], none], axis=0)
        else:
            yield jnp.zeros_like(v)
            yield jnp.zeros_like(v)
        row = lax.broadcasted_iota(jnp.int32, self.shape, 1)
        lane = lax.broadcasted_iota(jnp.int32, self.shape, 2)
        up, down = pltpu.roll(v, 1, 1), pltpu.roll(v, self.tile - 1, 1)
        if y == self.tile:
            up = jnp.where(row == 0, 0.0, up)
            down = jnp.where(row == self.tile - 1, 0.0, down)
        yield up
        yield down
        left, right = pltpu.roll(v, 1, 2), pltpu.roll(v, 127, 2)
        if x == 128:
            left = jnp.where(lane == 0, 0.0, left)
            right = jnp.where(lane == 127, 0.0, right)
        yield left
        yield right

    def prepare(self, mobility, source):
        z, y, x = self.size
        row = lax.broadcasted_iota(jnp.int32, self.shape, 1)
        lane = lax.broadcasted_iota(jnp.int32, self.shape, 2)
        inside = (row < y) & (lane < x)
        sums = [mobility + near for near in self.shifts(mobility)]
        self.diagonal = 0.5 * (
            ((sums[0] + sums[1]) + (sums[2] + sums[3])) + (sums[4] + sums[5])
        )
        h = jnp.where(inside, 0.4 / self.diagonal, 0.0)
        self.weights = [h * s for s in sums]
        self.first = (2.0 / self.factor) * h * source
        self.source = source

    def pull(self, v):
        t = [w * near for w, near in zip(self.weights, self.shifts(v))]
        return ((t[0] + t[1]) + (t[2] + t[3])) + (t[4] + t[5])

    def relax(self, v):
        return 0.2 * v + self.first + self.pull(v)

    def leftover(self, v):
        return self.source - self.factor * (self.diagonal * (v - 1.25 * self.pull(v)))


def lanes_2d(values, index):
    flat = values.reshape(-1, 128)
    rows = flat.shape[0]
    lane = lax.broadcasted_iota(jnp.int32, (rows, 128), 1)
    return gather(flat, index(lane)).reshape(values.shape)


def coarsen(values, fine, coarse, fine_ref, coarse_ref):
    z, y, x = coarse.size
    tile = fine.tile
    pairs = values.reshape(z, 2, tile, 128)
    fine_ref[0:z] = pairs[:, 0] + pairs[:, 1]
    rows = fine_ref[0:z, pl.ds(0, y, 2), :] + fine_ref[0:z, pl.ds(1, y, 2), :]
    coarse_ref[0:z, 0:y, :] = rows
    full = coarse_ref[0:z]
    full = full + pltpu.roll(full, 127, 2)
    full = lanes_2d(full, lambda lane: (2 * lane) & 127)
    lane = lax.broadcasted_iota(jnp.int32, full.shape, 2)
    return jnp.where(lane < x, 0.125 * full, 0.0)


def refine(values, fine, coarse, fine_ref):
    z, y, x = coarse.size
    wide = lanes_2d(values, lambda lane: lax.shift_right_logical(lane, 1))
    fine_ref[0:z, pl.ds(0, y, 2), :] = wide[:, 0:y]
    fine_ref[0:z, pl.ds(1, y, 2), :] = wide[:, 0:y]
    rows = fine_ref[0:z]
    return jnp.broadcast_to(rows[:, None], (z, 2, fine.tile, 128)).reshape(fine.shape)


def ascend(plan, n, m_ref, h_ref, e_ref, k_ref, below, v_ref, w_ref, emit):
    def start(a, b):
        for c in range(n):
            v_ref[a + 1, b + 1, c + 1] = k_ref[a, b, c] + below(a, b, c)

    over_pairs(n, start)
    fill_rim(plan, v_ref, n)

    def middle(a, b):
        for c in range(n):
            w_ref[a + 1, b + 1, c + 1] = (
                0.2 * v_ref[a + 1, b + 1, c + 1]
                + e_ref[a, b, c]
                + pull(m_ref, v_ref, h_ref, a, b, c)
            )

    over_pairs(n, middle)
    fill_rim(plan, w_ref, n)

    def last(a, b):
        for c in range(n):
            emit(
                a,
                b,
                c,
                0.2 * w_ref[a + 1, b + 1, c + 1]
                + e_ref[a, b, c]
                + pull(m_ref, w_ref, h_ref, a, b, c),
            )

    over_pairs(n, last)


def up_kernel(plan, *refs):
    coord_ref, joined, m0_in, h0, e0, k0, m1_in, h1, e1, k1, out = refs[:11]
    m0, v0, w0, m1, v1, w1, window = refs[11:18]
    r2, m2, v2 = refs[18:21]
    fine_refs = refs[21:24]
    coarse_refs = refs[24:27]
    tile = plan.tile
    gz, gy, gx = plan.counts
    iz, iy, ix = (lax.axis_index(axis) for axis in AXES)
    inside = inside_mask(plan, coord_ref)

    def unpack(z_block, carry):
        for z in range(4):
            for y_block in range(gy):
                value = jnp.zeros((8, 128), F32)
                for x_block in range(gx):
                    part = joined[(z_block * gy + y_block) * gx + x_block]
                    value = jnp.where(
                        between(32 * x_block, 32 * x_block + 32),
                        pltpu.roll(part, (32 * (x_block - z)) % 128, 1),
                        value,
                    )
                rows = slice(4 * y_block, 4 * y_block + 4)
                r2[4 * z_block + z, rows, :] = value[0:4]
                m2[4 * z_block + z, rows, :] = value[4:8]
        return carry

    lax.fori_loop(0, gz, unpack, 0)
    for ref in (*fine_refs, *coarse_refs):
        ref[...] = jnp.zeros(ref.shape, F32)

    levels = [Level(plan, level) for level in range(2, LEVELS + 1)]
    mobility, source = m2[...], r2[...]
    kept = []
    for i, level in enumerate(levels):
        level.prepare(mobility, source)
        if i < len(levels) - 1:
            e = level.first + level.first * 0.2 + level.pull(level.first)
            kept.append(e)
            args = (level, levels[i + 1], fine_refs[i], coarse_refs[i])
            mobility = coarsen(mobility, *args)
            source = coarsen(level.leftover(e), *args)
    level = levels[-1]
    v = level.first
    for repeat in range(COARSE - 1):
        v = level.relax(v)
    for i in range(len(levels) - 2, -1, -1):
        v = kept[i] + refine(v, levels[i], levels[i + 1], fine_refs[i])
        v = levels[i].relax(levels[i].relax(v))

    v2[...] = jnp.zeros(v2.shape, F32)
    margin = 0 if plan.near == 1 else 8
    v2[pl.ds(HALO, plan.coarse[0]), pl.ds(margin, plan.coarse[1]), :] = v
    planes = []
    for z in range(ZW):
        if plan.near == 1:
            planes.append(v2[4 * iz + z])
        else:
            planes.append(v2[4 * iz + z, pl.ds(4 * iy + 4, tile), :])
    for t in range(3):
        value = jnp.zeros((tile, 128), F32)
        for z in range(ZW):
            offset = z * XW - 128 * t
            low, high = max(offset, 0), min(offset + XW, 128)
            if low < high:
                shift = lax.rem(offset % 128 + HALO - 32 * ix + 256, 128)
                value = jnp.where(
                    between(low, high, tile), pltpu.roll(planes[z], shift, 1), value
                )
        lanes = slice(128 * t, 128 * t + 128)
        window[:, lanes] = jnp.where(inside[:, lanes], value, 0.0)

    def widen(n, source_ref, ref):
        def step(a, b):
            for c in range(n):
                ref[a + 1, b + 1, c + 1] = source_ref[a, b, c]

        over_pairs(n, step)
        fill_rim(plan, ref, n)

    widen(2, m1_in, m1)
    widen(4, m0_in, m0)
    below = window[...]

    def keep(a, b, c, value):
        v1[a + 1, b + 1, c + 1] = value

    ascend(plan, 2, m1, h1, e1, k1, lambda a, b, c: below, v1, w1, keep)

    def from_half(a, b, c):
        return v1[lax.div(a, 2) + 1, lax.div(b, 2) + 1, c // 2 + 1]

    def finish(a, b, c, value):
        v0[a + 1, b + 1, c + 1] = value

    ascend(plan, 4, m0, h0, e0, k0, from_half, v0, w0, finish)

    def store(pz, carry):
        for py in range(4):
            for z in range(4):
                base = (z + HALO) * XW + HALO
                value = jnp.zeros((tile, 128), F32)
                lane = lane_iota(tile)
                for px in range(4):
                    for t in range(3):
                        offset = base - 128 * t
                        low, high = max(offset, 0), min(offset + 32, 128)
                        if low < high:
                            index = (lax.shift_right_logical(lane, 2) + offset) & 127
                            here = (
                                ((lane & 3) == px)
                                & (lane >= 4 * (low - offset))
                                & (lane < 4 * (high - offset))
                            )
                            part = v0[pz + 1, py + 1, px + 1, :, 128 * t : 128 * t + 128]
                            value = jnp.where(here, gather(part, index), value)
                out[4 * z + pz, pl.ds(py, 4, 4), :] = own_rows(plan, value)
        return carry

    lax.fori_loop(0, 4, store, 0)


def call(kernel, outs, scratch, *args):
    return pl.pallas_call(
        kernel,
        out_shape=[jax.ShapeDtypeStruct(shape, F32) for shape in outs],
        scratch_shapes=[pltpu.VMEM(shape, F32) for shape in scratch],
        compiler_params=pltpu.CompilerParams(vmem_limit_bytes=48 * 1024 * 1024),
    )(*args)


def solution(mesh):
    plan = Plan(mesh)
    near, tile = plan.near, plan.tile
    z2, y2, x2 = plan.coarse
    full = (4, 4, 4, tile, LW)
    half = (2, 2, 2, tile, LW)
    full_rim = (6, 6, 6, tile, LW)
    half_rim = (4, 4, 4, tile, LW)
    y_swaps = list(range(near))

    def swap(values, *swaps):
        return lax.ppermute(values, AXES, plan.pairs(swaps))

    def on_device(residual, mobility):
        assert residual.shape == (16, 16, 128)
        beside = []
        for y in y_swaps:
            beside += [swap(residual, None, y, None), swap(mobility, None, y, None)]
        even, odd = call(edges_kernel, [(4, 16, 128)] * 2, [], residual, mobility)
        edges = [swap(even, None, None, 0), swap(odd, None, None, 1)]
        for y in y_swaps:
            edges += [swap(even, None, y, 0), swap(odd, None, y, 1)]
        pieces = (residual, mobility, *beside, *edges)
        sends = call(
            lambda *refs: z_pack_kernel(plan, *refs),
            [(plan.payload, 128)] * 2,
            [],
            table(edge_send_rows()),
            *pieces,
        )
        arrived = [swap(sends[0], 0, None, None), swap(sends[1], 1, None, None)]
        (own,) = call(
            lambda *refs: own_kernel(plan, *refs),
            [(2, *full)],
            [(2, 16, plan.rows, 128), (2, 4, plan.rows, 128)],
            table(edge_own_rows()),
            *pieces,
        )
        coordinates = coordinate_rows(tile)
        chunk, *state = call(
            lambda *refs: down_kernel(plan, *refs),
            [(plan.devices, 8, 128)] + [full] * 4 + [half] * 4,
            [full_rim, full, full_rim, full_rim, full]
            + [half_rim, half, half_rim, half_rim, half]
            + [(2, 2, EDGE, plan.rows, 128), (2, 4, plan.rows, 128)],
            table(edge_far_rows()),
            coordinates,
            own,
            *arrived,
        )
        joined = lax.all_to_all(chunk, AXES, 0, 0, tiled=True)
        levels = [Level(plan, level) for level in range(2, LEVELS + 1)]
        margin = 0 if near == 1 else 16
        (out,) = call(
            lambda *refs: up_kernel(plan, *refs),
            [(16, 16, 128)],
            [full_rim] * 3
            + [half_rim] * 3
            + [(tile, LW)]
            + [(z2, y2, 128)] * 2
            + [(z2 + 2 * HALO, y2 + margin, 128)]
            + [level.shape for level in levels[:-1]]
            + [level.shape for level in levels[1:]],
            coordinates,
            joined,
            *state,
        )
        return out

    spec = P(*AXES)
    return jax.shard_map(
        on_device, mesh=mesh, in_specs=(spec, spec), out_specs=spec, check_vma=False
    )
```

```python
import jax
import jax.numpy as jnp
import numpy as np
from jax import lax
from jax.experimental import pallas as pl
from jax.experimental.pallas import tpu as pltpu
from jax.sharding import PartitionSpec as P

LEVELS = 5
COARSE = 8
AXES = ("grp", "gy", "gx")
F32 = jnp.float32

HALO = 3
ZW = 4 + 2 * HALO
XW = 32 + 2 * HALO
LW = 384
EDGE = 4 * HALO
M_DEEP, M_FAR, R_DEEP, R_FAR = 11, 4, 10, 3
M_EDGE, R_EDGE = 11, 10


def lane_iota(rows=8):
    return lax.broadcasted_iota(jnp.int32, (rows, 128), 1)


def gather(source, index):
    return jnp.take_along_axis(source, index, axis=1, mode="promise_in_bounds")


def spread(source, offset, px):
    rows = source.shape[0]
    return gather(source, (4 * lane_iota(rows) + (px - 4 * offset)) & 127)


def between(low, high, rows=8):
    lane = lane_iota(rows)
    return (lane >= low) & (lane < high)


def table(rows):
    return jnp.asarray(np.repeat(np.stack(rows)[:, None, :], 8, axis=1).astype(np.int32))


def edge_send_rows():
    row = np.zeros(128, np.int64)
    base = 0
    for a, width in ((1, M_EDGE), (0, R_EDGE)):
        for side in (0, 1):
            first = EDGE - width if side == 0 else 0
            for z in range(HALO):
                for k in range(width):
                    row[base] = a * 48 + z * 12 + first + k + (1000 if side else 0)
                    base += 1
    return [row]


def edge_own_rows():
    rows = []
    for side, tiles in ((0, (0, 1)), (1, (1, 2))):
        for tile in tiles:
            row = np.full(128, -1, np.int64)
            for lane in range(128):
                z, x = divmod(128 * tile + lane, XW)
                x = x if side == 0 else x - (XW - HALO)
                if HALO <= z < HALO + 4 and 0 <= x < HALO:
                    row[lane] = (z - HALO) * 12 + 4 * x
            rows.append(row)
    return rows


def edge_far_rows():
    rows = []
    base_of = {(1, 0): 0, (1, 1): 33, (0, 0): 66, (0, 1): 96}
    for tile, first in ((0, 0), (2, HALO + 4)):
        for a, width in ((0, R_EDGE), (1, M_EDGE)):
            row = np.full(128, -1000, np.int64)
            for lane in range(128):
                z, x = divmod(128 * tile + lane, XW)
                if not first <= z < first + HALO:
                    continue
                for side in (0, 1):
                    k = 4 * x if side == 0 else 4 * (x - (XW - HALO))
                    if 0 <= k < EDGE:
                        start = base_of[a, side] + (z - first) * width
                        row[lane] = start + k - (EDGE - width if side == 0 else 0)
            rows.append(row)
    return rows


def coordinate_rows(rows):
    cells = np.arange(LW)
    z, x = cells // XW, cells % XW
    z = np.where(cells < ZW * XW, z, -1000000)
    both = np.stack([z, x])[:, None, :]
    return jnp.asarray(np.repeat(both, rows, axis=1).astype(np.int32))


class Plan:
    def __init__(self, mesh):
        self.counts = tuple(mesh.shape[axis] for axis in AXES)
        self.near = 1 if self.counts[1] == 2 else 2
        self.rows = 16 * (1 + self.near)
        self.cells = self.rows // 4
        self.tile = -(-self.cells // 8) * 8
        self.z_rows = 16 + 8 * self.near
        sizes = [
            M_DEEP * self.z_rows,
            M_FAR * 8 * self.near,
            R_DEEP * self.z_rows,
            R_FAR * 8 * self.near,
            4 * self.rows,
        ]
        self.starts = [sum(sizes[:i]) for i in range(len(sizes))]
        self.payload = sum(sizes)
        self.devices = self.counts[0] * self.counts[1] * self.counts[2]
        self.coarse = (4 * self.counts[0], 4 * self.counts[1], 32 * self.counts[2])

    def pairs(self, swaps):
        out = []
        for index in np.ndindex(*self.counts):
            there = []
            for axis, swap in enumerate(swaps):
                i, n = index[axis], self.counts[axis]
                j = i if swap is None else (i + 1 if i % 2 == swap else i - 1)
                if axis == 2:
                    j = j % n
                there.append(j)
            if all(0 <= j < n for j, n in zip(there, self.counts)):
                out.append(
                    (
                        int(np.ravel_multi_index(index, self.counts)),
                        int(np.ravel_multi_index(there, self.counts)),
                    )
                )
        return out

    def y_places(self):
        iy = lax.axis_index("gy")
        if self.near == 1:
            return 16 * iy, [(1 - iy, 16 * (1 - iy))]
        odd = lax.rem(iy, 2)
        return 16, [(1 - odd, 32 * (1 - odd)), (odd, 32 * odd)]


def is_even(axis):
    return lax.rem(lax.axis_index(axis), 2) == 0


def at(start, size):
    if isinstance(start, int):
        return pl.ds(start, size)
    return pl.ds(pl.multiple_of(start, 8), size)


def edges_kernel(r_ref, m_ref, even_ref, odd_ref):
    even = is_even("gx")
    for pz in range(4):
        for half in range(2):
            to_right = jnp.zeros((8, 128), F32)
            to_left = jnp.zeros((8, 128), F32)
            for a, ref in enumerate((r_ref, m_ref)):
                for z in range(4):
                    cells = ref[4 * z + pz, 8 * half : 8 * half + 8, :]
                    base = a * 48 + z * 12
                    here = between(base, base + EDGE)
                    shift = (base - (128 - EDGE)) % 128
                    to_right = jnp.where(here, pltpu.roll(cells, shift, 1), to_right)
                    to_left = jnp.where(here, pltpu.roll(cells, base, 1), to_left)
            rows = slice(8 * half, 8 * half + 8)
            even_ref[pz, rows, :] = jnp.where(even, to_right, to_left)
            odd_ref[pz, rows, :] = jnp.where(even, to_left, to_right)


def z_pack_kernel(plan, *refs):
    near = plan.near
    tab_ref, r_ref, m_ref = refs[:3]
    beside = [refs[3 + 2 * i : 5 + 2 * i] for i in range(near)]
    edges = [refs[3 + 2 * near + 2 * i : 5 + 2 * near + 2 * i] for i in range(1 + near)]
    outs = refs[-2:]
    own_row, places = plan.y_places()
    x_even = is_even("gx")
    z_even = is_even("grp")
    index = tab_ref[0]
    for swap, out in enumerate(outs):
        top = z_even if swap == 0 else jnp.logical_not(z_even)
        for a, ref, deep, far, start, far_start in (
            (1, m_ref, M_DEEP, M_FAR, plan.starts[0], plan.starts[1]),
            (0, r_ref, R_DEEP, R_FAR, plan.starts[2], plan.starts[3]),
        ):
            for d in range(1, deep + 1):
                plane = jnp.where(top, 16 - d, d - 1)
                row = start + (d - 1) * plan.z_rows
                out[row : row + 16, :] = ref[plane]
                for i, (side, _) in enumerate(places):
                    to = row + 16 + 8 * i
                    out[to : to + 8, :] = beside[i][a][plane, at(8 * (1 - side), 8), :]
                    if d <= far:
                        to = far_start + ((d - 1) * near + i) * 8
                        out[to : to + 8, :] = beside[i][a][plane, at(8 * side, 8), :]
        first = jnp.where(top, 12, 0)
        use_right = index >= 1000
        lanes = jnp.where(use_right, index - 1000, index) + first
        for i in range(1 + near):
            base = own_row if i == 0 else places[i - 1][1]
            even_ref, odd_ref = edges[i]
            for pz in range(4):
                for half in range(2):
                    rows = slice(8 * half, 8 * half + 8)
                    even, odd = even_ref[pz, rows, :], odd_ref[pz, rows, :]
                    left = gather(jnp.where(x_even, odd, even), lanes)
                    right = gather(jnp.where(x_even, even, odd), lanes)
                    to = at(plan.starts[4] + pz * plan.rows + base + 8 * half, 8)
                    out[to, :] = jnp.where(use_right, right, left)


def padded_rows(plan, cells):
    if plan.cells == plan.tile:
        return cells
    return jnp.concatenate(
        [cells, jnp.zeros((plan.tile - plan.cells, cells.shape[1]), F32)], axis=0
    )


def every_fourth(plan, ref, lead, py):
    return padded_rows(plan, ref[(*lead, pl.ds(py, plan.cells, 4), slice(None))])


def own_kernel(plan, *refs):
    near = plan.near
    tab_ref, r_ref, m_ref = refs[:3]
    beside = [refs[3 + 2 * i : 5 + 2 * i] for i in range(near)]
    edges = [refs[3 + 2 * near + 2 * i : 5 + 2 * near + 2 * i] for i in range(1 + near)]
    out, planes, sides = refs[-3:]
    tile = plan.tile
    own_row, places = plan.y_places()
    x_even = is_even("gx")
    blocks = [(own_row, (r_ref, m_ref))] + [(place[1], b) for place, b in zip(places, beside)]
    for i, (base, pair) in enumerate(blocks):
        for a in range(2):
            planes[a, :, at(base, 16), :] = pair[a][...]
        even, odd = edges[i][0][...], edges[i][1][...]
        sides[0, :, at(base, 16), :] = jnp.where(x_even, odd, even)
        sides[1, :, at(base, 16), :] = jnp.where(x_even, even, odd)

    def body(pz, carry):
        for a in range(2):
            for py in range(4):
                cells = [every_fourth(plan, planes, (a, 4 * z + pz), py) for z in range(4)]
                side = [every_fourth(plan, sides, (s, pz), py) for s in range(2)]
                for px in range(4):
                    for t in range(3):
                        value = jnp.zeros((tile, 128), F32)
                        for z in range(4):
                            offset = (z + HALO) * XW + HALO - 128 * t
                            low, high = max(offset, 0), min(offset + 32, 128)
                            if low < high:
                                value = jnp.where(
                                    between(low, high, tile),
                                    spread(cells[z], offset % 32, px),
                                    value,
                                )
                        for s in range(2):
                            if t - s in (0, 1):
                                index = tab_ref[2 * s + t - s]
                                index = jnp.concatenate([index] * (tile // 8), axis=0)
                                lanes = jnp.maximum(index, 0) + (48 * a + px)
                                value = jnp.where(index >= 0, gather(side[s], lanes), value)
                        out[a, pz, py, px, :, 128 * t : 128 * t + 128] = value
        return carry

    lax.fori_loop(0, 4, body, 0)


def inside_mask(plan, coord_ref):
    tile = plan.tile
    z = coord_ref[0] + (4 * lax.axis_index("grp") - HALO)
    x = coord_ref[1] + (32 * lax.axis_index("gx") - HALO)
    mask = (z >= 0) & (z < plan.coarse[0]) & (x >= 0) & (x < plan.coarse[2])
    if plan.near == 2:
        row = lax.broadcasted_iota(jnp.int32, (tile, LW), 0)
        y = row + (4 * lax.axis_index("gy") - 4)
        mask = mask & (row < plan.cells) & (y >= 0) & (y < plan.coarse[1])
    return mask


def roll_lanes(value, shift):
    return pltpu.roll(value, shift % LW, 1)


def fill_rim(plan, ref, n):
    tile = plan.tile
    row = lax.broadcasted_iota(jnp.int32, (tile, LW), 0)
    for i in range(1, n + 1):
        for j in range(1, n + 1):
            z_low, z_high = ref[n, i, j], ref[1, i, j]
            y_low, y_high = ref[i, n, j], ref[i, 1, j]
            x_low, x_high = ref[i, j, n], ref[i, j, 1]
            ref[0, i, j] = roll_lanes(z_low, XW)
            ref[n + 1, i, j] = roll_lanes(z_high, -XW)
            ref[i, 0, j] = jnp.where(row == 0, 0.0, pltpu.roll(y_low, 1, 0))
            ref[i, n + 1, j] = jnp.where(
                row == tile - 1, 0.0, pltpu.roll(y_high, tile - 1, 0)
            )
            ref[i, j, 0] = roll_lanes(x_low, 1)
            ref[i, j, n + 1] = roll_lanes(x_high, -1)


def around(ref, a, b, c):
    return (
        ref[a, b + 1, c + 1],
        ref[a + 2, b + 1, c + 1],
        ref[a + 1, b, c + 1],
        ref[a + 1, b + 2, c + 1],
        ref[a + 1, b + 1, c],
        ref[a + 1, b + 1, c + 2],
    )


def pull(m_ref, v_ref, h_ref, a, b, c):
    cells = around(v_ref, a, b, c)
    mobility = around(m_ref, a, b, c)
    total = ((cells[0] + cells[1]) + (cells[2] + cells[3])) + (cells[4] + cells[5])
    products = [m * v for m, v in zip(mobility, cells)]
    other = ((products[0] + products[1]) + (products[2] + products[3])) + (
        products[4] + products[5]
    )
    return h_ref[a, b, c] * (m_ref[a + 1, b + 1, c + 1] * total + other)


def over_pairs(n, step):
    if n == 2:
        for a, b in np.ndindex(2, 2):
            step(a, b)
        return

    def body(i, carry):
        step(lax.div(i, n), lax.rem(i, n))
        return carry

    lax.fori_loop(0, n * n, body, 0)


def descend(plan, n, factor, inside, m_ref, r_ref, v_ref, w_ref, d_ref, h_ref, e_ref, k_ref):
    fill_rim(plan, m_ref, n)

    def first(a, b):
        for c in range(n):
            s = around(m_ref, a, b, c)
            d = 3.0 * m_ref[a + 1, b + 1, c + 1] + 0.5 * (
                ((s[0] + s[1]) + (s[2] + s[3])) + (s[4] + s[5])
            )
            h = jnp.where(inside, 0.4 / d, 0.0)
            e = (2.0 / factor) * h * r_ref[a, b, c]
            d_ref[a, b, c] = d
            h_ref[a, b, c] = h
            e_ref[a, b, c] = e
            v_ref[a + 1, b + 1, c + 1] = e

    over_pairs(n, first)
    fill_rim(plan, v_ref, n)

    def second(a, b):
        for c in range(n):
            value = 1.2 * e_ref[a, b, c] + pull(m_ref, v_ref, h_ref, a, b, c)
            w_ref[a + 1, b + 1, c + 1] = value
            k_ref[a, b, c] = value

    over_pairs(n, second)
    fill_rim(plan, w_ref, n)


def leftover(factor, m_ref, r_ref, w_ref, d_ref, h_ref, a, b, c):
    away = w_ref[a + 1, b + 1, c + 1] - 1.25 * pull(m_ref, w_ref, h_ref, a, b, c)
    return r_ref[a, b, c] - factor * (d_ref[a, b, c] * away)


def down_kernel(plan, *refs):
    (tab_ref, coord_ref, own_ref, even_ref, odd_ref) = refs[:5]
    chunk, m0, h0, e0, k0, m1, h1, e1, k1 = refs[5:14]
    r0, v0, w0, d0, r1, v1, w1, d1, planes, sides = refs[14:]
    near, tile = plan.near, plan.tile
    own_row, places = plan.y_places()
    z_even = is_even("grp")
    inside = inside_mask(plan, coord_ref)

    for side in range(2):
        use_even = jnp.logical_not(z_even) if side == 0 else z_even

        def read(rows):
            return jnp.where(use_even, even_ref[rows, :], odd_ref[rows, :])

        for a, deep, far, start, far_start in (
            (1, M_DEEP, M_FAR, plan.starts[0], plan.starts[1]),
            (0, R_DEEP, R_FAR, plan.starts[2], plan.starts[3]),
        ):
            for d in range(1, EDGE + 1):
                plane = EDGE - d if side == 0 else d - 1
                if d > far:
                    planes[side, a, plane] = jnp.zeros((plan.rows, 128), F32)
                if d > deep:
                    continue
                row = start + (d - 1) * plan.z_rows
                planes[side, a, plane, at(own_row, 16), :] = read(slice(row, row + 16))
                for i, (y_side, base) in enumerate(places):
                    row_i = row + 16 + 8 * i
                    planes[side, a, plane, at(base + 8 * (1 - y_side), 8), :] = read(
                        slice(row_i, row_i + 8)
                    )
                    if d <= far:
                        row_i = far_start + ((d - 1) * near + i) * 8
                        planes[side, a, plane, at(base + 8 * y_side, 8), :] = read(
                            slice(row_i, row_i + 8)
                        )
        for pz in range(4):
            row = plan.starts[4] + pz * plan.rows
            sides[side, pz] = read(slice(row, row + plan.rows))

    def place(pz, carry):
        for a in range(2):
            for py in range(4):
                for side, t in ((0, 0), (1, 2)):
                    cells = [
                        every_fourth(plan, planes, (side, a, 4 * z + pz), py)
                        for z in range(HALO)
                    ]
                    edge = every_fourth(plan, sides, (side, pz), py)
                    index = tab_ref[2 * side + a]
                    index = jnp.concatenate([index] * (tile // 8), axis=0)
                    lanes = slice(128 * t, 128 * t + 128)
                    for px in range(4):
                        value = own_ref[a, pz, py, px, :, lanes]
                        for z in range(HALO):
                            offset = (z if side == 0 else z + HALO + 4) * XW + HALO - 128 * t
                            value = jnp.where(
                                between(offset, offset + 32, tile),
                                spread(cells[z], offset % 32, px),
                                value,
                            )
                        from_edge = jnp.clip(index + px, 0, 127)
                        value = jnp.where(index > -100, gather(edge, from_edge), value)
                        value = jnp.where(inside[:, lanes], value, 0.0)
                        if a == 1:
                            m0[pz + 1, py + 1, px + 1, :, lanes] = value
                        else:
                            r0[pz, py, px, :, lanes] = value
                for px in range(4):
                    lanes = slice(128, 256)
                    value = jnp.where(inside[:, lanes], own_ref[a, pz, py, px, :, lanes], 0.0)
                    if a == 1:
                        m0[pz + 1, py + 1, px + 1, :, lanes] = value
                    else:
                        r0[pz, py, px, :, lanes] = value
        return carry

    lax.fori_loop(0, 4, place, 0)

    descend(plan, 4, 1.0, inside, m0, r0, v0, w0, d0, h0, e0, k0)

    def restrict(a, b):
        for c in range(2):
            rest = jnp.zeros((tile, LW), F32)
            mobility = jnp.zeros((tile, LW), F32)
            for da in range(2):
                for db in range(2):
                    for dc in range(2):
                        i, j, k = 2 * a + da, 2 * b + db, 2 * c + dc
                        rest = rest + leftover(1.0, m0, r0, w0, d0, h0, i, j, k)
                        mobility = mobility + m0[i + 1, j + 1, k + 1]
            r1[a, b, c] = 0.125 * rest
            m1[a + 1, b + 1, c + 1] = 0.125 * mobility

    over_pairs(2, restrict)
    descend(plan, 2, 0.25, inside, m1, r1, v1, w1, d1, h1, e1, k1)
    rest = jnp.zeros((tile, LW), F32)
    mobility = jnp.zeros((tile, LW), F32)
    for a in range(2):
        for b in range(2):
            for c in range(2):
                rest = rest + leftover(0.25, m1, r1, w1, d1, h1, a, b, c)
                mobility = mobility + m1[a + 1, b + 1, c + 1]
    both = []
    for total in (rest, mobility):
        packed = jnp.zeros((tile, 128), F32)
        for t in range(3):
            part = 0.125 * total[:, 128 * t : 128 * t + 128]
            for z in range(4):
                offset = (z + HALO) * XW + HALO - 128 * t
                low, high = max(offset, 0), min(offset + 32, 128)
                if low < high:
                    move = 32 * z - offset
                    packed = jnp.where(
                        between(low + move, high + move, tile),
                        pltpu.roll(part, move % 128, 1),
                        packed,
                    )
        both.append(own_rows(plan, packed))
    block = jnp.concatenate(both, axis=0)

    def put(i, carry):
        chunk[i] = block
        return carry

    lax.fori_loop(0, plan.devices, put, 0, unroll=8)


def own_rows(plan, cells):
    if plan.near == 1:
        return jnp.where(lax.axis_index("gy") == 0, cells[0:4], cells[4:8])
    return cells[4:8]


class Level:
    def __init__(self, plan, level):
        self.size = tuple(n >> (level - 2) for n in plan.coarse)
        self.tile = max(8, self.size[1])
        self.shape = (self.size[0], self.tile, 128)
        self.factor = 0.25**level

    def shifts(self, v):
        z, y, x = self.size
        if z > 1:
            none = jnp.zeros((1, self.tile, 128), F32)
            yield jnp.concatenate([none, v[:-1]], axis=0)
            yield jnp.concatenate([v[1:], none], axis=0)
        else:
            yield jnp.zeros_like(v)
            yield jnp.zeros_like(v)
        row = lax.broadcasted_iota(jnp.int32, self.shape, 1)
        lane = lax.broadcasted_iota(jnp.int32, self.shape, 2)
        up, down = pltpu.roll(v, 1, 1), pltpu.roll(v, self.tile - 1, 1)
        if y == self.tile:
            up = jnp.where(row == 0, 0.0, up)
            down = jnp.where(row == self.tile - 1, 0.0, down)
        yield up
        yield down
        left, right = pltpu.roll(v, 1, 2), pltpu.roll(v, 127, 2)
        if x == 128:
            left = jnp.where(lane == 0, 0.0, left)
            right = jnp.where(lane == 127, 0.0, right)
        yield left
        yield right

    def prepare(self, mobility, source):
        z, y, x = self.size
        row = lax.broadcasted_iota(jnp.int32, self.shape, 1)
        lane = lax.broadcasted_iota(jnp.int32, self.shape, 2)
        inside = (row < y) & (lane < x)
        sums = [mobility + near for near in self.shifts(mobility)]
        self.diagonal = 0.5 * (
            ((sums[0] + sums[1]) + (sums[2] + sums[3])) + (sums[4] + sums[5])
        )
        h = jnp.where(inside, 0.4 / self.diagonal, 0.0)
        self.weights = [h * s for s in sums]
        self.first = (2.0 / self.factor) * h * source
        self.source = source

    def pull(self, v):
        t = [w * near for w, near in zip(self.weights, self.shifts(v))]
        return ((t[0] + t[1]) + (t[2] + t[3])) + (t[4] + t[5])

    def relax(self, v):
        return 0.2 * v + self.first + self.pull(v)

    def leftover(self, v):
        return self.source - self.factor * (self.diagonal * (v - 1.25 * self.pull(v)))


def lanes_2d(values, index):
    flat = values.reshape(-1, 128)
    rows = flat.shape[0]
    lane = lax.broadcasted_iota(jnp.int32, (rows, 128), 1)
    return gather(flat, index(lane)).reshape(values.shape)


def coarsen(values, fine, coarse, fine_ref, coarse_ref):
    z, y, x = coarse.size
    tile = fine.tile
    pairs = values.reshape(z, 2, tile, 128)
    fine_ref[0:z] = pairs[:, 0] + pairs[:, 1]
    rows = fine_ref[0:z, pl.ds(0, y, 2), :] + fine_ref[0:z, pl.ds(1, y, 2), :]
    coarse_ref[0:z, 0:y, :] = rows
    full = coarse_ref[0:z]
    full = full + pltpu.roll(full, 127, 2)
    full = lanes_2d(full, lambda lane: (2 * lane) & 127)
    lane = lax.broadcasted_iota(jnp.int32, full.shape, 2)
    return jnp.where(lane < x, 0.125 * full, 0.0)


def refine(values, fine, coarse, fine_ref):
    z, y, x = coarse.size
    wide = lanes_2d(values, lambda lane: lax.shift_right_logical(lane, 1))
    fine_ref[0:z, pl.ds(0, y, 2), :] = wide[:, 0:y]
    fine_ref[0:z, pl.ds(1, y, 2), :] = wide[:, 0:y]
    rows = fine_ref[0:z]
    return jnp.broadcast_to(rows[:, None], (z, 2, fine.tile, 128)).reshape(fine.shape)


def ascend(plan, n, m_ref, h_ref, e_ref, k_ref, below, v_ref, w_ref, emit):
    def start(a, b):
        for c in range(n):
            v_ref[a + 1, b + 1, c + 1] = k_ref[a, b, c] + below(a, b, c)

    over_pairs(n, start)
    fill_rim(plan, v_ref, n)

    def middle(a, b):
        for c in range(n):
            w_ref[a + 1, b + 1, c + 1] = (
                0.2 * v_ref[a + 1, b + 1, c + 1]
                + e_ref[a, b, c]
                + pull(m_ref, v_ref, h_ref, a, b, c)
            )

    over_pairs(n, middle)
    fill_rim(plan, w_ref, n)

    def last(a, b):
        for c in range(n):
            emit(
                a,
                b,
                c,
                0.2 * w_ref[a + 1, b + 1, c + 1]
                + e_ref[a, b, c]
                + pull(m_ref, w_ref, h_ref, a, b, c),
            )

    over_pairs(n, last)


def up_kernel(plan, *refs):
    coord_ref, joined, m0, h0, e0, k0, m1, h1, e1, k1, out = refs[:11]
    v0, w0, v1, w1, window, r2, m2, v2 = refs[11:19]
    fine_refs = refs[19:22]
    coarse_refs = refs[22:25]
    tile = plan.tile
    gz, gy, gx = plan.counts
    iz, iy, ix = (lax.axis_index(axis) for axis in AXES)
    inside = inside_mask(plan, coord_ref)

    def unpack(z_block, carry):
        for z in range(4):
            for y_block in range(gy):
                value = jnp.zeros((8, 128), F32)
                for x_block in range(gx):
                    part = joined[(z_block * gy + y_block) * gx + x_block]
                    value = jnp.where(
                        between(32 * x_block, 32 * x_block + 32),
                        pltpu.roll(part, (32 * (x_block - z)) % 128, 1),
                        value,
                    )
                rows = slice(4 * y_block, 4 * y_block + 4)
                r2[4 * z_block + z, rows, :] = value[0:4]
                m2[4 * z_block + z, rows, :] = value[4:8]
        return carry

    lax.fori_loop(0, gz, unpack, 0)
    for ref in (*fine_refs, *coarse_refs):
        ref[...] = jnp.zeros(ref.shape, F32)

    levels = [Level(plan, level) for level in range(2, LEVELS + 1)]
    mobility, source = m2[...], r2[...]
    kept = []
    for i, level in enumerate(levels):
        level.prepare(mobility, source)
        if i < len(levels) - 1:
            e = level.first + level.first * 0.2 + level.pull(level.first)
            kept.append(e)
            args = (level, levels[i + 1], fine_refs[i], coarse_refs[i])
            mobility = coarsen(mobility, *args)
            source = coarsen(level.leftover(e), *args)
    level = levels[-1]
    v = level.first
    for repeat in range(COARSE - 1):
        v = level.relax(v)
    for i in range(len(levels) - 2, -1, -1):
        v = kept[i] + refine(v, levels[i], levels[i + 1], fine_refs[i])
        v = levels[i].relax(levels[i].relax(v))

    v2[...] = jnp.zeros(v2.shape, F32)
    margin = 0 if plan.near == 1 else 8
    v2[pl.ds(HALO, plan.coarse[0]), pl.ds(margin, plan.coarse[1]), :] = v
    planes = []
    for z in range(ZW):
        if plan.near == 1:
            planes.append(v2[4 * iz + z])
        else:
            planes.append(v2[4 * iz + z, pl.ds(4 * iy + 4, tile), :])
    for t in range(3):
        value = jnp.zeros((tile, 128), F32)
        for z in range(ZW):
            offset = z * XW - 128 * t
            low, high = max(offset, 0), min(offset + XW, 128)
            if low < high:
                shift = lax.rem(offset % 128 + HALO - 32 * ix + 256, 128)
                value = jnp.where(
                    between(low, high, tile), pltpu.roll(planes[z], shift, 1), value
                )
        lanes = slice(128 * t, 128 * t + 128)
        window[:, lanes] = jnp.where(inside[:, lanes], value, 0.0)

    below = window[...]

    def keep(a, b, c, value):
        v1[a + 1, b + 1, c + 1] = value

    ascend(plan, 2, m1, h1, e1, k1, lambda a, b, c: below, v1, w1, keep)

    def from_half(a, b, c):
        return v1[lax.shift_right_logical(a, 1) + 1, lax.shift_right_logical(b, 1) + 1, c // 2 + 1]

    def finish(a, b, c, value):
        v0[a + 1, b + 1, c + 1] = value

    ascend(plan, 4, m0, h0, e0, k0, from_half, v0, w0, finish)

    def store(pz, carry):
        for py in range(4):
            for z in range(4):
                base = (z + HALO) * XW + HALO
                value = jnp.zeros((tile, 128), F32)
                lane = lane_iota(tile)
                for px in range(4):
                    for t in range(3):
                        offset = base - 128 * t
                        low, high = max(offset, 0), min(offset + 32, 128)
                        if low < high:
                            index = (lax.shift_right_logical(lane, 2) + offset) & 127
                            here = (
                                ((lane & 3) == px)
                                & (lane >= 4 * (low - offset))
                                & (lane < 4 * (high - offset))
                            )
                            part = v0[pz + 1, py + 1, px + 1, :, 128 * t : 128 * t + 128]
                            value = jnp.where(here, gather(part, index), value)
                out[4 * z + pz, pl.ds(py, 4, 4), :] = own_rows(plan, value)
        return carry

    lax.fori_loop(0, 4, store, 0)


def call(kernel, outs, scratch, *args):
    return pl.pallas_call(
        kernel,
        out_shape=[jax.ShapeDtypeStruct(shape, F32) for shape in outs],
        scratch_shapes=[pltpu.VMEM(shape, F32) for shape in scratch],
        compiler_params=pltpu.CompilerParams(vmem_limit_bytes=48 * 1024 * 1024),
    )(*args)


def solution(mesh):
    plan = Plan(mesh)
    near, tile = plan.near, plan.tile
    z2, y2, x2 = plan.coarse
    full = (4, 4, 4, tile, LW)
    half = (2, 2, 2, tile, LW)
    full_rim = (6, 6, 6, tile, LW)
    half_rim = (4, 4, 4, tile, LW)
    y_swaps = list(range(near))

    def swap(values, *swaps):
        return lax.ppermute(values, AXES, plan.pairs(swaps))

    def on_device(residual, mobility):
        assert residual.shape == (16, 16, 128)
        beside = []
        for y in y_swaps:
            beside += [swap(residual, None, y, None), swap(mobility, None, y, None)]
        even, odd = call(edges_kernel, [(4, 16, 128)] * 2, [], residual, mobility)
        edges = [swap(even, None, None, 0), swap(odd, None, None, 1)]
        for y in y_swaps:
            edges += [swap(even, None, y, 0), swap(odd, None, y, 1)]
        pieces = (residual, mobility, *beside, *edges)
        sends = call(
            lambda *refs: z_pack_kernel(plan, *refs),
            [(plan.payload, 128)] * 2,
            [],
            table(edge_send_rows()),
            *pieces,
        )
        arrived = [swap(sends[0], 0, None, None), swap(sends[1], 1, None, None)]
        (own,) = call(
            lambda *refs: own_kernel(plan, *refs),
            [(2, *full)],
            [(2, 16, plan.rows, 128), (2, 4, plan.rows, 128)],
            table(edge_own_rows()),
            *pieces,
        )
        coordinates = coordinate_rows(tile)
        chunk, *state = call(
            lambda *refs: down_kernel(plan, *refs),
            [(plan.devices, 8, 128)] + [full_rim] + [full] * 3 + [half_rim] + [half] * 3,
            [full, full_rim, full_rim, full]
            + [half, half_rim, half_rim, half]
            + [(2, 2, EDGE, plan.rows, 128), (2, 4, plan.rows, 128)],
            table(edge_far_rows()),
            coordinates,
            own,
            *arrived,
        )
        joined = lax.all_to_all(chunk, AXES, 0, 0, tiled=True)
        levels = [Level(plan, level) for level in range(2, LEVELS + 1)]
        margin = 0 if near == 1 else 16
        (out,) = call(
            lambda *refs: up_kernel(plan, *refs),
            [(16, 16, 128)],
            [full_rim] * 2
            + [half_rim] * 2
            + [(tile, LW)]
            + [(z2, y2, 128)] * 2
            + [(z2 + 2 * HALO, y2 + margin, 128)]
            + [level.shape for level in levels[:-1]]
            + [level.shape for level in levels[1:]],
            coordinates,
            joined,
            *state,
        )
        return out

    spec = P(*AXES)
    return jax.shard_map(
        on_device, mesh=mesh, in_specs=(spec, spec), out_specs=spec, check_vma=False
    )
```

```python
import jax
import jax.numpy as jnp
import numpy as np
from jax import lax
from jax.experimental import pallas as pl
from jax.experimental.pallas import tpu as pltpu
from jax.sharding import PartitionSpec as P

LEVELS = 5
COARSE = 8
AXES = ("grp", "gy", "gx")
F32 = jnp.float32

HALO = 3
ZW = 4 + 2 * HALO
XW = 32 + 2 * HALO
LW = 384
EDGE = 4 * HALO
M_DEEP, M_FAR, R_DEEP, R_FAR = 11, 4, 10, 3
M_EDGE, R_EDGE = 11, 10


def lane_iota(rows=8):
    return lax.broadcasted_iota(jnp.int32, (rows, 128), 1)


LANES = lax.GatherDimensionNumbers(
    offset_dims=(),
    collapsed_slice_dims=(1,),
    start_index_map=(1,),
    operand_batching_dims=(0,),
    start_indices_batching_dims=(0,),
)


def gather(source, index):
    return lax.gather(
        source, index[..., None], LANES, (1, 1), mode=lax.GatherScatterMode.PROMISE_IN_BOUNDS
    )


def every_lane(offset, px, rows):
    return (4 * lane_iota(rows) + ((px - 4 * offset) % 128)) & 127


def between(low, high, rows=8):
    lane = lane_iota(rows)
    return (lane >= low) & (lane < high)


def window_cells(t, rows):
    cell = lane_iota(rows) + 128 * t
    z = jnp.zeros((rows, 128), jnp.int32)
    for k in range(1, ZW + 1):
        z = z + (cell >= k * XW).astype(jnp.int32)
    return z, cell - z * XW


EDGE_STARTS = {(1, 0): 0, (1, 1): 33, (0, 0): 66, (0, 1): 96}


def edge_send_lanes():
    lane = lane_iota()
    mobile = lane < 66
    right = ((lane >= 33) & mobile) | (lane >= 96)
    start = jnp.where(mobile, jnp.where(right, 33, 0), jnp.where(right, 96, 66))
    width = jnp.where(mobile, M_EDGE, R_EDGE)
    t = lane - start
    z = (t >= width).astype(jnp.int32) + (t >= 2 * width).astype(jnp.int32)
    first = jnp.where(right, 0, EDGE - width)
    return jnp.minimum(jnp.where(mobile, 48, 0) + z * 12 + first + t - z * width, 95), right


def edge_own_lanes(side, t, rows):
    z, x = window_cells(t, rows)
    x = x if side == 0 else x - (XW - HALO)
    here = (z >= HALO) & (z < HALO + 4) & (x >= 0) & (x < HALO)
    return jnp.where(here, (z - HALO) * 12 + 4 * x, 0), here


def edge_far_lanes(side, a, rows):
    z, x = window_cells(2 * side, rows)
    z = z - (HALO + 4) * side
    width = M_EDGE if a == 1 else R_EDGE
    left, right = x < HALO, x >= XW - HALO
    here = (z >= 0) & (z < HALO) & (left | right)
    index = jnp.where(
        left,
        EDGE_STARTS[a, 0] + z * width + 4 * x - (EDGE - width),
        EDGE_STARTS[a, 1] + z * width + 4 * (x - (XW - HALO)),
    )
    return jnp.where(here, index, 4), here


class Plan:
    def __init__(self, mesh):
        self.counts = tuple(mesh.shape[axis] for axis in AXES)
        self.near = 1 if self.counts[1] == 2 else 2
        self.rows = 16 * (1 + self.near)
        self.cells = self.rows // 4
        self.tile = -(-self.cells // 8) * 8
        self.z_rows = 8 * self.near
        sizes = [
            M_DEEP * self.z_rows,
            M_FAR * self.z_rows,
            R_DEEP * self.z_rows,
            R_FAR * self.z_rows,
            4 * self.rows,
        ]
        self.starts = [sum(sizes[:i]) for i in range(len(sizes))]
        self.payload = sum(sizes)
        self.devices = self.counts[0] * self.counts[1] * self.counts[2]
        self.coarse = (4 * self.counts[0], 4 * self.counts[1], 32 * self.counts[2])

    def pairs(self, swaps):
        out = []
        for index in np.ndindex(*self.counts):
            there = []
            for axis, swap in enumerate(swaps):
                i, n = index[axis], self.counts[axis]
                j = i if swap is None else (i + 1 if i % 2 == swap else i - 1)
                if axis == 2:
                    j = j % n
                there.append(j)
            if not all(0 <= j < n for j, n in zip(there, self.counts)):
                there = [index[0], index[1], index[2] ^ 1]
            out.append(
                (
                    int(np.ravel_multi_index(index, self.counts)),
                    int(np.ravel_multi_index(there, self.counts)),
                )
            )
        return out

    def y_places(self):
        iy = lax.axis_index("gy")
        if self.near == 1:
            return 16 * iy, [(1 - iy, 16 * (1 - iy))]
        odd = lax.rem(iy, 2)
        return 16, [(1 - odd, 32 * (1 - odd)), (odd, 32 * odd)]


def is_even(axis):
    return lax.rem(lax.axis_index(axis), 2) == 0


def at(start, size):
    if isinstance(start, int):
        return pl.ds(start, size)
    return pl.ds(pl.multiple_of(start, 8), size)


def edges_kernel(r_hbm, m_hbm, r_ref, m_ref, even_ref, odd_ref, even_z_ref, odd_z_ref, sems):
    copies = [
        pltpu.make_async_copy(r_hbm, r_ref, sems.at[0]),
        pltpu.make_async_copy(m_hbm, m_ref, sems.at[1]),
    ]
    for copy in copies:
        copy.start()
    for copy in copies:
        copy.wait()
    z_even = is_even("grp")
    for swap, out in enumerate((even_z_ref, odd_z_ref)):
        top = z_even if swap == 0 else jnp.logical_not(z_even)
        row = 0
        for ref, deep in ((m_ref, M_DEEP), (r_ref, R_DEEP)):
            for d in range(1, deep + 1):
                out[row : row + 16, :] = ref[jnp.where(top, 16 - d, d - 1)]
                row += 16
    even = is_even("gx")
    for pz in range(4):
        for half in range(2):
            to_right = jnp.zeros((8, 128), F32)
            to_left = jnp.zeros((8, 128), F32)
            for a, ref in enumerate((r_ref, m_ref)):
                for z in range(4):
                    cells = ref[4 * z + pz, 8 * half : 8 * half + 8, :]
                    base = a * 48 + z * 12
                    here = between(base, base + EDGE)
                    shift = (base - (128 - EDGE)) % 128
                    to_right = jnp.where(here, pltpu.roll(cells, shift, 1), to_right)
                    to_left = jnp.where(here, pltpu.roll(cells, base, 1), to_left)
            rows = slice(8 * half, 8 * half + 8)
            even_ref[pz, rows, :] = jnp.where(even, to_right, to_left)
            odd_ref[pz, rows, :] = jnp.where(even, to_left, to_right)


def z_pack_kernel(plan, *refs):
    near = plan.near
    beside = [refs[2 * i : 2 + 2 * i] for i in range(near)]
    edges = [refs[2 * near + 2 * i : 2 + 2 * near + 2 * i] for i in range(1 + near)]
    outs = refs[-2:]
    own_row, places = plan.y_places()
    x_even = is_even("gx")
    z_even = is_even("grp")
    lanes_0, use_right = edge_send_lanes()
    for swap, out in enumerate(outs):
        top = z_even if swap == 0 else jnp.logical_not(z_even)
        for a, deep, far, start, far_start in (
            (1, M_DEEP, M_FAR, plan.starts[0], plan.starts[1]),
            (0, R_DEEP, R_FAR, plan.starts[2], plan.starts[3]),
        ):
            for d in range(1, deep + 1):
                plane = jnp.where(top, 16 - d, d - 1)
                row = (d - 1) * plan.z_rows
                for i, (side, _) in enumerate(places):
                    to = start + row + 8 * i
                    out[to : to + 8, :] = beside[i][a][plane, at(8 * (1 - side), 8), :]
                    if d <= far:
                        to = far_start + row + 8 * i
                        out[to : to + 8, :] = beside[i][a][plane, at(8 * side, 8), :]
        lanes = lanes_0 + jnp.where(top, 12, 0)
        for i in range(1 + near):
            base = own_row if i == 0 else places[i - 1][1]
            even_ref, odd_ref = edges[i]
            for pz in range(4):
                for half in range(2):
                    rows = slice(8 * half, 8 * half + 8)
                    even, odd = even_ref[pz, rows, :], odd_ref[pz, rows, :]
                    left = gather(jnp.where(x_even, odd, even), lanes)
                    right = gather(jnp.where(x_even, even, odd), lanes)
                    to = at(plan.starts[4] + pz * plan.rows + base + 8 * half, 8)
                    out[to, :] = jnp.where(use_right, right, left)


def padded_rows(plan, cells):
    if plan.cells == plan.tile:
        return cells
    return jnp.concatenate(
        [cells, jnp.zeros((plan.tile - plan.cells, cells.shape[1]), F32)], axis=0
    )


def every_fourth(plan, ref, lead, py):
    return padded_rows(plan, ref[(*lead, pl.ds(py, plan.cells, 4), slice(None))])


def own_kernel(plan, *refs):
    near = plan.near
    r_ref, m_ref = refs[:2]
    beside = [refs[2 + 2 * i : 4 + 2 * i] for i in range(near)]
    edges = [refs[2 + 2 * near + 2 * i : 4 + 2 * near + 2 * i] for i in range(1 + near)]
    out, planes, sides = refs[-3:]
    tile = plan.tile
    own_row, places = plan.y_places()
    x_even = is_even("gx")
    blocks = [(own_row, (r_ref, m_ref))] + [(place[1], b) for place, b in zip(places, beside)]
    for i, (base, pair) in enumerate(blocks):
        for a in range(2):
            planes[a, :, at(base, 16), :] = pair[a][...]
        even, odd = edges[i][0][...], edges[i][1][...]
        sides[0, :, at(base, 16), :] = jnp.where(x_even, odd, even)
        sides[1, :, at(base, 16), :] = jnp.where(x_even, even, odd)

    offsets = [(z + HALO) * XW + HALO for z in range(4)]
    index = [[every_lane(offset, px, tile) for px in range(4)] for offset in offsets]
    from_edge = {(s, t): edge_own_lanes(s, t, tile) for s, t in ((0, 0), (0, 1), (1, 1), (1, 2))}

    def body(pz, carry):
        for a in range(2):
            for py in range(4):
                cells = [every_fourth(plan, planes, (a, 4 * z + pz), py) for z in range(4)]
                side = [every_fourth(plan, sides, (s, pz), py) for s in range(2)]
                for px in range(4):
                    parts = [gather(cells[z], index[z][px]) for z in range(4)]
                    for t in range(3):
                        value = jnp.zeros((tile, 128), F32)
                        for z in range(4):
                            offset = offsets[z] - 128 * t
                            low, high = max(offset, 0), min(offset + 32, 128)
                            if low < high:
                                value = jnp.where(between(low, high, tile), parts[z], value)
                        for s in range(2):
                            if (s, t) in from_edge:
                                lanes, here = from_edge[s, t]
                                lanes = lanes + (48 * a + px)
                                value = jnp.where(here, gather(side[s], lanes), value)
                        out[a, pz, py, px, :, 128 * t : 128 * t + 128] = value
        return carry

    lax.fori_loop(0, 4, body, 0)


def inside_mask(plan):
    tile = plan.tile
    masks = []
    for t in range(3):
        z, x = window_cells(t, tile)
        here = z < ZW
        z = z + (4 * lax.axis_index("grp") - HALO)
        x = x + (32 * lax.axis_index("gx") - HALO)
        here = here & (z >= 0) & (z < plan.coarse[0]) & (x >= 0) & (x < plan.coarse[2])
        if plan.near == 2:
            row = lax.broadcasted_iota(jnp.int32, (tile, 128), 0)
            y = row + (4 * lax.axis_index("gy") - 4)
            here = here & (row < plan.cells) & (y >= 0) & (y < plan.coarse[1])
        masks.append(jnp.where(here, 1.0, 0.0))
    return jnp.concatenate(masks, axis=1) > 0.5


def roll_lanes(value, shift):
    return pltpu.roll(value, shift % LW, 1)


def fill_rim(plan, ref, n):
    tile = plan.tile
    row = lax.broadcasted_iota(jnp.int32, (tile, LW), 0)
    for i in range(1, n + 1):
        for j in range(1, n + 1):
            z_low, z_high = ref[n, i, j], ref[1, i, j]
            y_low, y_high = ref[i, n, j], ref[i, 1, j]
            x_low, x_high = ref[i, j, n], ref[i, j, 1]
            ref[0, i, j] = roll_lanes(z_low, XW)
            ref[n + 1, i, j] = roll_lanes(z_high, -XW)
            ref[i, 0, j] = jnp.where(row == 0, 0.0, pltpu.roll(y_low, 1, 0))
            ref[i, n + 1, j] = jnp.where(
                row == tile - 1, 0.0, pltpu.roll(y_high, tile - 1, 0)
            )
            ref[i, j, 0] = roll_lanes(x_low, 1)
            ref[i, j, n + 1] = roll_lanes(x_high, -1)


def around(ref, a, b, c):
    return (
        ref[a, b + 1, c + 1],
        ref[a + 2, b + 1, c + 1],
        ref[a + 1, b, c + 1],
        ref[a + 1, b + 2, c + 1],
        ref[a + 1, b + 1, c],
        ref[a + 1, b + 1, c + 2],
    )


def pull(m_ref, v_ref, h_ref, a, b, c):
    cells = around(v_ref, a, b, c)
    mobility = around(m_ref, a, b, c)
    total = ((cells[0] + cells[1]) + (cells[2] + cells[3])) + (cells[4] + cells[5])
    products = [m * v for m, v in zip(mobility, cells)]
    other = ((products[0] + products[1]) + (products[2] + products[3])) + (
        products[4] + products[5]
    )
    return h_ref[a, b, c] * (m_ref[a + 1, b + 1, c + 1] * total + other)


def over_pairs(n, step):
    if n == 2:
        for a, b in np.ndindex(2, 2):
            step(a, b)
        return

    def body(i, carry):
        step(lax.div(i, n), lax.rem(i, n))
        return carry

    lax.fori_loop(0, n * n, body, 0)


def descend(plan, n, factor, inside, m_ref, r_ref, v_ref, w_ref, d_ref, h_ref, e_ref, k_ref):
    fill_rim(plan, m_ref, n)

    def first(a, b):
        for c in range(n):
            s = around(m_ref, a, b, c)
            d = 3.0 * m_ref[a + 1, b + 1, c + 1] + 0.5 * (
                ((s[0] + s[1]) + (s[2] + s[3])) + (s[4] + s[5])
            )
            h = jnp.where(inside, 0.4 / d, 0.0)
            e = (2.0 / factor) * h * r_ref[a, b, c]
            d_ref[a, b, c] = d
            h_ref[a, b, c] = h
            e_ref[a, b, c] = e
            v_ref[a + 1, b + 1, c + 1] = e

    over_pairs(n, first)
    fill_rim(plan, v_ref, n)

    def second(a, b):
        for c in range(n):
            value = 1.2 * e_ref[a, b, c] + pull(m_ref, v_ref, h_ref, a, b, c)
            w_ref[a + 1, b + 1, c + 1] = value
            k_ref[a, b, c] = value

    over_pairs(n, second)
    fill_rim(plan, w_ref, n)


def leftover(factor, m_ref, r_ref, w_ref, d_ref, h_ref, a, b, c):
    away = w_ref[a + 1, b + 1, c + 1] - 1.25 * pull(m_ref, w_ref, h_ref, a, b, c)
    return r_ref[a, b, c] - factor * (d_ref[a, b, c] * away)


def down_kernel(plan, *refs):
    own_ref, even_own, odd_own, even_ref, odd_ref = refs[:5]
    chunk, m0, h0, e0, k0, m1, h1, e1, k1 = refs[5:14]
    r0, v0, w0, d0, r1, v1, w1, d1, planes, sides = refs[14:]
    near, tile = plan.near, plan.tile
    own_row, places = plan.y_places()
    z_even = is_even("grp")
    inside = inside_mask(plan)

    for side in range(2):
        use_even = jnp.logical_not(z_even) if side == 0 else z_even

        def read(rows, even=even_ref, odd=odd_ref):
            return jnp.where(use_even, even[rows, :], odd[rows, :])

        for a, deep, far, start, far_start, own_start in (
            (1, M_DEEP, M_FAR, plan.starts[0], plan.starts[1], 0),
            (0, R_DEEP, R_FAR, plan.starts[2], plan.starts[3], 16 * M_DEEP),
        ):
            for d in range(1, EDGE + 1):
                plane = EDGE - d if side == 0 else d - 1
                if d > far:
                    planes[side, a, plane] = jnp.zeros((plan.rows, 128), F32)
                if d > deep:
                    continue
                row = own_start + 16 * (d - 1)
                planes[side, a, plane, at(own_row, 16), :] = read(
                    slice(row, row + 16), even_own, odd_own
                )
                row = (d - 1) * plan.z_rows
                for i, (y_side, base) in enumerate(places):
                    row_i = start + row + 8 * i
                    planes[side, a, plane, at(base + 8 * (1 - y_side), 8), :] = read(
                        slice(row_i, row_i + 8)
                    )
                    if d <= far:
                        row_i = far_start + row + 8 * i
                        planes[side, a, plane, at(base + 8 * y_side, 8), :] = read(
                            slice(row_i, row_i + 8)
                        )
        for pz in range(4):
            row = plan.starts[4] + pz * plan.rows
            sides[side, pz] = read(slice(row, row + plan.rows))

    first = [HALO, (HALO + 4) * XW + HALO - 256]
    index = [
        [[every_lane(first[side] + z * XW, px, tile) for px in range(4)] for z in range(HALO)]
        for side in range(2)
    ]
    here = [
        [between(first[side] + z * XW, first[side] + z * XW + 32, tile) for z in range(HALO)]
        for side in range(2)
    ]
    from_edge = {(s, a): edge_far_lanes(s, a, tile) for s in range(2) for a in range(2)}

    def place(pz, carry):
        for a in range(2):
            for py in range(4):
                cells = [
                    [every_fourth(plan, planes, (s, a, 4 * z + pz), py) for z in range(HALO)]
                    for s in range(2)
                ]
                edge = [every_fourth(plan, sides, (s, pz), py) for s in range(2)]
                for px in range(4):
                    for t in range(3):
                        lanes = slice(128 * t, 128 * t + 128)
                        value = own_ref[a, pz, py, px, :, lanes]
                        if t != 1:
                            s = t // 2
                            for z in range(HALO):
                                part = gather(cells[s][z], index[s][z][px])
                                value = jnp.where(here[s][z], part, value)
                            place_of, at_edge = from_edge[s, a]
                            part = gather(edge[s], place_of + px)
                            value = jnp.where(at_edge, part, value)
                        value = jnp.where(inside[:, lanes], value, 0.0)
                        if a == 1:
                            m0[pz + 1, py + 1, px + 1, :, lanes] = value
                        else:
                            r0[pz, py, px, :, lanes] = value
        return carry

    lax.fori_loop(0, 4, place, 0)

    descend(plan, 4, 1.0, inside, m0, r0, v0, w0, d0, h0, e0, k0)

    def restrict(a, b):
        for c in range(2):
            rest = jnp.zeros((tile, LW), F32)
            mobility = jnp.zeros((tile, LW), F32)
            for da in range(2):
                for db in range(2):
                    for dc in range(2):
                        i, j, k = 2 * a + da, 2 * b + db, 2 * c + dc
                        rest = rest + leftover(1.0, m0, r0, w0, d0, h0, i, j, k)
                        mobility = mobility + m0[i + 1, j + 1, k + 1]
            r1[a, b, c] = 0.125 * rest
            m1[a + 1, b + 1, c + 1] = 0.125 * mobility

    over_pairs(2, restrict)
    descend(plan, 2, 0.25, inside, m1, r1, v1, w1, d1, h1, e1, k1)
    rest = jnp.zeros((tile, LW), F32)
    mobility = jnp.zeros((tile, LW), F32)
    for a in range(2):
        for b in range(2):
            for c in range(2):
                rest = rest + leftover(0.25, m1, r1, w1, d1, h1, a, b, c)
                mobility = mobility + m1[a + 1, b + 1, c + 1]
    both = []
    for total in (rest, mobility):
        packed = jnp.zeros((tile, 128), F32)
        for t in range(3):
            part = 0.125 * total[:, 128 * t : 128 * t + 128]
            for z in range(4):
                offset = (z + HALO) * XW + HALO - 128 * t
                low, high = max(offset, 0), min(offset + 32, 128)
                if low < high:
                    move = 32 * z - offset
                    packed = jnp.where(
                        between(low + move, high + move, tile),
                        pltpu.roll(part, move % 128, 1),
                        packed,
                    )
        both.append(own_rows(plan, packed))
    block = jnp.concatenate(both, axis=0)

    def put(i, carry):
        chunk[i] = block
        return carry

    lax.fori_loop(0, plan.devices, put, 0, unroll=8)


def own_rows(plan, cells):
    if plan.near == 1:
        return jnp.where(lax.axis_index("gy") == 0, cells[0:4], cells[4:8])
    return cells[4:8]


class Level:
    def __init__(self, plan, level):
        self.size = tuple(n >> (level - 2) for n in plan.coarse)
        self.tile = max(8, self.size[1])
        self.shape = (self.size[0], self.tile, 128)
        self.factor = 0.25**level

    def shifts(self, v):
        z, y, x = self.size
        if z > 1:
            none = jnp.zeros((1, self.tile, 128), F32)
            yield jnp.concatenate([none, v[:-1]], axis=0)
            yield jnp.concatenate([v[1:], none], axis=0)
        else:
            yield jnp.zeros_like(v)
            yield jnp.zeros_like(v)
        row = lax.broadcasted_iota(jnp.int32, self.shape, 1)
        lane = lax.broadcasted_iota(jnp.int32, self.shape, 2)
        up, down = pltpu.roll(v, 1, 1), pltpu.roll(v, self.tile - 1, 1)
        if y == self.tile:
            up = jnp.where(row == 0, 0.0, up)
            down = jnp.where(row == self.tile - 1, 0.0, down)
        yield up
        yield down
        left, right = pltpu.roll(v, 1, 2), pltpu.roll(v, 127, 2)
        if x == 128:
            left = jnp.where(lane == 0, 0.0, left)
            right = jnp.where(lane == 127, 0.0, right)
        yield left
        yield right

    def prepare(self, mobility, source):
        z, y, x = self.size
        row = lax.broadcasted_iota(jnp.int32, self.shape, 1)
        lane = lax.broadcasted_iota(jnp.int32, self.shape, 2)
        inside = (row < y) & (lane < x)
        sums = [mobility + near for near in self.shifts(mobility)]
        self.diagonal = 0.5 * (
            ((sums[0] + sums[1]) + (sums[2] + sums[3])) + (sums[4] + sums[5])
        )
        h = jnp.where(inside, 0.4 / self.diagonal, 0.0)
        self.weights = [h * s for s in sums]
        self.first = (2.0 / self.factor) * h * source
        self.source = source

    def pull(self, v):
        t = [w * near for w, near in zip(self.weights, self.shifts(v))]
        return ((t[0] + t[1]) + (t[2] + t[3])) + (t[4] + t[5])

    def relax(self, v):
        return 0.2 * v + self.first + self.pull(v)

    def leftover(self, v):
        return self.source - self.factor * (self.diagonal * (v - 1.25 * self.pull(v)))


def lanes_2d(values, index):
    flat = values.reshape(-1, 128)
    rows = flat.shape[0]
    lane = lax.broadcasted_iota(jnp.int32, (rows, 128), 1)
    return gather(flat, index(lane)).reshape(values.shape)


def coarsen(values, fine, coarse, fine_ref, coarse_ref):
    z, y, x = coarse.size
    tile = fine.tile
    pairs = values.reshape(z, 2, tile, 128)
    fine_ref[0:z] = pairs[:, 0] + pairs[:, 1]
    rows = fine_ref[0:z, pl.ds(0, y, 2), :] + fine_ref[0:z, pl.ds(1, y, 2), :]
    coarse_ref[0:z, 0:y, :] = rows
    full = coarse_ref[0:z]
    full = full + pltpu.roll(full, 127, 2)
    full = lanes_2d(full, lambda lane: (2 * lane) & 127)
    lane = lax.broadcasted_iota(jnp.int32, full.shape, 2)
    return jnp.where(lane < x, 0.125 * full, 0.0)


def refine(values, fine, coarse, fine_ref):
    z, y, x = coarse.size
    wide = lanes_2d(values, lambda lane: lax.shift_right_logical(lane, 1))
    fine_ref[0:z, pl.ds(0, y, 2), :] = wide[:, 0:y]
    fine_ref[0:z, pl.ds(1, y, 2), :] = wide[:, 0:y]
    rows = fine_ref[0:z]
    return jnp.broadcast_to(rows[:, None], (z, 2, fine.tile, 128)).reshape(fine.shape)


def ascend(plan, n, m_ref, h_ref, e_ref, k_ref, below, v_ref, w_ref, emit):
    def start(a, b):
        for c in range(n):
            v_ref[a + 1, b + 1, c + 1] = k_ref[a, b, c] + below(a, b, c)

    over_pairs(n, start)
    fill_rim(plan, v_ref, n)

    def middle(a, b):
        for c in range(n):
            w_ref[a + 1, b + 1, c + 1] = (
                0.2 * v_ref[a + 1, b + 1, c + 1]
                + e_ref[a, b, c]
                + pull(m_ref, v_ref, h_ref, a, b, c)
            )

    over_pairs(n, middle)
    fill_rim(plan, w_ref, n)

    def last(a, b):
        for c in range(n):
            emit(
                a,
                b,
                c,
                0.2 * w_ref[a + 1, b + 1, c + 1]
                + e_ref[a, b, c]
                + pull(m_ref, w_ref, h_ref, a, b, c),
            )

    over_pairs(n, last)


def up_kernel(plan, *refs):
    joined, m0, h0, e0, k0, m1, h1, e1, k1, out = refs[:10]
    v0, w0, v1, w1, window, r2, m2, v2 = refs[10:18]
    fine_refs = refs[18:21]
    coarse_refs = refs[21:24]
    tile = plan.tile
    gz, gy, gx = plan.counts
    iz, iy, ix = (lax.axis_index(axis) for axis in AXES)
    inside = inside_mask(plan)

    def unpack(z_block, carry):
        for z in range(4):
            for y_block in range(gy):
                value = jnp.zeros((8, 128), F32)
                for x_block in range(gx):
                    part = joined[(z_block * gy + y_block) * gx + x_block]
                    value = jnp.where(
                        between(32 * x_block, 32 * x_block + 32),
                        pltpu.roll(part, (32 * (x_block - z)) % 128, 1),
                        value,
                    )
                rows = slice(4 * y_block, 4 * y_block + 4)
                r2[4 * z_block + z, rows, :] = value[0:4]
                m2[4 * z_block + z, rows, :] = value[4:8]
        return carry

    lax.fori_loop(0, gz, unpack, 0)
    for ref in (*fine_refs, *coarse_refs):
        ref[...] = jnp.zeros(ref.shape, F32)

    levels = [Level(plan, level) for level in range(2, LEVELS + 1)]
    mobility, source = m2[...], r2[...]
    kept = []
    for i, level in enumerate(levels):
        level.prepare(mobility, source)
        if i < len(levels) - 1:
            e = level.first + level.first * 0.2 + level.pull(level.first)
            kept.append(e)
            args = (level, levels[i + 1], fine_refs[i], coarse_refs[i])
            mobility = coarsen(mobility, *args)
            source = coarsen(level.leftover(e), *args)
    level = levels[-1]
    v = level.first
    for repeat in range(COARSE - 1):
        v = level.relax(v)
    for i in range(len(levels) - 2, -1, -1):
        v = kept[i] + refine(v, levels[i], levels[i + 1], fine_refs[i])
        v = levels[i].relax(levels[i].relax(v))

    v2[...] = jnp.zeros(v2.shape, F32)
    margin = 0 if plan.near == 1 else 8
    v2[pl.ds(HALO, plan.coarse[0]), pl.ds(margin, plan.coarse[1]), :] = v
    planes = []
    for z in range(ZW):
        if plan.near == 1:
            planes.append(v2[4 * iz + z])
        else:
            planes.append(v2[4 * iz + z, pl.ds(4 * iy + 4, tile), :])
    for t in range(3):
        value = jnp.zeros((tile, 128), F32)
        for z in range(ZW):
            offset = z * XW - 128 * t
            low, high = max(offset, 0), min(offset + XW, 128)
            if low < high:
                shift = lax.rem(offset % 128 + HALO - 32 * ix + 256, 128)
                value = jnp.where(
                    between(low, high, tile), pltpu.roll(planes[z], shift, 1), value
                )
        lanes = slice(128 * t, 128 * t + 128)
        window[:, lanes] = jnp.where(inside[:, lanes], value, 0.0)

    below = window[...]

    def keep(a, b, c, value):
        v1[a + 1, b + 1, c + 1] = value

    ascend(plan, 2, m1, h1, e1, k1, lambda a, b, c: below, v1, w1, keep)

    def from_half(a, b, c):
        return v1[lax.shift_right_logical(a, 1) + 1, lax.shift_right_logical(b, 1) + 1, c // 2 + 1]

    def finish(a, b, c, value):
        v0[a + 1, b + 1, c + 1] = value

    ascend(plan, 4, m0, h0, e0, k0, from_half, v0, w0, finish)

    lane = lane_iota(tile)
    turns = [(lane & 3) == px for px in range(4)]
    starts = [(z + HALO) * XW + HALO for z in range(4)]
    index = [(lax.shift_right_logical(lane, 2) + start % 128) & 127 for start in starts]

    def store(pz, carry):
        for py in range(4):
            parts = [
                [v0[pz + 1, py + 1, px + 1, :, 128 * t : 128 * t + 128] for t in range(3)]
                for px in range(4)
            ]
            for z, start in enumerate(starts):
                low, high = start // 128, (start + 31) // 128
                value = None
                for px in range(4):
                    part = parts[px][low]
                    if low != high:
                        part = jnp.where(lane >= 64, part, parts[px][high])
                    part = gather(part, index[z])
                    value = part if value is None else jnp.where(turns[px], part, value)
                out[4 * z + pz, pl.ds(py, 4, 4), :] = own_rows(plan, value)
        return carry

    lax.fori_loop(0, 4, store, 0)


def call(plan, kernel, outs, scratch, *args, specs=None):
    more = {} if specs is None else dict(in_specs=specs)
    return pl.pallas_call(
        kernel,
        out_shape=[jax.ShapeDtypeStruct(shape, F32) for shape in outs],
        scratch_shapes=[
            pltpu.VMEM(shape, F32) if isinstance(shape, tuple) else shape for shape in scratch
        ],
        compiler_params=pltpu.CompilerParams(
            vmem_limit_bytes=(3 * plan.tile + plan.coarse[0] // 4) * 1024 * 1024
        ),
        **more,
    )(*args)


def solution(mesh):
    plan = Plan(mesh)
    near, tile = plan.near, plan.tile
    z2, y2, x2 = plan.coarse
    full = (4, 4, 4, tile, LW)
    half = (2, 2, 2, tile, LW)
    full_rim = (6, 6, 6, tile, LW)
    half_rim = (4, 4, 4, tile, LW)
    y_swaps = list(range(near))

    def swap(values, *swaps):
        return lax.ppermute(values, AXES, plan.pairs(swaps))

    def on_device(residual, mobility):
        assert residual.shape == (16, 16, 128)
        beside = []
        for y in y_swaps:
            beside += [swap(residual, None, y, None), swap(mobility, None, y, None)]
        residual, mobility, even, odd, even_z, odd_z = call(
            plan,
            edges_kernel,
            [(16, 16, 128)] * 2 + [(4, 16, 128)] * 2 + [(16 * (M_DEEP + R_DEEP), 128)] * 2,
            [pltpu.SemaphoreType.DMA((2,))],
            residual,
            mobility,
            specs=[pl.BlockSpec(memory_space=pltpu.HBM)] * 2,
        )
        z_own = [swap(even_z, 0, None, None), swap(odd_z, 1, None, None)]
        edges = [swap(even, None, None, 0), swap(odd, None, None, 1)]
        for y in y_swaps:
            edges += [swap(even, None, y, 0), swap(odd, None, y, 1)]
        sends = call(
            plan,
            lambda *refs: z_pack_kernel(plan, *refs),
            [(plan.payload, 128)] * 2,
            [],
            *beside,
            *edges,
        )
        arrived = [swap(sends[0], 0, None, None), swap(sends[1], 1, None, None)]
        (own,) = call(
            plan,
            lambda *refs: own_kernel(plan, *refs),
            [(2, *full)],
            [(2, 16, plan.rows, 128), (2, 4, plan.rows, 128)],
            residual,
            mobility,
            *beside,
            *edges,
        )
        chunk, *state = call(
            plan,
            lambda *refs: down_kernel(plan, *refs),
            [(plan.devices, 8, 128)] + [full_rim] + [full] * 3 + [half_rim] + [half] * 3,
            [full, full_rim, full_rim, full]
            + [half, half_rim, half_rim, half]
            + [(2, 2, EDGE, plan.rows, 128), (2, 4, plan.rows, 128)],
            own,
            *z_own,
            *arrived,
        )
        joined = lax.all_to_all(chunk, AXES, 0, 0, tiled=True)
        levels = [Level(plan, level) for level in range(2, LEVELS + 1)]
        margin = 0 if near == 1 else 16
        (out,) = call(
            plan,
            lambda *refs: up_kernel(plan, *refs),
            [(16, 16, 128)],
            [full_rim] * 2
            + [half_rim] * 2
            + [(tile, LW)]
            + [(z2, y2, 128)] * 2
            + [(z2 + 2 * HALO, y2 + margin, 128)]
            + [level.shape for level in levels[:-1]]
            + [level.shape for level in levels[1:]],
            joined,
            *state,
        )
        return out

    spec = P(*AXES)
    return jax.shard_map(
        on_device, mesh=mesh, in_specs=(spec, spec), out_specs=spec, check_vma=False
    )
```

```python
import jax
import jax.numpy as jnp
import numpy as np
from jax import lax
from jax.experimental import pallas as pl
from jax.experimental.pallas import tpu as pltpu
from jax.sharding import PartitionSpec as P

LEVELS = 5
COARSE = 8
AXES = ("grp", "gy", "gx")
F32 = jnp.float32

HALO = 3
ZW = 4 + 2 * HALO
XW = 32 + 2 * HALO
LW = 384
EDGE = 4 * HALO
M_DEEP, M_FAR, R_DEEP, R_FAR = 11, 4, 10, 3
M_EDGE, R_EDGE = 11, 10
Y_FAR = 3
Y_ROWS = 16 * (8 + Y_FAR)


def lane_iota(rows=8):
    return lax.broadcasted_iota(jnp.int32, (rows, 128), 1)


LANES = lax.GatherDimensionNumbers(
    offset_dims=(),
    collapsed_slice_dims=(1,),
    start_index_map=(1,),
    operand_batching_dims=(0,),
    start_indices_batching_dims=(0,),
)


def gather(source, index):
    return lax.gather(
        source, index[..., None], LANES, (1, 1), mode=lax.GatherScatterMode.PROMISE_IN_BOUNDS
    )


def every_lane(offset, px, rows):
    return (4 * lane_iota(rows) + ((px - 4 * offset) % 128)) & 127


def between(low, high, rows=8):
    lane = lane_iota(rows)
    return (lane >= low) & (lane < high)


def window_cells(t, rows):
    cell = lane_iota(rows) + 128 * t
    z = jnp.zeros((rows, 128), jnp.int32)
    for k in range(1, ZW + 1):
        z = z + (cell >= k * XW).astype(jnp.int32)
    return z, cell - z * XW


EDGE_STARTS = {(1, 0): 0, (1, 1): 33, (0, 0): 66, (0, 1): 96}


def edge_send_lanes():
    lane = lane_iota()
    mobile = lane < 66
    right = ((lane >= 33) & mobile) | (lane >= 96)
    start = jnp.where(mobile, jnp.where(right, 33, 0), jnp.where(right, 96, 66))
    width = jnp.where(mobile, M_EDGE, R_EDGE)
    t = lane - start
    z = (t >= width).astype(jnp.int32) + (t >= 2 * width).astype(jnp.int32)
    first = jnp.where(right, 0, EDGE - width)
    return jnp.minimum(jnp.where(mobile, 48, 0) + z * 12 + first + t - z * width, 95), right


def edge_own_lanes(side, t, rows):
    z, x = window_cells(t, rows)
    x = x if side == 0 else x - (XW - HALO)
    here = (z >= HALO) & (z < HALO + 4) & (x >= 0) & (x < HALO)
    return jnp.where(here, (z - HALO) * 12 + 4 * x, 0), here


def edge_far_lanes(side, a, rows):
    z, x = window_cells(2 * side, rows)
    z = z - (HALO + 4) * side
    width = M_EDGE if a == 1 else R_EDGE
    left, right = x < HALO, x >= XW - HALO
    here = (z >= 0) & (z < HALO) & (left | right)
    index = jnp.where(
        left,
        EDGE_STARTS[a, 0] + z * width + 4 * x - (EDGE - width),
        EDGE_STARTS[a, 1] + z * width + 4 * (x - (XW - HALO)),
    )
    return jnp.where(here, index, 4), here


class Plan:
    def __init__(self, mesh):
        self.counts = tuple(mesh.shape[axis] for axis in AXES)
        self.near = 1 if self.counts[1] == 2 else 2
        self.rows = 16 * (1 + self.near)
        self.cells = self.rows // 4
        self.tile = -(-self.cells // 8) * 8
        self.z_rows = 8 * self.near
        sizes = [
            M_DEEP * self.z_rows,
            M_FAR * self.z_rows,
            R_DEEP * self.z_rows,
            R_FAR * self.z_rows,
            4 * self.rows,
        ]
        self.starts = [sum(sizes[:i]) for i in range(len(sizes))]
        self.payload = sum(sizes)
        self.devices = self.counts[0] * self.counts[1] * self.counts[2]
        self.coarse = (4 * self.counts[0], 4 * self.counts[1], 32 * self.counts[2])

    def pairs(self, swaps):
        out = []
        for index in np.ndindex(*self.counts):
            there = []
            for axis, swap in enumerate(swaps):
                i, n = index[axis], self.counts[axis]
                j = i if swap is None else (i + 1 if i % 2 == swap else i - 1)
                if axis == 2:
                    j = j % n
                there.append(j)
            if not all(0 <= j < n for j, n in zip(there, self.counts)):
                there = [index[0], index[1], index[2] ^ 1]
            out.append(
                (
                    int(np.ravel_multi_index(index, self.counts)),
                    int(np.ravel_multi_index(there, self.counts)),
                )
            )
        return out

    def y_places(self):
        iy = lax.axis_index("gy")
        if self.near == 1:
            return 16 * iy, [(1 - iy, 16 * (1 - iy))]
        odd = lax.rem(iy, 2)
        return 16, [(1 - odd, 32 * (1 - odd)), (odd, 32 * odd)]


def is_even(axis):
    return lax.rem(lax.axis_index(axis), 2) == 0


def at(start, size):
    if isinstance(start, int):
        return pl.ds(start, size)
    return pl.ds(pl.multiple_of(start, 8), size)


def first_kernel(plan, cells_ref, *outs):
    z_even = is_even("grp")
    for swap, out in enumerate(outs[:2]):
        top = z_even if swap == 0 else jnp.logical_not(z_even)
        row = 0
        for a, deep in ((1, M_DEEP), (0, R_DEEP)):
            for d in range(1, deep + 1):
                out[row : row + 16, :] = cells_ref[a, jnp.where(top, 16 - d, d - 1)]
                row += 16
    for out, (side, _) in zip(outs[2:], plan.y_places()[1]):
        last = side == 1
        for a in range(2):
            near, far = a * Y_ROWS, a * Y_ROWS + 128
            for plane in range(16):
                cells = cells_ref[a, plane]
                rows = jnp.where(last, cells[8:16], cells[0:8])
                out[near + 8 * plane : near + 8 * plane + 8, :] = rows
                rows = jnp.where(last, cells[8 - Y_FAR : 8], cells[8 : 8 + Y_FAR])
                out[far + Y_FAR * plane : far + Y_FAR * (plane + 1), :] = rows


def edges_kernel(plan, *refs):
    cells_ref = refs[0]
    arrived = refs[1 : 1 + plan.near]
    beside = refs[1 + plan.near : 1 + 2 * plan.near]
    even_ref, odd_ref = refs[-2:]
    own_row, places = plan.y_places()
    even = is_even("gx")
    for ref, out, (side, _) in zip(arrived, beside, places):
        following = side == 1
        for a in range(2):
            near, far = a * Y_ROWS, a * Y_ROWS + 128
            for plane in range(16):
                rows = ref[near + 8 * plane : near + 8 * plane + 8, :]
                more = ref[far + Y_FAR * plane : far + Y_FAR * (plane + 1), :]
                none = jnp.zeros((8 - Y_FAR, 128), F32)
                after = jnp.concatenate([more, none], axis=0)
                before = jnp.concatenate([none, more], axis=0)
                out[a, plane, 0:8, :] = jnp.where(following, rows, before)
                out[a, plane, 8:16, :] = jnp.where(following, after, rows)
    for i, block in enumerate((cells_ref, *beside)):
        start = own_row if i == 0 else places[i - 1][1]
        for pz in range(4):
            for half in range(2):
                to_right = jnp.zeros((8, 128), F32)
                to_left = jnp.zeros((8, 128), F32)
                for a in range(2):
                    for z in range(4):
                        cells = block[a, 4 * z + pz, 8 * half : 8 * half + 8, :]
                        base = a * 48 + z * 12
                        here = between(base, base + EDGE)
                        shift = (base - (128 - EDGE)) % 128
                        to_right = jnp.where(here, pltpu.roll(cells, shift, 1), to_right)
                        to_left = jnp.where(here, pltpu.roll(cells, base, 1), to_left)
                rows = at(start + 8 * half, 8)
                even_ref[pz, rows, :] = jnp.where(even, to_right, to_left)
                odd_ref[pz, rows, :] = jnp.where(even, to_left, to_right)


def z_pack_kernel(plan, *refs):
    near = plan.near
    beside = refs[:near]
    x_even_ref, x_odd_ref = refs[near : near + 2]
    outs = refs[-2:]
    places = plan.y_places()[1]
    x_even = is_even("gx")
    z_even = is_even("grp")
    lanes_0, use_right = edge_send_lanes()
    for swap, out in enumerate(outs):
        top = z_even if swap == 0 else jnp.logical_not(z_even)
        for a, deep, far, start, far_start in (
            (1, M_DEEP, M_FAR, plan.starts[0], plan.starts[1]),
            (0, R_DEEP, R_FAR, plan.starts[2], plan.starts[3]),
        ):
            for d in range(1, deep + 1):
                plane = jnp.where(top, 16 - d, d - 1)
                row = (d - 1) * plan.z_rows
                for i, (side, _) in enumerate(places):
                    to = start + row + 8 * i
                    out[to : to + 8, :] = beside[i][a, plane, at(8 * (1 - side), 8), :]
                    if d <= far:
                        to = far_start + row + 8 * i
                        out[to : to + 8, :] = beside[i][a, plane, at(8 * side, 8), :]
        lanes = lanes_0 + jnp.where(top, 12, 0)
        for pz in range(4):
            for row in range(0, plan.rows, 8):
                even, odd = x_even_ref[pz, row : row + 8, :], x_odd_ref[pz, row : row + 8, :]
                left = gather(jnp.where(x_even, odd, even), lanes)
                right = gather(jnp.where(x_even, even, odd), lanes)
                to = plan.starts[4] + pz * plan.rows + row
                out[to : to + 8, :] = jnp.where(use_right, right, left)


def padded_rows(plan, cells):
    if plan.cells == plan.tile:
        return cells
    return jnp.concatenate(
        [cells, jnp.zeros((plan.tile - plan.cells, cells.shape[1]), F32)], axis=0
    )


def every_fourth(plan, ref, lead, py):
    return padded_rows(plan, ref[(*lead, pl.ds(py, plan.cells, 4), slice(None))])


def own_kernel(plan, *refs):
    near = plan.near
    cells_ref, *beside = refs[: 1 + near]
    x_even_ref, x_odd_ref = refs[1 + near : 3 + near]
    out, planes, sides = refs[-3:]
    tile = plan.tile
    own_row, places = plan.y_places()
    x_even = is_even("gx")
    planes[:, :, at(own_row, 16), :] = cells_ref[...]
    for (_, base), block in zip(places, beside):
        planes[:, :, at(base, 16), :] = block[...]
    even, odd = x_even_ref[...], x_odd_ref[...]
    sides[0] = jnp.where(x_even, odd, even)
    sides[1] = jnp.where(x_even, even, odd)

    offsets = [(z + HALO) * XW + HALO for z in range(4)]
    index = [[every_lane(offset, px, tile) for px in range(4)] for offset in offsets]
    from_edge = {(s, t): edge_own_lanes(s, t, tile) for s, t in ((0, 0), (0, 1), (1, 1), (1, 2))}

    def body(pz, carry):
        for a in range(2):
            for py in range(4):
                cells = [every_fourth(plan, planes, (a, 4 * z + pz), py) for z in range(4)]
                side = [every_fourth(plan, sides, (s, pz), py) for s in range(2)]
                for px in range(4):
                    parts = [gather(cells[z], index[z][px]) for z in range(4)]
                    for t in range(3):
                        value = jnp.zeros((tile, 128), F32)
                        for z in range(4):
                            offset = offsets[z] - 128 * t
                            low, high = max(offset, 0), min(offset + 32, 128)
                            if low < high:
                                value = jnp.where(between(low, high, tile), parts[z], value)
                        for s in range(2):
                            if (s, t) in from_edge:
                                lanes, here = from_edge[s, t]
                                lanes = lanes + (48 * a + px)
                                value = jnp.where(here, gather(side[s], lanes), value)
                        out[a, pz, py, px, :, 128 * t : 128 * t + 128] = value
        return carry

    lax.fori_loop(0, 4, body, 0)


def inside_mask(plan):
    tile = plan.tile
    masks = []
    for t in range(3):
        z, x = window_cells(t, tile)
        here = z < ZW
        z = z + (4 * lax.axis_index("grp") - HALO)
        x = x + (32 * lax.axis_index("gx") - HALO)
        here = here & (z >= 0) & (z < plan.coarse[0]) & (x >= 0) & (x < plan.coarse[2])
        if plan.near == 2:
            row = lax.broadcasted_iota(jnp.int32, (tile, 128), 0)
            y = row + (4 * lax.axis_index("gy") - 4)
            here = here & (row < plan.cells) & (y >= 0) & (y < plan.coarse[1])
        masks.append(jnp.where(here, 1.0, 0.0))
    return jnp.concatenate(masks, axis=1) > 0.5


def roll_lanes(value, shift):
    return pltpu.roll(value, shift % LW, 1)


def fill_rim(plan, ref, n):
    tile = plan.tile
    row = lax.broadcasted_iota(jnp.int32, (tile, LW), 0)
    for i in range(1, n + 1):
        for j in range(1, n + 1):
            z_low, z_high = ref[n, i, j], ref[1, i, j]
            y_low, y_high = ref[i, n, j], ref[i, 1, j]
            x_low, x_high = ref[i, j, n], ref[i, j, 1]
            ref[0, i, j] = roll_lanes(z_low, XW)
            ref[n + 1, i, j] = roll_lanes(z_high, -XW)
            ref[i, 0, j] = jnp.where(row == 0, 0.0, pltpu.roll(y_low, 1, 0))
            ref[i, n + 1, j] = jnp.where(
                row == tile - 1, 0.0, pltpu.roll(y_high, tile - 1, 0)
            )
            ref[i, j, 0] = roll_lanes(x_low, 1)
            ref[i, j, n + 1] = roll_lanes(x_high, -1)


def around(ref, a, b, c):
    return (
        ref[a, b + 1, c + 1],
        ref[a + 2, b + 1, c + 1],
        ref[a + 1, b, c + 1],
        ref[a + 1, b + 2, c + 1],
        ref[a + 1, b + 1, c],
        ref[a + 1, b + 1, c + 2],
    )


def pull(m_ref, v_ref, h_ref, a, b, c):
    cells = around(v_ref, a, b, c)
    mobility = around(m_ref, a, b, c)
    total = ((cells[0] + cells[1]) + (cells[2] + cells[3])) + (cells[4] + cells[5])
    products = [m * v for m, v in zip(mobility, cells)]
    other = ((products[0] + products[1]) + (products[2] + products[3])) + (
        products[4] + products[5]
    )
    return h_ref[a, b, c] * (m_ref[a + 1, b + 1, c + 1] * total + other)


def over_pairs(n, step):
    if n == 2:
        for a, b in np.ndindex(2, 2):
            step(a, b)
        return

    def body(i, carry):
        step(lax.div(i, n), lax.rem(i, n))
        return carry

    lax.fori_loop(0, n * n, body, 0)


def descend(plan, n, factor, inside, m_ref, r_ref, v_ref, w_ref, d_ref, h_ref, e_ref, k_ref):
    fill_rim(plan, m_ref, n)

    def first(a, b):
        for c in range(n):
            s = around(m_ref, a, b, c)
            d = 3.0 * m_ref[a + 1, b + 1, c + 1] + 0.5 * (
                ((s[0] + s[1]) + (s[2] + s[3])) + (s[4] + s[5])
            )
            h = jnp.where(inside, 0.4 / d, 0.0)
            e = (2.0 / factor) * h * r_ref[a, b, c]
            d_ref[a, b, c] = d
            h_ref[a, b, c] = h
            e_ref[a, b, c] = e
            v_ref[a + 1, b + 1, c + 1] = e

    over_pairs(n, first)
    fill_rim(plan, v_ref, n)

    def second(a, b):
        for c in range(n):
            value = 1.2 * e_ref[a, b, c] + pull(m_ref, v_ref, h_ref, a, b, c)
            w_ref[a + 1, b + 1, c + 1] = value
            k_ref[a, b, c] = value

    over_pairs(n, second)
    fill_rim(plan, w_ref, n)


def leftover(factor, m_ref, r_ref, w_ref, d_ref, h_ref, a, b, c):
    away = w_ref[a + 1, b + 1, c + 1] - 1.25 * pull(m_ref, w_ref, h_ref, a, b, c)
    return r_ref[a, b, c] - factor * (d_ref[a, b, c] * away)


def down_kernel(plan, *refs):
    own_ref, even_own, odd_own, even_ref, odd_ref = refs[:5]
    chunk, m0, h0, e0, k0, m1, h1, e1, k1 = refs[5:14]
    r0, v0, w0, d0, r1, v1, w1, d1, planes, sides = refs[14:]
    near, tile = plan.near, plan.tile
    own_row, places = plan.y_places()
    z_even = is_even("grp")
    inside = inside_mask(plan)

    for side in range(2):
        use_even = jnp.logical_not(z_even) if side == 0 else z_even

        def read(rows, even=even_ref, odd=odd_ref):
            return jnp.where(use_even, even[rows, :], odd[rows, :])

        for a, deep, far, start, far_start, own_start in (
            (1, M_DEEP, M_FAR, plan.starts[0], plan.starts[1], 0),
            (0, R_DEEP, R_FAR, plan.starts[2], plan.starts[3], 16 * M_DEEP),
        ):
            for d in range(1, EDGE + 1):
                plane = EDGE - d if side == 0 else d - 1
                if d > far:
                    planes[side, a, plane] = jnp.zeros((plan.rows, 128), F32)
                if d > deep:
                    continue
                row = own_start + 16 * (d - 1)
                planes[side, a, plane, at(own_row, 16), :] = read(
                    slice(row, row + 16), even_own, odd_own
                )
                row = (d - 1) * plan.z_rows
                for i, (y_side, base) in enumerate(places):
                    row_i = start + row + 8 * i
                    planes[side, a, plane, at(base + 8 * (1 - y_side), 8), :] = read(
                        slice(row_i, row_i + 8)
                    )
                    if d <= far:
                        row_i = far_start + row + 8 * i
                        planes[side, a, plane, at(base + 8 * y_side, 8), :] = read(
                            slice(row_i, row_i + 8)
                        )
        for pz in range(4):
            row = plan.starts[4] + pz * plan.rows
            sides[side, pz] = read(slice(row, row + plan.rows))

    first = [HALO, (HALO + 4) * XW + HALO - 256]
    index = [
        [[every_lane(first[side] + z * XW, px, tile) for px in range(4)] for z in range(HALO)]
        for side in range(2)
    ]
    here = [
        [between(first[side] + z * XW, first[side] + z * XW + 32, tile) for z in range(HALO)]
        for side in range(2)
    ]
    from_edge = {(s, a): edge_far_lanes(s, a, tile) for s in range(2) for a in range(2)}

    def place(pz, carry):
        for a in range(2):
            for py in range(4):
                cells = [
                    [every_fourth(plan, planes, (s, a, 4 * z + pz), py) for z in range(HALO)]
                    for s in range(2)
                ]
                edge = [every_fourth(plan, sides, (s, pz), py) for s in range(2)]
                for px in range(4):
                    for t in range(3):
                        lanes = slice(128 * t, 128 * t + 128)
                        value = own_ref[a, pz, py, px, :, lanes]
                        if t != 1:
                            s = t // 2
                            for z in range(HALO):
                                part = gather(cells[s][z], index[s][z][px])
                                value = jnp.where(here[s][z], part, value)
                            place_of, at_edge = from_edge[s, a]
                            part = gather(edge[s], place_of + px)
                            value = jnp.where(at_edge, part, value)
                        value = jnp.where(inside[:, lanes], value, 0.0)
                        if a == 1:
                            m0[pz + 1, py + 1, px + 1, :, lanes] = value
                        else:
                            r0[pz, py, px, :, lanes] = value
        return carry

    lax.fori_loop(0, 4, place, 0)

    descend(plan, 4, 1.0, inside, m0, r0, v0, w0, d0, h0, e0, k0)

    def restrict(a, b):
        for c in range(2):
            rest = jnp.zeros((tile, LW), F32)
            mobility = jnp.zeros((tile, LW), F32)
            for da in range(2):
                for db in range(2):
                    for dc in range(2):
                        i, j, k = 2 * a + da, 2 * b + db, 2 * c + dc
                        rest = rest + leftover(1.0, m0, r0, w0, d0, h0, i, j, k)
                        mobility = mobility + m0[i + 1, j + 1, k + 1]
            r1[a, b, c] = 0.125 * rest
            m1[a + 1, b + 1, c + 1] = 0.125 * mobility

    over_pairs(2, restrict)
    descend(plan, 2, 0.25, inside, m1, r1, v1, w1, d1, h1, e1, k1)
    rest = jnp.zeros((tile, LW), F32)
    mobility = jnp.zeros((tile, LW), F32)
    for a in range(2):
        for b in range(2):
            for c in range(2):
                rest = rest + leftover(0.25, m1, r1, w1, d1, h1, a, b, c)
                mobility = mobility + m1[a + 1, b + 1, c + 1]
    both = []
    for total in (rest, mobility):
        packed = jnp.zeros((tile, 128), F32)
        for t in range(3):
            part = 0.125 * total[:, 128 * t : 128 * t + 128]
            for z in range(4):
                offset = (z + HALO) * XW + HALO - 128 * t
                low, high = max(offset, 0), min(offset + 32, 128)
                if low < high:
                    move = 32 * z - offset
                    packed = jnp.where(
                        between(low + move, high + move, tile),
                        pltpu.roll(part, move % 128, 1),
                        packed,
                    )
        both.append(own_rows(plan, packed))
    block = jnp.concatenate(both, axis=0)

    def put(i, carry):
        chunk[i] = block
        return carry

    lax.fori_loop(0, plan.devices, put, 0, unroll=8)


def own_rows(plan, cells):
    if plan.near == 1:
        return jnp.where(lax.axis_index("gy") == 0, cells[0:4], cells[4:8])
    return cells[4:8]


class Level:
    def __init__(self, plan, level):
        self.size = tuple(n >> (level - 2) for n in plan.coarse)
        self.tile = max(8, self.size[1])
        self.shape = (self.size[0], self.tile, 128)
        self.factor = 0.25**level

    def shifts(self, v):
        z, y, x = self.size
        if z > 1:
            none = jnp.zeros((1, self.tile, 128), F32)
            yield jnp.concatenate([none, v[:-1]], axis=0)
            yield jnp.concatenate([v[1:], none], axis=0)
        else:
            yield jnp.zeros_like(v)
            yield jnp.zeros_like(v)
        row = lax.broadcasted_iota(jnp.int32, self.shape, 1)
        lane = lax.broadcasted_iota(jnp.int32, self.shape, 2)
        up, down = pltpu.roll(v, 1, 1), pltpu.roll(v, self.tile - 1, 1)
        if y == self.tile:
            up = jnp.where(row == 0, 0.0, up)
            down = jnp.where(row == self.tile - 1, 0.0, down)
        yield up
        yield down
        left, right = pltpu.roll(v, 1, 2), pltpu.roll(v, 127, 2)
        if x == 128:
            left = jnp.where(lane == 0, 0.0, left)
            right = jnp.where(lane == 127, 0.0, right)
        yield left
        yield right

    def prepare(self, mobility, source):
        z, y, x = self.size
        row = lax.broadcasted_iota(jnp.int32, self.shape, 1)
        lane = lax.broadcasted_iota(jnp.int32, self.shape, 2)
        inside = (row < y) & (lane < x)
        sums = [mobility + near for near in self.shifts(mobility)]
        self.diagonal = 0.5 * (
            ((sums[0] + sums[1]) + (sums[2] + sums[3])) + (sums[4] + sums[5])
        )
        h = jnp.where(inside, 0.4 / self.diagonal, 0.0)
        self.weights = [h * s for s in sums]
        self.first = (2.0 / self.factor) * h * source
        self.source = source

    def pull(self, v):
        t = [w * near for w, near in zip(self.weights, self.shifts(v))]
        return ((t[0] + t[1]) + (t[2] + t[3])) + (t[4] + t[5])

    def relax(self, v):
        return 0.2 * v + self.first + self.pull(v)

    def leftover(self, v):
        return self.source - self.factor * (self.diagonal * (v - 1.25 * self.pull(v)))


def lanes_2d(values, index):
    flat = values.reshape(-1, 128)
    rows = flat.shape[0]
    lane = lax.broadcasted_iota(jnp.int32, (rows, 128), 1)
    return gather(flat, index(lane)).reshape(values.shape)


def coarsen(values, fine, coarse, fine_ref, coarse_ref):
    z, y, x = coarse.size
    tile = fine.tile
    pairs = values.reshape(z, 2, tile, 128)
    fine_ref[0:z] = pairs[:, 0] + pairs[:, 1]
    rows = fine_ref[0:z, pl.ds(0, y, 2), :] + fine_ref[0:z, pl.ds(1, y, 2), :]
    coarse_ref[0:z, 0:y, :] = rows
    full = coarse_ref[0:z]
    full = full + pltpu.roll(full, 127, 2)
    full = lanes_2d(full, lambda lane: (2 * lane) & 127)
    lane = lax.broadcasted_iota(jnp.int32, full.shape, 2)
    return jnp.where(lane < x, 0.125 * full, 0.0)


def refine(values, fine, coarse, fine_ref):
    z, y, x = coarse.size
    wide = lanes_2d(values, lambda lane: lax.shift_right_logical(lane, 1))
    fine_ref[0:z, pl.ds(0, y, 2), :] = wide[:, 0:y]
    fine_ref[0:z, pl.ds(1, y, 2), :] = wide[:, 0:y]
    rows = fine_ref[0:z]
    return jnp.broadcast_to(rows[:, None], (z, 2, fine.tile, 128)).reshape(fine.shape)


def ascend(plan, n, m_ref, h_ref, e_ref, k_ref, below, v_ref, w_ref, emit):
    def start(a, b):
        for c in range(n):
            v_ref[a + 1, b + 1, c + 1] = k_ref[a, b, c] + below(a, b, c)

    over_pairs(n, start)
    fill_rim(plan, v_ref, n)

    def middle(a, b):
        for c in range(n):
            w_ref[a + 1, b + 1, c + 1] = (
                0.2 * v_ref[a + 1, b + 1, c + 1]
                + e_ref[a, b, c]
                + pull(m_ref, v_ref, h_ref, a, b, c)
            )

    over_pairs(n, middle)
    fill_rim(plan, w_ref, n)

    def last(a, b):
        for c in range(n):
            emit(
                a,
                b,
                c,
                0.2 * w_ref[a + 1, b + 1, c + 1]
                + e_ref[a, b, c]
                + pull(m_ref, w_ref, h_ref, a, b, c),
            )

    over_pairs(n, last)


def up_kernel(plan, *refs):
    joined, m0, h0, e0, k0, m1, h1, e1, k1, out = refs[:10]
    v0, w0, v1, w1, window, r2, m2, v2 = refs[10:18]
    fine_refs = refs[18:21]
    coarse_refs = refs[21:24]
    tile = plan.tile
    gz, gy, gx = plan.counts
    iz, iy, ix = (lax.axis_index(axis) for axis in AXES)
    inside = inside_mask(plan)

    def unpack(z_block, carry):
        for z in range(4):
            for y_block in range(gy):
                value = jnp.zeros((8, 128), F32)
                for x_block in range(gx):
                    part = joined[(z_block * gy + y_block) * gx + x_block]
                    value = jnp.where(
                        between(32 * x_block, 32 * x_block + 32),
                        pltpu.roll(part, (32 * (x_block - z)) % 128, 1),
                        value,
                    )
                rows = slice(4 * y_block, 4 * y_block + 4)
                r2[4 * z_block + z, rows, :] = value[0:4]
                m2[4 * z_block + z, rows, :] = value[4:8]
        return carry

    lax.fori_loop(0, gz, unpack, 0)
    for ref in (*fine_refs, *coarse_refs):
        ref[...] = jnp.zeros(ref.shape, F32)

    levels = [Level(plan, level) for level in range(2, LEVELS + 1)]
    mobility, source = m2[...], r2[...]
    kept = []
    for i, level in enumerate(levels):
        level.prepare(mobility, source)
        if i < len(levels) - 1:
            e = level.first + level.first * 0.2 + level.pull(level.first)
            kept.append(e)
            args = (level, levels[i + 1], fine_refs[i], coarse_refs[i])
            mobility = coarsen(mobility, *args)
            source = coarsen(level.leftover(e), *args)
    level = levels[-1]
    v = level.first
    for repeat in range(COARSE - 1):
        v = level.relax(v)
    for i in range(len(levels) - 2, -1, -1):
        v = kept[i] + refine(v, levels[i], levels[i + 1], fine_refs[i])
        v = levels[i].relax(levels[i].relax(v))

    v2[...] = jnp.zeros(v2.shape, F32)
    margin = 0 if plan.near == 1 else 8
    v2[pl.ds(HALO, plan.coarse[0]), pl.ds(margin, plan.coarse[1]), :] = v
    planes = []
    for z in range(ZW):
        if plan.near == 1:
            planes.append(v2[4 * iz + z])
        else:
            planes.append(v2[4 * iz + z, pl.ds(4 * iy + 4, tile), :])
    for t in range(3):
        value = jnp.zeros((tile, 128), F32)
        for z in range(ZW):
            offset = z * XW - 128 * t
            low, high = max(offset, 0), min(offset + XW, 128)
            if low < high:
                shift = lax.rem(offset % 128 + HALO - 32 * ix + 256, 128)
                value = jnp.where(
                    between(low, high, tile), pltpu.roll(planes[z], shift, 1), value
                )
        lanes = slice(128 * t, 128 * t + 128)
        window[:, lanes] = jnp.where(inside[:, lanes], value, 0.0)

    below = window[...]

    def keep(a, b, c, value):
        v1[a + 1, b + 1, c + 1] = value

    ascend(plan, 2, m1, h1, e1, k1, lambda a, b, c: below, v1, w1, keep)

    def from_half(a, b, c):
        return v1[lax.shift_right_logical(a, 1) + 1, lax.shift_right_logical(b, 1) + 1, c // 2 + 1]

    def finish(a, b, c, value):
        v0[a + 1, b + 1, c + 1] = value

    ascend(plan, 4, m0, h0, e0, k0, from_half, v0, w0, finish)

    lane = lane_iota(tile)
    turns = [(lane & 3) == px for px in range(4)]
    starts = [(z + HALO) * XW + HALO for z in range(4)]
    index = [(lax.shift_right_logical(lane, 2) + start % 128) & 127 for start in starts]

    def store(pz, carry):
        for py in range(4):
            parts = [
                [v0[pz + 1, py + 1, px + 1, :, 128 * t : 128 * t + 128] for t in range(3)]
                for px in range(4)
            ]
            for z, start in enumerate(starts):
                low, high = start // 128, (start + 31) // 128
                value = None
                for px in range(4):
                    part = parts[px][low]
                    if low != high:
                        part = jnp.where(lane >= 64, part, parts[px][high])
                    part = gather(part, index[z])
                    value = part if value is None else jnp.where(turns[px], part, value)
                out[4 * z + pz, pl.ds(py, 4, 4), :] = own_rows(plan, value)
        return carry

    lax.fori_loop(0, 4, store, 0)


def call(plan, kernel, outs, scratch, *args):
    return pl.pallas_call(
        kernel,
        out_shape=[jax.ShapeDtypeStruct(shape, F32) for shape in outs],
        scratch_shapes=[pltpu.VMEM(shape, F32) for shape in scratch],
        compiler_params=pltpu.CompilerParams(
            vmem_limit_bytes=(3 * plan.tile + plan.coarse[0] // 4) * 1024 * 1024
        ),
    )(*args)


def solution(mesh):
    plan = Plan(mesh)
    near, tile = plan.near, plan.tile
    z2, y2, x2 = plan.coarse
    full = (4, 4, 4, tile, LW)
    half = (2, 2, 2, tile, LW)
    full_rim = (6, 6, 6, tile, LW)
    half_rim = (4, 4, 4, tile, LW)

    def swap(values, *swaps):
        return lax.ppermute(values, AXES, plan.pairs(swaps))

    def on_device(residual, mobility):
        assert residual.shape == (16, 16, 128)
        cells = jnp.stack([residual, mobility])
        even, odd, *rows = call(
            plan,
            lambda *refs: first_kernel(plan, *refs),
            [(16 * (M_DEEP + R_DEEP), 128)] * 2 + [(2 * Y_ROWS, 128)] * near,
            [],
            cells,
        )
        arrived = [swap(values, None, y, None) for y, values in enumerate(rows)]
        z_own = [swap(even, 0, None, None), swap(odd, 1, None, None)]
        *beside, even, odd = call(
            plan,
            lambda *refs: edges_kernel(plan, *refs),
            [(2, 16, 16, 128)] * near + [(4, plan.rows, 128)] * 2,
            [],
            cells,
            *arrived,
        )
        edges = [swap(even, None, None, 0), swap(odd, None, None, 1)]
        sends = call(
            plan,
            lambda *refs: z_pack_kernel(plan, *refs),
            [(plan.payload, 128)] * 2,
            [],
            *beside,
            *edges,
            *z_own,
        )
        arrived = [swap(sends[0], 0, None, None), swap(sends[1], 1, None, None)]
        (own,) = call(
            plan,
            lambda *refs: own_kernel(plan, *refs),
            [(2, *full)],
            [(2, 16, plan.rows, 128), (2, 4, plan.rows, 128)],
            cells,
            *beside,
            *edges,
        )
        chunk, *state = call(
            plan,
            lambda *refs: down_kernel(plan, *refs),
            [(plan.devices, 8, 128)] + [full_rim] + [full] * 3 + [half_rim] + [half] * 3,
            [full, full_rim, full_rim, full]
            + [half, half_rim, half_rim, half]
            + [(2, 2, EDGE, plan.rows, 128), (2, 4, plan.rows, 128)],
            own,
            *z_own,
            *arrived,
        )
        joined = lax.all_to_all(chunk, AXES, 0, 0, tiled=True)
        levels = [Level(plan, level) for level in range(2, LEVELS + 1)]
        margin = 0 if near == 1 else 16
        (out,) = call(
            plan,
            lambda *refs: up_kernel(plan, *refs),
            [(16, 16, 128)],
            [full_rim] * 2
            + [half_rim] * 2
            + [(tile, LW)]
            + [(z2, y2, 128)] * 2
            + [(z2 + 2 * HALO, y2 + margin, 128)]
            + [level.shape for level in levels[:-1]]
            + [level.shape for level in levels[1:]],
            joined,
            *state,
        )
        return out

    spec = P(*AXES)
    return jax.shard_map(
        on_device, mesh=mesh, in_specs=(spec, spec), out_specs=spec, check_vma=False
    )
```

```python
import jax
import jax.numpy as jnp
import numpy as np
from jax import lax
from jax.experimental import pallas as pl
from jax.experimental.pallas import tpu as pltpu
from jax.sharding import PartitionSpec as P

LEVELS = 5
COARSE = 8
AXES = ("grp", "gy", "gx")
F32 = jnp.float32

HALO = 3
ZW = 4 + 2 * HALO
XW = 32 + 2 * HALO
LW = 384
EDGE = 4 * HALO
M_DEEP, M_FAR, R_DEEP, R_FAR = 11, 4, 10, 3
M_EDGE, R_EDGE = 11, 10
Y_FAR = 3
Y_ROWS = 16 * (8 + Y_FAR)


def lane_iota(rows=8):
    return lax.broadcasted_iota(jnp.int32, (rows, 128), 1)


LANES = lax.GatherDimensionNumbers(
    offset_dims=(),
    collapsed_slice_dims=(1,),
    start_index_map=(1,),
    operand_batching_dims=(0,),
    start_indices_batching_dims=(0,),
)


def gather(source, index):
    return lax.gather(
        source, index[..., None], LANES, (1, 1), mode=lax.GatherScatterMode.PROMISE_IN_BOUNDS
    )


def every_lane(offset, px, rows):
    return (4 * lane_iota(rows) + ((px - 4 * offset) % 128)) & 127


def between(low, high, rows=8):
    lane = lane_iota(rows)
    return (lane >= low) & (lane < high)


def window_cells(t, rows):
    cell = lane_iota(rows) + 128 * t
    z = jnp.zeros((rows, 128), jnp.int32)
    for k in range(1, ZW + 1):
        z = z + (cell >= k * XW).astype(jnp.int32)
    return z, cell - z * XW


EDGE_STARTS = {(1, 0): 0, (1, 1): 33, (0, 0): 66, (0, 1): 96}


def edge_send_lanes():
    lane = lane_iota()
    mobile = lane < 66
    right = ((lane >= 33) & mobile) | (lane >= 96)
    start = jnp.where(mobile, jnp.where(right, 33, 0), jnp.where(right, 96, 66))
    width = jnp.where(mobile, M_EDGE, R_EDGE)
    t = lane - start
    z = (t >= width).astype(jnp.int32) + (t >= 2 * width).astype(jnp.int32)
    first = jnp.where(right, 0, EDGE - width)
    return jnp.minimum(jnp.where(mobile, 48, 0) + z * 12 + first + t - z * width, 95), right


def edge_own_lanes(side, t, rows):
    z, x = window_cells(t, rows)
    x = x if side == 0 else x - (XW - HALO)
    here = (z >= HALO) & (z < HALO + 4) & (x >= 0) & (x < HALO)
    return jnp.where(here, (z - HALO) * 12 + 4 * x, 0), here


def halo_start(side):
    return 0 if side == 0 else (HALO + 4) * XW - 256


def halo_cells(side, px, rows):
    p = (lane_iota(rows) - (halo_start(side) + 32 * px)) & 127
    z = (p >= XW).astype(jnp.int32) + (p >= 2 * XW).astype(jnp.int32)
    return z, p - z * XW, p < HALO * XW


def halo_turn(side, px, rows):
    z, x, _ = halo_cells(side, px, rows)
    return jnp.where((x >= HALO) & (x < XW - HALO), z, 3)


def halo_lanes(side, z, rows):
    q = (lane_iota(rows) - (halo_start(side) + z * XW + HALO)) & 127
    return 4 * (q & 31) + lax.shift_right_logical(q, 5)


def edge_far_lanes(side, a, rows):
    width = M_EDGE if a == 1 else R_EDGE
    index = jnp.zeros((rows, 128), jnp.int32)
    for px in range(4):
        z, x, here = halo_cells(side, px, rows)
        left = EDGE_STARTS[a, 0] + z * width + 4 * x + px - (EDGE - width)
        right = EDGE_STARTS[a, 1] + z * width + 4 * (x - (XW - HALO)) + px
        index = jnp.where(here & (x < HALO), left, index)
        index = jnp.where(here & (x >= XW - HALO), right, index)
    return jnp.clip(index, 0, 127)


class Plan:
    def __init__(self, mesh):
        self.counts = tuple(mesh.shape[axis] for axis in AXES)
        self.near = 1 if self.counts[1] == 2 else 2
        self.rows = 16 * (1 + self.near)
        self.cells = self.rows // 4
        self.tile = -(-self.cells // 8) * 8
        self.z_rows = 8 * self.near
        sizes = [
            M_DEEP * self.z_rows,
            M_FAR * self.z_rows,
            R_DEEP * self.z_rows,
            R_FAR * self.z_rows,
            4 * self.rows,
        ]
        self.starts = [sum(sizes[:i]) for i in range(len(sizes))]
        self.payload = sum(sizes)
        self.devices = self.counts[0] * self.counts[1] * self.counts[2]
        self.coarse = (4 * self.counts[0], 4 * self.counts[1], 32 * self.counts[2])

    def pairs(self, swaps):
        out = []
        for index in np.ndindex(*self.counts):
            there = []
            for axis, swap in enumerate(swaps):
                i, n = index[axis], self.counts[axis]
                j = i if swap is None else (i + 1 if i % 2 == swap else i - 1)
                if axis == 2:
                    j = j % n
                there.append(j)
            if not all(0 <= j < n for j, n in zip(there, self.counts)):
                there = [index[0], index[1], index[2] ^ 1]
            out.append(
                (
                    int(np.ravel_multi_index(index, self.counts)),
                    int(np.ravel_multi_index(there, self.counts)),
                )
            )
        return out

    def y_places(self):
        iy = lax.axis_index("gy")
        if self.near == 1:
            return 16 * iy, [(1 - iy, 16 * (1 - iy))]
        odd = lax.rem(iy, 2)
        return 16, [(1 - odd, 32 * (1 - odd)), (odd, 32 * odd)]


def is_even(axis):
    return lax.rem(lax.axis_index(axis), 2) == 0


def at(start, size):
    if isinstance(start, int):
        return pl.ds(start, size)
    return pl.ds(pl.multiple_of(start, 8), size)


def first_kernel(plan, cells_ref, *outs):
    z_even = is_even("grp")
    for swap, out in enumerate(outs[:2]):
        top = z_even if swap == 0 else jnp.logical_not(z_even)
        row = 0
        for a, deep in ((1, M_DEEP), (0, R_DEEP)):
            for d in range(1, deep + 1):
                out[row : row + 16, :] = cells_ref[a, jnp.where(top, 16 - d, d - 1)]
                row += 16
    for out, (side, _) in zip(outs[2:], plan.y_places()[1]):
        last = side == 1
        for a in range(2):
            near, far = a * Y_ROWS, a * Y_ROWS + 128
            for plane in range(16):
                cells = cells_ref[a, plane]
                rows = jnp.where(last, cells[8:16], cells[0:8])
                out[near + 8 * plane : near + 8 * plane + 8, :] = rows
                rows = jnp.where(last, cells[8 - Y_FAR : 8], cells[8 : 8 + Y_FAR])
                out[far + Y_FAR * plane : far + Y_FAR * (plane + 1), :] = rows


def edges_kernel(plan, *refs):
    cells_ref = refs[0]
    arrived = refs[1 : 1 + plan.near]
    beside = refs[1 + plan.near : 1 + 2 * plan.near]
    even_ref, odd_ref = refs[-2:]
    own_row, places = plan.y_places()
    even = is_even("gx")
    for ref, out, (side, _) in zip(arrived, beside, places):
        following = side == 1
        for a in range(2):
            near, far = a * Y_ROWS, a * Y_ROWS + 128
            for plane in range(16):
                rows = ref[near + 8 * plane : near + 8 * plane + 8, :]
                more = ref[far + Y_FAR * plane : far + Y_FAR * (plane + 1), :]
                none = jnp.zeros((8 - Y_FAR, 128), F32)
                after = jnp.concatenate([more, none], axis=0)
                before = jnp.concatenate([none, more], axis=0)
                out[a, plane, 0:8, :] = jnp.where(following, rows, before)
                out[a, plane, 8:16, :] = jnp.where(following, after, rows)
    for i, block in enumerate((cells_ref, *beside)):
        start = own_row if i == 0 else places[i - 1][1]
        for pz in range(4):
            for half in range(2):
                to_right = jnp.zeros((8, 128), F32)
                to_left = jnp.zeros((8, 128), F32)
                for a in range(2):
                    for z in range(4):
                        cells = block[a, 4 * z + pz, 8 * half : 8 * half + 8, :]
                        base = a * 48 + z * 12
                        here = between(base, base + EDGE)
                        shift = (base - (128 - EDGE)) % 128
                        to_right = jnp.where(here, pltpu.roll(cells, shift, 1), to_right)
                        to_left = jnp.where(here, pltpu.roll(cells, base, 1), to_left)
                rows = at(start + 8 * half, 8)
                even_ref[pz, rows, :] = jnp.where(even, to_right, to_left)
                odd_ref[pz, rows, :] = jnp.where(even, to_left, to_right)


def z_pack_kernel(plan, *refs):
    near = plan.near
    beside = refs[:near]
    x_odd_ref, x_even_ref = refs[near : near + 2]
    outs = refs[-2:]
    places = plan.y_places()[1]
    x_even = is_even("gx")
    z_even = is_even("grp")
    lanes_0, use_right = edge_send_lanes()
    for swap, out in enumerate(outs):
        top = z_even if swap == 0 else jnp.logical_not(z_even)
        for a, deep, far, start, far_start in (
            (1, M_DEEP, M_FAR, plan.starts[0], plan.starts[1]),
            (0, R_DEEP, R_FAR, plan.starts[2], plan.starts[3]),
        ):
            for d in range(1, deep + 1):
                plane = jnp.where(top, 16 - d, d - 1)
                row = (d - 1) * plan.z_rows
                for i, (side, _) in enumerate(places):
                    to = start + row + 8 * i
                    out[to : to + 8, :] = beside[i][a, plane, at(8 * (1 - side), 8), :]
                    if d <= far:
                        to = far_start + row + 8 * i
                        out[to : to + 8, :] = beside[i][a, plane, at(8 * side, 8), :]
        lanes = lanes_0 + jnp.where(top, 12, 0)
        for pz in range(4):
            for row in range(0, plan.rows, 8):
                even, odd = x_even_ref[pz, row : row + 8, :], x_odd_ref[pz, row : row + 8, :]
                left = gather(jnp.where(x_even, odd, even), lanes)
                right = gather(jnp.where(x_even, even, odd), lanes)
                to = plan.starts[4] + pz * plan.rows + row
                out[to : to + 8, :] = jnp.where(use_right, right, left)


def padded_rows(plan, cells):
    if plan.cells == plan.tile:
        return cells
    return jnp.concatenate(
        [cells, jnp.zeros((plan.tile - plan.cells, cells.shape[1]), F32)], axis=0
    )


def every_fourth(plan, ref, lead, py):
    return padded_rows(plan, ref[(*lead, pl.ds(py, plan.cells, 4), slice(None))])


def own_kernel(plan, *refs):
    near = plan.near
    cells_ref, *beside = refs[: 1 + near]
    x_odd_ref, x_even_ref = refs[1 + near : 3 + near]
    out, planes, sides = refs[-3:]
    tile = plan.tile
    own_row, places = plan.y_places()
    x_even = is_even("gx")
    planes[:, :, at(own_row, 16), :] = cells_ref[...]
    for (_, base), block in zip(places, beside):
        planes[:, :, at(base, 16), :] = block[...]
    even, odd = x_even_ref[...], x_odd_ref[...]
    sides[0] = jnp.where(x_even, odd, even)
    sides[1] = jnp.where(x_even, even, odd)

    inside = inside_mask(plan)
    offsets = [(z + HALO) * XW + HALO for z in range(4)]
    index = [[every_lane(offset, px, tile) for px in range(4)] for offset in offsets]
    from_edge = {(s, t): edge_own_lanes(s, t, tile) for s, t in ((0, 0), (0, 1), (1, 1), (1, 2))}

    def body(pz, carry):
        for a in range(2):
            for py in range(4):
                cells = [every_fourth(plan, planes, (a, 4 * z + pz), py) for z in range(4)]
                side = [every_fourth(plan, sides, (s, pz), py) for s in range(2)]
                for px in range(4):
                    parts = [gather(cells[z], index[z][px]) for z in range(4)]
                    for t in range(3):
                        value = jnp.zeros((tile, 128), F32)
                        for z in range(4):
                            offset = offsets[z] - 128 * t
                            low, high = max(offset, 0), min(offset + 32, 128)
                            if low < high:
                                value = jnp.where(between(low, high, tile), parts[z], value)
                        for s in range(2):
                            if (s, t) in from_edge:
                                lanes, here = from_edge[s, t]
                                lanes = lanes + (48 * a + px)
                                value = jnp.where(here, gather(side[s], lanes), value)
                        lanes = slice(128 * t, 128 * t + 128)
                        out[a, pz, py, px, :, lanes] = jnp.where(inside[:, lanes], value, 0.0)
        return carry

    lax.fori_loop(0, 4, body, 0)


def inside_mask(plan):
    tile = plan.tile
    masks = []
    for t in range(3):
        z, x = window_cells(t, tile)
        here = z < ZW
        z = z + (4 * lax.axis_index("grp") - HALO)
        x = x + (32 * lax.axis_index("gx") - HALO)
        here = here & (z >= 0) & (z < plan.coarse[0]) & (x >= 0) & (x < plan.coarse[2])
        if plan.near == 2:
            row = lax.broadcasted_iota(jnp.int32, (tile, 128), 0)
            y = row + (4 * lax.axis_index("gy") - 4)
            here = here & (row < plan.cells) & (y >= 0) & (y < plan.coarse[1])
        masks.append(jnp.where(here, 1.0, 0.0))
    return jnp.concatenate(masks, axis=1) > 0.5


def roll_lanes(value, shift):
    return pltpu.roll(value, shift % LW, 1)


def fill_rim(plan, ref, n):
    tile = plan.tile
    row = lax.broadcasted_iota(jnp.int32, (tile, LW), 0)
    for i in range(1, n + 1):
        for j in range(1, n + 1):
            z_low, z_high = ref[n, i, j], ref[1, i, j]
            y_low, y_high = ref[i, n, j], ref[i, 1, j]
            x_low, x_high = ref[i, j, n], ref[i, j, 1]
            ref[0, i, j] = roll_lanes(z_low, XW)
            ref[n + 1, i, j] = roll_lanes(z_high, -XW)
            ref[i, 0, j] = jnp.where(row == 0, 0.0, pltpu.roll(y_low, 1, 0))
            ref[i, n + 1, j] = jnp.where(
                row == tile - 1, 0.0, pltpu.roll(y_high, tile - 1, 0)
            )
            ref[i, j, 0] = roll_lanes(x_low, 1)
            ref[i, j, n + 1] = roll_lanes(x_high, -1)


def around(ref, a, b, c):
    return (
        ref[a, b + 1, c + 1],
        ref[a + 2, b + 1, c + 1],
        ref[a + 1, b, c + 1],
        ref[a + 1, b + 2, c + 1],
        ref[a + 1, b + 1, c],
        ref[a + 1, b + 1, c + 2],
    )


def around_rimless(plan, ref, n, a, b, c):
    tile = plan.tile
    row = lax.broadcasted_iota(jnp.int32, (tile, LW), 0)
    return (
        ref[a - 1, b, c] if a > 0 else roll_lanes(ref[n - 1, b, c], XW),
        ref[a + 1, b, c] if a < n - 1 else roll_lanes(ref[0, b, c], -XW),
        ref[a, b - 1, c] if b > 0 else jnp.where(row == 0, 0.0, pltpu.roll(ref[a, n - 1, c], 1, 0)),
        ref[a, b + 1, c]
        if b < n - 1
        else jnp.where(row == tile - 1, 0.0, pltpu.roll(ref[a, 0, c], tile - 1, 0)),
        ref[a, b, c - 1] if c > 0 else roll_lanes(ref[a, b, n - 1], 1),
        ref[a, b, c + 1] if c < n - 1 else roll_lanes(ref[a, b, 0], -1),
    )


def pull(plan, n, m_ref, v_ref, h_ref, a, b, c):
    cells = around_rimless(plan, v_ref, n, a, b, c)
    mobility = around(m_ref, a, b, c)
    total = ((cells[0] + cells[1]) + (cells[2] + cells[3])) + (cells[4] + cells[5])
    products = [m * v for m, v in zip(mobility, cells)]
    other = ((products[0] + products[1]) + (products[2] + products[3])) + (
        products[4] + products[5]
    )
    return h_ref[a, b, c] * (m_ref[a + 1, b + 1, c + 1] * total + other)


def descend(plan, n, factor, inside, m_ref, r_ref, d_ref, h_ref, e_ref, k_ref):
    fill_rim(plan, m_ref, n)
    for a, b, c in np.ndindex(n, n, n):
        s = around(m_ref, a, b, c)
        d = 3.0 * m_ref[a + 1, b + 1, c + 1] + 0.5 * (
            ((s[0] + s[1]) + (s[2] + s[3])) + (s[4] + s[5])
        )
        h = jnp.where(inside, 0.4 / d, 0.0)
        d_ref[a, b, c] = d
        h_ref[a, b, c] = h
        e_ref[a, b, c] = (2.0 / factor) * h * r_ref[a, b, c]
    for a, b, c in np.ndindex(n, n, n):
        k_ref[a, b, c] = 1.2 * e_ref[a, b, c] + pull(plan, n, m_ref, e_ref, h_ref, a, b, c)


def leftover(plan, n, factor, m_ref, r_ref, d_ref, h_ref, k_ref, a, b, c):
    away = k_ref[a, b, c] - 1.25 * pull(plan, n, m_ref, k_ref, h_ref, a, b, c)
    return r_ref[a, b, c] - factor * (d_ref[a, b, c] * away)


def down_kernel(plan, *refs):
    own_ref, odd_own, even_own, odd_ref, even_ref = refs[:5]
    chunk, m0, h0, e0, k0, m1, h1, e1, k1 = refs[5:14]
    r0, d0, r1, d1, planes, sides = refs[14:]
    near, tile = plan.near, plan.tile
    own_row, places = plan.y_places()
    z_even = is_even("grp")
    inside = inside_mask(plan)

    for side in range(2):
        use_even = jnp.logical_not(z_even) if side == 0 else z_even

        def read(rows, even=even_ref, odd=odd_ref):
            return jnp.where(use_even, even[rows, :], odd[rows, :])

        for a, deep, far, start, far_start, own_start in (
            (1, M_DEEP, M_FAR, plan.starts[0], plan.starts[1], 0),
            (0, R_DEEP, R_FAR, plan.starts[2], plan.starts[3], 16 * M_DEEP),
        ):
            for d in range(1, EDGE + 1):
                plane = EDGE - d if side == 0 else d - 1
                if d > far:
                    planes[side, a, plane] = jnp.zeros((plan.rows, 128), F32)
                if d > deep:
                    continue
                row = own_start + 16 * (d - 1)
                planes[side, a, plane, at(own_row, 16), :] = read(
                    slice(row, row + 16), even_own, odd_own
                )
                row = (d - 1) * plan.z_rows
                for i, (y_side, base) in enumerate(places):
                    row_i = start + row + 8 * i
                    planes[side, a, plane, at(base + 8 * (1 - y_side), 8), :] = read(
                        slice(row_i, row_i + 8)
                    )
                    if d <= far:
                        row_i = far_start + row + 8 * i
                        planes[side, a, plane, at(base + 8 * y_side, 8), :] = read(
                            slice(row_i, row_i + 8)
                        )
        for pz in range(4):
            row = plan.starts[4] + pz * plan.rows
            sides[side, pz] = read(slice(row, row + plan.rows))

    index = [[halo_lanes(side, z, tile) for z in range(HALO)] for side in range(2)]
    turns = [[halo_turn(side, px, tile) for px in range(4)] for side in range(2)]
    edge_index = [[edge_far_lanes(side, a, tile) for a in range(2)] for side in range(2)]
    keep = []
    for side, t in ((0, 0), (1, 2)):
        z, _ = window_cells(t, tile)
        z = (z < HALO) if side == 0 else (z >= HALO + 4)
        keep.append(z & inside[:, 128 * t : 128 * t + 128])

    def place(pz, carry):
        for a in range(2):
            for py in range(4):
                for side, t in ((0, 0), (1, 2)):
                    lanes = slice(128 * t, 128 * t + 128)
                    parts = [
                        gather(
                            every_fourth(plan, planes, (side, a, 4 * z + pz), py), index[side][z]
                        )
                        for z in range(HALO)
                    ]
                    edge = gather(
                        every_fourth(plan, sides, (side, pz), py), edge_index[side][a]
                    )
                    for px in range(4):
                        turn = turns[side][px]
                        value = jnp.where(turn == 1, parts[1], parts[0])
                        value = jnp.where(turn == 2, parts[2], value)
                        value = jnp.where(turn == 3, edge, value)
                        if px > 0:
                            value = pltpu.roll(value, 128 - 32 * px, 1)
                        value = jnp.where(
                            keep[side], value, own_ref[a, pz, py, px, :, lanes]
                        )
                        if a == 1:
                            m0[pz + 1, py + 1, px + 1, :, lanes] = value
                        else:
                            r0[pz, py, px, :, lanes] = value
                for px in range(4):
                    lanes = slice(128, 256)
                    value = own_ref[a, pz, py, px, :, lanes]
                    if a == 1:
                        m0[pz + 1, py + 1, px + 1, :, lanes] = value
                    else:
                        r0[pz, py, px, :, lanes] = value
        return carry

    lax.fori_loop(0, 4, place, 0)

    descend(plan, 4, 1.0, inside, m0, r0, d0, h0, e0, k0)
    for a, b, c in np.ndindex(2, 2, 2):
        rest = jnp.zeros((tile, LW), F32)
        mobility = jnp.zeros((tile, LW), F32)
        for da, db, dc in np.ndindex(2, 2, 2):
            i, j, k = 2 * a + da, 2 * b + db, 2 * c + dc
            rest = rest + leftover(plan, 4, 1.0, m0, r0, d0, h0, k0, i, j, k)
            mobility = mobility + m0[i + 1, j + 1, k + 1]
        r1[a, b, c] = 0.125 * rest
        m1[a + 1, b + 1, c + 1] = 0.125 * mobility
    descend(plan, 2, 0.25, inside, m1, r1, d1, h1, e1, k1)
    rest = jnp.zeros((tile, LW), F32)
    mobility = jnp.zeros((tile, LW), F32)
    for a, b, c in np.ndindex(2, 2, 2):
        rest = rest + leftover(plan, 2, 0.25, m1, r1, d1, h1, k1, a, b, c)
        mobility = mobility + m1[a + 1, b + 1, c + 1]
    both = []
    for total in (rest, mobility):
        packed = jnp.zeros((tile, 128), F32)
        for t in range(3):
            part = 0.125 * total[:, 128 * t : 128 * t + 128]
            for z in range(4):
                offset = (z + HALO) * XW + HALO - 128 * t
                low, high = max(offset, 0), min(offset + 32, 128)
                if low < high:
                    move = 32 * z - offset
                    packed = jnp.where(
                        between(low + move, high + move, tile),
                        pltpu.roll(part, move % 128, 1),
                        packed,
                    )
        both.append(own_rows(plan, packed))
    block = jnp.concatenate(both, axis=0)

    def put(i, carry):
        chunk[i] = block
        return carry

    lax.fori_loop(0, plan.devices, put, 0, unroll=8)


def own_rows(plan, cells):
    if plan.near == 1:
        return jnp.where(lax.axis_index("gy") == 0, cells[0:4], cells[4:8])
    return cells[4:8]


class Level:
    def __init__(self, plan, level):
        self.size = tuple(n >> (level - 2) for n in plan.coarse)
        self.tile = max(8, self.size[1])
        self.shape = (self.size[0], self.tile, 128)
        self.factor = 0.25**level

    def shifts(self, v):
        z, y, x = self.size
        if z > 1:
            none = jnp.zeros((1, self.tile, 128), F32)
            yield jnp.concatenate([none, v[:-1]], axis=0)
            yield jnp.concatenate([v[1:], none], axis=0)
        else:
            yield jnp.zeros_like(v)
            yield jnp.zeros_like(v)
        row = lax.broadcasted_iota(jnp.int32, self.shape, 1)
        lane = lax.broadcasted_iota(jnp.int32, self.shape, 2)
        up, down = pltpu.roll(v, 1, 1), pltpu.roll(v, self.tile - 1, 1)
        if y == self.tile:
            up = jnp.where(row == 0, 0.0, up)
            down = jnp.where(row == self.tile - 1, 0.0, down)
        yield up
        yield down
        left, right = pltpu.roll(v, 1, 2), pltpu.roll(v, 127, 2)
        if x == 128:
            left = jnp.where(lane == 0, 0.0, left)
            right = jnp.where(lane == 127, 0.0, right)
        yield left
        yield right

    def prepare(self, mobility, source):
        z, y, x = self.size
        row = lax.broadcasted_iota(jnp.int32, self.shape, 1)
        lane = lax.broadcasted_iota(jnp.int32, self.shape, 2)
        inside = (row < y) & (lane < x)
        sums = [mobility + near for near in self.shifts(mobility)]
        self.diagonal = 0.5 * (
            ((sums[0] + sums[1]) + (sums[2] + sums[3])) + (sums[4] + sums[5])
        )
        h = jnp.where(inside, 0.4 / self.diagonal, 0.0)
        self.weights = [h * s for s in sums]
        self.first = (2.0 / self.factor) * h * source
        self.source = source

    def pull(self, v):
        t = [w * near for w, near in zip(self.weights, self.shifts(v))]
        return ((t[0] + t[1]) + (t[2] + t[3])) + (t[4] + t[5])

    def relax(self, v):
        return 0.2 * v + self.first + self.pull(v)

    def leftover(self, v):
        return self.source - self.factor * (self.diagonal * (v - 1.25 * self.pull(v)))


def lanes_2d(values, index):
    flat = values.reshape(-1, 128)
    rows = flat.shape[0]
    lane = lax.broadcasted_iota(jnp.int32, (rows, 128), 1)
    return gather(flat, index(lane)).reshape(values.shape)


def coarsen(values, fine, coarse, fine_ref, coarse_ref):
    z, y, x = coarse.size
    tile = fine.tile
    pairs = values.reshape(z, 2, tile, 128)
    fine_ref[0:z] = pairs[:, 0] + pairs[:, 1]
    rows = fine_ref[0:z, pl.ds(0, y, 2), :] + fine_ref[0:z, pl.ds(1, y, 2), :]
    coarse_ref[0:z, 0:y, :] = rows
    full = coarse_ref[0:z]
    full = full + pltpu.roll(full, 127, 2)
    full = lanes_2d(full, lambda lane: (2 * lane) & 127)
    lane = lax.broadcasted_iota(jnp.int32, full.shape, 2)
    return jnp.where(lane < x, 0.125 * full, 0.0)


def refine(values, fine, coarse, fine_ref):
    z, y, x = coarse.size
    wide = lanes_2d(values, lambda lane: lax.shift_right_logical(lane, 1))
    fine_ref[0:z, pl.ds(0, y, 2), :] = wide[:, 0:y]
    fine_ref[0:z, pl.ds(1, y, 2), :] = wide[:, 0:y]
    rows = fine_ref[0:z]
    return jnp.broadcast_to(rows[:, None], (z, 2, fine.tile, 128)).reshape(fine.shape)


def ascend(plan, n, m_ref, h_ref, e_ref, k_ref, below, v_ref, w_ref):
    for a, b, c in np.ndindex(n, n, n):
        v_ref[a, b, c] = k_ref[a, b, c] + below(a, b, c)
    for old, new in ((v_ref, w_ref), (w_ref, v_ref)):
        for a, b, c in np.ndindex(n, n, n):
            new[a, b, c] = (
                0.2 * old[a, b, c]
                + e_ref[a, b, c]
                + pull(plan, n, m_ref, old, h_ref, a, b, c)
            )


def up_kernel(plan, *refs):
    joined, m0, h0, e0, k0, m1, h1, e1, k1, out = refs[:10]
    v0, w0, v1, w1, window, r2, m2, v2 = refs[10:18]
    fine_refs = refs[18:21]
    coarse_refs = refs[21:24]
    tile = plan.tile
    gz, gy, gx = plan.counts
    iz, iy, ix = (lax.axis_index(axis) for axis in AXES)
    inside = inside_mask(plan)

    def unpack(z_block, carry):
        for z in range(4):
            for y_block in range(gy):
                value = jnp.zeros((8, 128), F32)
                for x_block in range(gx):
                    part = joined[(z_block * gy + y_block) * gx + x_block]
                    value = jnp.where(
                        between(32 * x_block, 32 * x_block + 32),
                        pltpu.roll(part, (32 * (x_block - z)) % 128, 1),
                        value,
                    )
                rows = slice(4 * y_block, 4 * y_block + 4)
                r2[4 * z_block + z, rows, :] = value[0:4]
                m2[4 * z_block + z, rows, :] = value[4:8]
        return carry

    lax.fori_loop(0, gz, unpack, 0)
    for ref in (*fine_refs, *coarse_refs):
        ref[...] = jnp.zeros(ref.shape, F32)

    levels = [Level(plan, level) for level in range(2, LEVELS + 1)]
    mobility, source = m2[...], r2[...]
    kept = []
    for i, level in enumerate(levels):
        level.prepare(mobility, source)
        if i < len(levels) - 1:
            e = level.first + level.first * 0.2 + level.pull(level.first)
            kept.append(e)
            args = (level, levels[i + 1], fine_refs[i], coarse_refs[i])
            mobility = coarsen(mobility, *args)
            source = coarsen(level.leftover(e), *args)
    level = levels[-1]
    v = level.first
    for repeat in range(COARSE - 1):
        v = level.relax(v)
    for i in range(len(levels) - 2, -1, -1):
        v = kept[i] + refine(v, levels[i], levels[i + 1], fine_refs[i])
        v = levels[i].relax(levels[i].relax(v))

    v2[...] = jnp.zeros(v2.shape, F32)
    margin = 0 if plan.near == 1 else 8
    v2[pl.ds(HALO, plan.coarse[0]), pl.ds(margin, plan.coarse[1]), :] = v
    planes = []
    for z in range(ZW):
        if plan.near == 1:
            planes.append(v2[4 * iz + z])
        else:
            planes.append(v2[4 * iz + z, pl.ds(4 * iy + 4, tile), :])
    for t in range(3):
        value = jnp.zeros((tile, 128), F32)
        for z in range(ZW):
            offset = z * XW - 128 * t
            low, high = max(offset, 0), min(offset + XW, 128)
            if low < high:
                shift = lax.rem(offset % 128 + HALO - 32 * ix + 256, 128)
                value = jnp.where(
                    between(low, high, tile), pltpu.roll(planes[z], shift, 1), value
                )
        lanes = slice(128 * t, 128 * t + 128)
        window[:, lanes] = jnp.where(inside[:, lanes], value, 0.0)

    below = window[...]

    ascend(plan, 2, m1, h1, e1, k1, lambda a, b, c: below, v1, w1)
    ascend(plan, 4, m0, h0, e0, k0, lambda a, b, c: v1[a // 2, b // 2, c // 2], v0, w0)

    lane = lane_iota(tile)
    natural = 32 * (lane & 3) + lax.shift_right_logical(lane, 2)
    starts = [(z + HALO) * XW + HALO for z in range(4)]
    places_of = [(lane - start) & 127 for start in starts]
    index = [(natural + start) & 127 for start in starts]

    def store(pz, carry):
        for py in range(4):
            parts = [
                [v0[pz, py, px, :, 128 * t : 128 * t + 128] for t in range(3)]
                for px in range(4)
            ]
            parts = [
                [part if px == 0 else pltpu.roll(part, 32 * px, 1) for part in row]
                for px, row in enumerate(parts)
            ]
            for z, start in enumerate(starts):
                low, high = start // 128, (start + 31) // 128
                value = None
                for px in range(4):
                    part = parts[px][low]
                    if low != high:
                        first = (places_of[z] & 31) < 128 - start % 128
                        part = jnp.where(first, part, parts[px][high])
                    turn = lax.shift_right_logical(places_of[z], 5) == px
                    value = part if value is None else jnp.where(turn, part, value)
                value = gather(value, index[z])
                out[4 * z + pz, pl.ds(py, 4, 4), :] = own_rows(plan, value)
        return carry

    lax.fori_loop(0, 4, store, 0, unroll=4)


def call(plan, kernel, outs, scratch, *args):
    return pl.pallas_call(
        kernel,
        out_shape=[jax.ShapeDtypeStruct(shape, F32) for shape in outs],
        scratch_shapes=[pltpu.VMEM(shape, F32) for shape in scratch],
        compiler_params=pltpu.CompilerParams(
            vmem_limit_bytes=(3 * plan.tile + plan.coarse[0] // 4) * 1024 * 1024
        ),
    )(*args)


def solution(mesh):
    plan = Plan(mesh)
    near, tile = plan.near, plan.tile
    z2, y2, x2 = plan.coarse
    full = (4, 4, 4, tile, LW)
    half = (2, 2, 2, tile, LW)
    full_rim = (6, 6, 6, tile, LW)
    half_rim = (4, 4, 4, tile, LW)

    def swap(values, *swaps):
        return lax.ppermute(values, AXES, plan.pairs(swaps))

    def on_device(residual, mobility):
        assert residual.shape == (16, 16, 128)
        cells = jnp.stack([residual, mobility])
        even, odd, *rows = call(
            plan,
            lambda *refs: first_kernel(plan, *refs),
            [(16 * (M_DEEP + R_DEEP), 128)] * 2 + [(2 * Y_ROWS, 128)] * near,
            [],
            cells,
        )
        arrived = [swap(values, None, y, None) for y, values in enumerate(rows)]
        z_own = [swap(odd, 1, None, None), swap(even, 0, None, None)][::-1]
        *beside, even, odd = call(
            plan,
            lambda *refs: edges_kernel(plan, *refs),
            [(2, 16, 16, 128)] * near + [(4, plan.rows, 128)] * 2,
            [],
            cells,
            *arrived,
        )
        edges = [swap(odd, None, None, 1), swap(even, None, None, 0)][::-1]
        sends = call(
            plan,
            lambda *refs: z_pack_kernel(plan, *refs),
            [(plan.payload, 128)] * 2,
            [],
            *beside,
            *edges[::-1],
            *z_own,
        )
        arrived = [swap(sends[1], 1, None, None), swap(sends[0], 0, None, None)][::-1]
        (own,) = call(
            plan,
            lambda *refs: own_kernel(plan, *refs),
            [(2, *full)],
            [(2, 16, plan.rows, 128), (2, 4, plan.rows, 128)],
            cells,
            *beside,
            *edges[::-1],
        )
        chunk, *state = call(
            plan,
            lambda *refs: down_kernel(plan, *refs),
            [(plan.devices, 8, 128)] + [full_rim] + [full] * 3 + [half_rim] + [half] * 3,
            [full] * 2
            + [half] * 2
            + [(2, 2, EDGE, plan.rows, 128), (2, 4, plan.rows, 128)],
            own,
            *z_own[::-1],
            *arrived[::-1],
        )
        joined = lax.all_to_all(chunk, AXES, 0, 0, tiled=True)
        levels = [Level(plan, level) for level in range(2, LEVELS + 1)]
        margin = 0 if near == 1 else 16
        (out,) = call(
            plan,
            lambda *refs: up_kernel(plan, *refs),
            [(16, 16, 128)],
            [full] * 2
            + [half] * 2
            + [(tile, LW)]
            + [(z2, y2, 128)] * 2
            + [(z2 + 2 * HALO, y2 + margin, 128)]
            + [level.shape for level in levels[:-1]]
            + [level.shape for level in levels[1:]],
            joined,
            *state,
        )
        return out

    spec = P(*AXES)
    return jax.shard_map(
        on_device, mesh=mesh, in_specs=(spec, spec), out_specs=spec, check_vma=False
    )
```

```python
import jax
import jax.numpy as jnp
import numpy as np
from jax import lax
from jax.experimental import pallas as pl
from jax.experimental.pallas import tpu as pltpu
from jax.sharding import PartitionSpec as P

LEVELS = 5
COARSE = 8
AXES = ("grp", "gy", "gx")
F32 = jnp.float32

HALO = 3
ZW = 4 + 2 * HALO
XW = 32 + 2 * HALO
LW = 384
EDGE = 4 * HALO
M_DEEP, M_FAR, R_DEEP, R_FAR = 11, 4, 10, 3

NEAR_TILES = (
    [[(1, d, 0)] for d in range(1, 7)]
    + [[(0, d, 0)] for d in range(1, 6)]
    + [[(1, 7, 0), (1, 11, 6)], [(1, 8, 0), (1, 10, 5)], [(0, 6, 0), (0, 10, 6)]]
    + [[(0, 7, 0), (0, 9, 5)], [(1, 9, 0), (0, 8, 4)]]
)
FAR_TILES = [[(1, 1, 0), (1, 2, 3), (0, 1, 6)], [(0, 2, 0), (1, 3, 2), (0, 3, 4), (1, 4, 5)]]
BESIDE_ROWS = 8 * (len(NEAR_TILES) + len(FAR_TILES) + 1)
M_EDGE, R_EDGE = 11, 10
Y_FAR = 3
Y_ROWS = 16 * (8 + Y_FAR)


def lane_iota(rows=8):
    return lax.broadcasted_iota(jnp.int32, (rows, 128), 1)


LANES = lax.GatherDimensionNumbers(
    offset_dims=(),
    collapsed_slice_dims=(1,),
    start_index_map=(1,),
    operand_batching_dims=(0,),
    start_indices_batching_dims=(0,),
)


def gather(source, index):
    return lax.gather(
        source, index[..., None], LANES, (1, 1), mode=lax.GatherScatterMode.PROMISE_IN_BOUNDS
    )


def every_lane(offset, px, rows):
    return (4 * lane_iota(rows) + ((px - 4 * offset) % 128)) & 127


def between(low, high, rows=8):
    lane = lane_iota(rows)
    return (lane >= low) & (lane < high)


def window_cells(t, rows):
    cell = lane_iota(rows) + 128 * t
    z = jnp.zeros((rows, 128), jnp.int32)
    for k in range(1, ZW + 1):
        z = z + (cell >= k * XW).astype(jnp.int32)
    return z, cell - z * XW


EDGE_STARTS = {(1, 0): 0, (1, 1): 33, (0, 0): 66, (0, 1): 96}


def edge_send_lanes():
    lane = lane_iota()
    mobile = lane < 66
    right = ((lane >= 33) & mobile) | (lane >= 96)
    start = jnp.where(mobile, jnp.where(right, 33, 0), jnp.where(right, 96, 66))
    width = jnp.where(mobile, M_EDGE, R_EDGE)
    t = lane - start
    z = (t >= width).astype(jnp.int32) + (t >= 2 * width).astype(jnp.int32)
    first = jnp.where(right, 0, EDGE - width)
    return jnp.minimum(jnp.where(mobile, 48, 0) + z * 12 + first + t - z * width, 95), right


def edge_own_lanes(side, t, rows):
    z, x = window_cells(t, rows)
    x = x if side == 0 else x - (XW - HALO)
    here = (z >= HALO) & (z < HALO + 4) & (x >= 0) & (x < HALO)
    return jnp.where(here, (z - HALO) * 12 + 4 * x, 0), here


def halo_start(side):
    return 0 if side == 0 else (HALO + 4) * XW - 256


def halo_cells(side, px, rows):
    p = (lane_iota(rows) - (halo_start(side) + 32 * px)) & 127
    z = (p >= XW).astype(jnp.int32) + (p >= 2 * XW).astype(jnp.int32)
    return z, p - z * XW, p < HALO * XW


def halo_turn(side, px, rows):
    z, x, _ = halo_cells(side, px, rows)
    return jnp.where((x >= HALO) & (x < XW - HALO), z, 3)


def halo_lanes(side, z, rows):
    q = (lane_iota(rows) - (halo_start(side) + z * XW + HALO)) & 127
    return 4 * (q & 31) + lax.shift_right_logical(q, 5)


def edge_far_lanes(side, a, rows):
    width = M_EDGE if a == 1 else R_EDGE
    index = jnp.zeros((rows, 128), jnp.int32)
    for px in range(4):
        z, x, here = halo_cells(side, px, rows)
        left = EDGE_STARTS[a, 0] + z * width + 4 * x + px - (EDGE - width)
        right = EDGE_STARTS[a, 1] + z * width + 4 * (x - (XW - HALO)) + px
        index = jnp.where(here & (x < HALO), left, index)
        index = jnp.where(here & (x >= XW - HALO), right, index)
    return jnp.clip(index, 0, 127)


class Plan:
    def __init__(self, mesh):
        self.counts = tuple(mesh.shape[axis] for axis in AXES)
        self.near = 1 if self.counts[1] == 2 else 2
        self.rows = 16 * (1 + self.near)
        self.cells = self.rows // 4
        self.tile = -(-self.cells // 8) * 8
        self.edge_start = BESIDE_ROWS * self.near
        self.payload = self.edge_start + 32 * (2 + self.near)
        self.devices = self.counts[0] * self.counts[1] * self.counts[2]
        self.coarse = (4 * self.counts[0], 4 * self.counts[1], 32 * self.counts[2])

    def pairs(self, swaps):
        out = []
        for index in np.ndindex(*self.counts):
            there = []
            for axis, swap in enumerate(swaps):
                i, n = index[axis], self.counts[axis]
                j = i if swap is None else (i + 1 if i % 2 == swap else i - 1)
                if axis == 2:
                    j = j % n
                there.append(j)
            if not all(0 <= j < n for j, n in zip(there, self.counts)):
                there = [index[0], index[1], index[2] ^ 1]
            out.append(
                (
                    int(np.ravel_multi_index(index, self.counts)),
                    int(np.ravel_multi_index(there, self.counts)),
                )
            )
        return out

    def y_places(self):
        iy = lax.axis_index("gy")
        if self.near == 1:
            return 16 * iy, [(1 - iy, 16 * (1 - iy))]
        odd = lax.rem(iy, 2)
        return 16, [(1 - odd, 32 * (1 - odd)), (odd, 32 * odd)]


def is_even(axis):
    return lax.rem(lax.axis_index(axis), 2) == 0


def at(start, size):
    if isinstance(start, int):
        return pl.ds(start, size)
    return pl.ds(pl.multiple_of(start, 8), size)


def first_kernel(plan, cells_ref, *outs):
    z_even = is_even("grp")
    for swap, out in enumerate(outs[:2]):
        top = z_even if swap == 0 else jnp.logical_not(z_even)
        row = 0
        for a, deep in ((1, M_DEEP), (0, R_DEEP)):
            for d in range(1, deep + 1):
                out[row : row + 16, :] = cells_ref[a, jnp.where(top, 16 - d, d - 1)]
                row += 16
    for out, (side, _) in zip(outs[2:], plan.y_places()[1]):
        last = side == 1
        for a in range(2):
            near, far = a * Y_ROWS, a * Y_ROWS + 128
            for plane in range(16):
                cells = cells_ref[a, plane]
                rows = jnp.where(last, cells[8:16], cells[0:8])
                out[near + 8 * plane : near + 8 * plane + 8, :] = rows
                rows = jnp.where(last, cells[8 - Y_FAR : 8], cells[8 : 8 + Y_FAR])
                out[far + Y_FAR * plane : far + Y_FAR * (plane + 1), :] = rows


def edges_kernel(plan, *refs):
    cells_ref = refs[0]
    arrived = refs[1 : 1 + plan.near]
    beside = refs[1 + plan.near : 1 + 2 * plan.near]
    even_ref, odd_ref = refs[-2:]
    own_row, places = plan.y_places()
    even = is_even("gx")
    for ref, out, (side, _) in zip(arrived, beside, places):
        following = side == 1
        for a in range(2):
            near, far = a * Y_ROWS, a * Y_ROWS + 128
            for plane in range(16):
                rows = ref[near + 8 * plane : near + 8 * plane + 8, :]
                more = ref[far + Y_FAR * plane : far + Y_FAR * (plane + 1), :]
                none = jnp.zeros((8 - Y_FAR, 128), F32)
                after = jnp.concatenate([more, none], axis=0)
                before = jnp.concatenate([none, more], axis=0)
                out[a, plane, 0:8, :] = jnp.where(following, rows, before)
                out[a, plane, 8:16, :] = jnp.where(following, after, rows)
    for i, block in enumerate((cells_ref, *beside)):
        start = own_row if i == 0 else places[i - 1][1]
        for pz in range(4):
            for half in range(2):
                to_right = jnp.zeros((8, 128), F32)
                to_left = jnp.zeros((8, 128), F32)
                for a in range(2):
                    for z in range(4):
                        cells = block[a, 4 * z + pz, 8 * half : 8 * half + 8, :]
                        base = a * 48 + z * 12
                        here = between(base, base + EDGE)
                        shift = (base - (128 - EDGE)) % 128
                        to_right = jnp.where(here, pltpu.roll(cells, shift, 1), to_right)
                        to_left = jnp.where(here, pltpu.roll(cells, base, 1), to_left)
                rows = at(start + 8 * half, 8)
                even_ref[pz, rows, :] = jnp.where(even, to_right, to_left)
                odd_ref[pz, rows, :] = jnp.where(even, to_left, to_right)


def packed(pieces, following):
    row = lax.broadcasted_iota(jnp.int32, (8, 128), 0)
    row = jnp.where(following, row, 7 - row)
    out = None
    for value, first in pieces:
        if out is None:
            out = value
        else:
            moved = pltpu.roll(value, jnp.where(following, first, 8 - first), 0)
            out = jnp.where(row >= first, moved, out)
    return out


def unpacked(value, first, following):
    if first == 0:
        return value
    return pltpu.roll(value, jnp.where(following, 8 - first, first), 0)


def z_pack_kernel(plan, *refs):
    near = plan.near
    beside = refs[:near]
    x_odd_ref, x_even_ref = refs[near : near + 2]
    outs = refs[-2:]
    own_row, places = plan.y_places()
    x_even = is_even("gx")
    z_even = is_even("grp")
    lanes_0, use_right = edge_send_lanes()
    for swap, out in enumerate(outs):
        top = z_even if swap == 0 else jnp.logical_not(z_even)
        lanes = lanes_0 + jnp.where(top, 12, 0)

        def edge(pz, row):
            even, odd = x_even_ref[pz, at(row, 8), :], x_odd_ref[pz, at(row, 8), :]
            left = gather(jnp.where(x_even, odd, even), lanes)
            right = gather(jnp.where(x_even, even, odd), lanes)
            return jnp.where(use_right, right, left)

        for i, (side, base) in enumerate(places):
            following = side == 1
            to = i * BESIDE_ROWS
            for tiles, row in ((NEAR_TILES, 8 * (1 - side)), (FAR_TILES, 8 * side)):
                for pieces in tiles:
                    values = [
                        (beside[i][a, jnp.where(top, 16 - d, d - 1), at(row, 8), :], first)
                        for a, d, first in pieces
                    ]
                    out[to : to + 8, :] = packed(values, following)
                    to += 8
            values = [(edge(pz, base + 8 * side), 2 * pz) for pz in range(4)]
            out[to : to + 8, :] = packed(values, following)
        to = plan.edge_start
        rows = [own_row, own_row + 8] + [base + 8 * (1 - side) for side, base in places]
        for pz in range(4):
            for row in rows:
                out[to : to + 8, :] = edge(pz, row)
                to += 8


def padded_rows(plan, cells):
    if plan.cells == plan.tile:
        return cells
    return jnp.concatenate(
        [cells, jnp.zeros((plan.tile - plan.cells, cells.shape[1]), F32)], axis=0
    )


def every_fourth(plan, ref, lead, py):
    return padded_rows(plan, ref[(*lead, pl.ds(py, plan.cells, 4), slice(None))])


def own_kernel(plan, *refs):
    near = plan.near
    cells_ref, *beside = refs[: 1 + near]
    x_odd_ref, x_even_ref = refs[1 + near : 3 + near]
    out, planes, sides = refs[-3:]
    tile = plan.tile
    own_row, places = plan.y_places()
    x_even = is_even("gx")
    planes[:, :, at(own_row, 16), :] = cells_ref[...]
    for (_, base), block in zip(places, beside):
        planes[:, :, at(base, 16), :] = block[...]
    even, odd = x_even_ref[...], x_odd_ref[...]
    sides[0] = jnp.where(x_even, odd, even)
    sides[1] = jnp.where(x_even, even, odd)

    inside = inside_mask(plan)
    offsets = [(z + HALO) * XW + HALO for z in range(4)]
    index = [[every_lane(offset, px, tile) for px in range(4)] for offset in offsets]
    from_edge = {(s, t): edge_own_lanes(s, t, tile) for s, t in ((0, 0), (0, 1), (1, 1), (1, 2))}

    def body(pz, carry):
        for a in range(2):
            for py in range(4):
                cells = [every_fourth(plan, planes, (a, 4 * z + pz), py) for z in range(4)]
                side = [every_fourth(plan, sides, (s, pz), py) for s in range(2)]
                for px in range(4):
                    parts = [gather(cells[z], index[z][px]) for z in range(4)]
                    for t in range(3):
                        value = jnp.zeros((tile, 128), F32)
                        for z in range(4):
                            offset = offsets[z] - 128 * t
                            low, high = max(offset, 0), min(offset + 32, 128)
                            if low < high:
                                value = jnp.where(between(low, high, tile), parts[z], value)
                        for s in range(2):
                            if (s, t) in from_edge:
                                lanes, here = from_edge[s, t]
                                lanes = lanes + (48 * a + px)
                                value = jnp.where(here, gather(side[s], lanes), value)
                        lanes = slice(128 * t, 128 * t + 128)
                        out[a, pz, py, px, :, lanes] = jnp.where(inside[:, lanes], value, 0.0)
        return carry

    lax.fori_loop(0, 4, body, 0)


def inside_tile(plan, t):
    tile = plan.tile
    z, x = window_cells(t, tile)
    here = z < ZW
    z = z + (4 * lax.axis_index("grp") - HALO)
    x = x + (32 * lax.axis_index("gx") - HALO)
    here = here & (z >= 0) & (z < plan.coarse[0]) & (x >= 0) & (x < plan.coarse[2])
    if plan.near == 2:
        row = lax.broadcasted_iota(jnp.int32, (tile, 128), 0)
        y = row + (4 * lax.axis_index("gy") - 4)
        here = here & (row < plan.cells) & (y >= 0) & (y < plan.coarse[1])
    return here


def inside_mask(plan):
    masks = [jnp.where(inside_tile(plan, t), 1.0, 0.0) for t in range(3)]
    return jnp.concatenate(masks, axis=1) > 0.5


def roll_lanes(value, shift):
    return pltpu.roll(value, shift % LW, 1)


def fill_rim(plan, ref, n):
    tile = plan.tile
    row = lax.broadcasted_iota(jnp.int32, (tile, LW), 0)
    for i in range(1, n + 1):
        for j in range(1, n + 1):
            z_low, z_high = ref[n, i, j], ref[1, i, j]
            y_low, y_high = ref[i, n, j], ref[i, 1, j]
            x_low, x_high = ref[i, j, n], ref[i, j, 1]
            ref[0, i, j] = roll_lanes(z_low, XW)
            ref[n + 1, i, j] = roll_lanes(z_high, -XW)
            ref[i, 0, j] = jnp.where(row == 0, 0.0, pltpu.roll(y_low, 1, 0))
            ref[i, n + 1, j] = jnp.where(
                row == tile - 1, 0.0, pltpu.roll(y_high, tile - 1, 0)
            )
            ref[i, j, 0] = roll_lanes(x_low, 1)
            ref[i, j, n + 1] = roll_lanes(x_high, -1)


def around(ref, a, b, c):
    return (
        ref[a, b + 1, c + 1],
        ref[a + 2, b + 1, c + 1],
        ref[a + 1, b, c + 1],
        ref[a + 1, b + 2, c + 1],
        ref[a + 1, b + 1, c],
        ref[a + 1, b + 1, c + 2],
    )


def around_rimless(plan, ref, n, a, b, c):
    tile = plan.tile
    row = lax.broadcasted_iota(jnp.int32, (tile, LW), 0)
    return (
        ref[a - 1, b, c] if a > 0 else roll_lanes(ref[n - 1, b, c], XW),
        ref[a + 1, b, c] if a < n - 1 else roll_lanes(ref[0, b, c], -XW),
        ref[a, b - 1, c] if b > 0 else jnp.where(row == 0, 0.0, pltpu.roll(ref[a, n - 1, c], 1, 0)),
        ref[a, b + 1, c]
        if b < n - 1
        else jnp.where(row == tile - 1, 0.0, pltpu.roll(ref[a, 0, c], tile - 1, 0)),
        ref[a, b, c - 1] if c > 0 else roll_lanes(ref[a, b, n - 1], 1),
        ref[a, b, c + 1] if c < n - 1 else roll_lanes(ref[a, b, 0], -1),
    )


def pull(plan, n, m_ref, v_ref, h_ref, a, b, c):
    cells = around_rimless(plan, v_ref, n, a, b, c)
    mobility = around(m_ref, a, b, c)
    total = ((cells[0] + cells[1]) + (cells[2] + cells[3])) + (cells[4] + cells[5])
    products = [m * v for m, v in zip(mobility, cells)]
    other = ((products[0] + products[1]) + (products[2] + products[3])) + (
        products[4] + products[5]
    )
    return h_ref[a, b, c] * (m_ref[a + 1, b + 1, c + 1] * total + other)


def descend(plan, n, factor, inside, m_ref, r_ref, d_ref, h_ref, e_ref, k_ref):
    fill_rim(plan, m_ref, n)
    for a, b, c in np.ndindex(n, n, n):
        s = around(m_ref, a, b, c)
        d = 3.0 * m_ref[a + 1, b + 1, c + 1] + 0.5 * (
            ((s[0] + s[1]) + (s[2] + s[3])) + (s[4] + s[5])
        )
        h = jnp.where(inside, 0.4 / d, 0.0)
        d_ref[a, b, c] = d
        h_ref[a, b, c] = h
        e_ref[a, b, c] = (2.0 / factor) * h * r_ref[a, b, c]
    for a, b, c in np.ndindex(n, n, n):
        k_ref[a, b, c] = 1.2 * e_ref[a, b, c] + pull(plan, n, m_ref, e_ref, h_ref, a, b, c)


def leftover(plan, n, factor, m_ref, r_ref, d_ref, h_ref, k_ref, a, b, c):
    away = k_ref[a, b, c] - 1.25 * pull(plan, n, m_ref, k_ref, h_ref, a, b, c)
    return r_ref[a, b, c] - factor * (d_ref[a, b, c] * away)


def place_halo(plan, swap, own_ref, z_own_ref, z_ref, planes, sides, emit):
    near, tile = plan.near, plan.tile
    own_row, places = plan.y_places()
    upper = is_even("grp")
    if swap == 1:
        upper = jnp.logical_not(upper)

    def choose(make):
        return jnp.where(upper, make(1), make(0))

    def plane_of(d):
        return jnp.where(upper, d - 1, EDGE - d)

    for a, deep, far in ((1, M_DEEP, M_FAR), (0, R_DEEP, R_FAR)):
        for d in range(far + 1, EDGE + 1):
            planes[a, plane_of(d)] = jnp.zeros((plan.rows, 128), F32)
        for d in range(1, deep + 1):
            row = 16 * (d - 1) if a == 1 else 16 * (M_DEEP + d - 1)
            planes[a, plane_of(d), at(own_row, 16), :] = z_own_ref[row : row + 16, :]
    for i, (side, base) in enumerate(places):
        following = side == 1
        row = i * BESIDE_ROWS
        for tiles, to in ((NEAR_TILES, base + 8 * (1 - side)), (FAR_TILES, base + 8 * side)):
            for pieces in tiles:
                for a, d, first in pieces:
                    planes[a, plane_of(d), at(to, 8), :] = unpacked(
                        z_ref[row : row + 8, :], first, following
                    )
                row += 8
        for pz in range(4):
            sides[pz, at(base + 8 * side, 8), :] = unpacked(
                z_ref[row : row + 8, :], 2 * pz, following
            )
    row = plan.edge_start
    rows = [own_row, own_row + 8] + [base + 8 * (1 - side) for side, base in places]
    for pz in range(4):
        for to in rows:
            sides[pz, at(to, 8), :] = z_ref[row : row + 8, :]
            row += 8

    index = [choose(lambda side: halo_lanes(side, z, tile)) for z in range(HALO)]
    turns = [choose(lambda side: halo_turn(side, px, tile)) for px in range(4)]
    edge_index = [choose(lambda side: edge_far_lanes(side, a, tile)) for a in range(2)]

    def kept(side):
        z, _ = window_cells(2 * side, tile)
        z = (z < HALO) if side == 0 else (z >= HALO + 4)
        return (z & inside_tile(plan, 2 * side)).astype(jnp.int32)

    keep = choose(kept) > 0
    lanes = pl.ds(pl.multiple_of(jnp.where(upper, 256, 0), 128), 128)

    def place(pz, carry):
        for a in range(2):
            for py in range(4):
                parts = [
                    gather(every_fourth(plan, planes, (a, 4 * z + pz), py), index[z])
                    for z in range(HALO)
                ]
                edge = gather(every_fourth(plan, sides, (pz,), py), edge_index[a])
                for px in range(4):
                    turn = turns[px]
                    value = jnp.where(turn == 1, parts[1], parts[0])
                    value = jnp.where(turn == 2, parts[2], value)
                    value = jnp.where(turn == 3, edge, value)
                    if px > 0:
                        value = pltpu.roll(value, 128 - 32 * px, 1)
                    value = jnp.where(keep, value, own_ref[a, pz, py, px, :, lanes])
                    emit(a, pz, py, px, lanes, value)
        return carry

    lax.fori_loop(0, 4, place, 0)


def place_kernel(plan, own_ref, z_own_ref, z_ref, out, planes, sides):
    def emit(a, pz, py, px, lanes, value):
        out[a, pz, py, px] = value

    place_halo(plan, 1, own_ref, z_own_ref, z_ref, planes, sides, emit)


def down_kernel(plan, *refs):
    own_ref, other_ref, z_own_ref, z_ref = refs[:4]
    chunk, m0, h0, e0, k0, m1, h1, e1, k1 = refs[4:13]
    r0, d0, r1, d1, planes, sides = refs[13:]
    tile = plan.tile
    inside = inside_mask(plan)
    rest = pl.ds(pl.multiple_of(jnp.where(is_even("grp"), 0, 256), 128), 128)

    def emit(a, pz, py, px, lanes, value):
        for lanes_i, value_i in (
            (lanes, value),
            (rest, other_ref[a, pz, py, px]),
            (slice(128, 256), own_ref[a, pz, py, px, :, 128:256]),
        ):
            if a == 1:
                m0[pz + 1, py + 1, px + 1, :, lanes_i] = value_i
            else:
                r0[pz, py, px, :, lanes_i] = value_i

    place_halo(plan, 0, own_ref, z_own_ref, z_ref, planes, sides, emit)

    descend(plan, 4, 1.0, inside, m0, r0, d0, h0, e0, k0)
    for a, b, c in np.ndindex(2, 2, 2):
        rest = jnp.zeros((tile, LW), F32)
        mobility = jnp.zeros((tile, LW), F32)
        for da, db, dc in np.ndindex(2, 2, 2):
            i, j, k = 2 * a + da, 2 * b + db, 2 * c + dc
            rest = rest + leftover(plan, 4, 1.0, m0, r0, d0, h0, k0, i, j, k)
            mobility = mobility + m0[i + 1, j + 1, k + 1]
        r1[a, b, c] = 0.125 * rest
        m1[a + 1, b + 1, c + 1] = 0.125 * mobility
    descend(plan, 2, 0.25, inside, m1, r1, d1, h1, e1, k1)
    rest = jnp.zeros((tile, LW), F32)
    mobility = jnp.zeros((tile, LW), F32)
    for a, b, c in np.ndindex(2, 2, 2):
        rest = rest + leftover(plan, 2, 0.25, m1, r1, d1, h1, k1, a, b, c)
        mobility = mobility + m1[a + 1, b + 1, c + 1]
    both = []
    for total in (rest, mobility):
        packed = jnp.zeros((tile, 128), F32)
        for t in range(3):
            part = 0.125 * total[:, 128 * t : 128 * t + 128]
            for z in range(4):
                offset = (z + HALO) * XW + HALO - 128 * t
                low, high = max(offset, 0), min(offset + 32, 128)
                if low < high:
                    move = 32 * z - offset
                    packed = jnp.where(
                        between(low + move, high + move, tile),
                        pltpu.roll(part, move % 128, 1),
                        packed,
                    )
        both.append(own_rows(plan, packed))
    block = jnp.concatenate(both, axis=0)

    def put(i, carry):
        chunk[i] = block
        return carry

    lax.fori_loop(0, plan.devices, put, 0, unroll=8)


def own_rows(plan, cells):
    if plan.near == 1:
        return jnp.where(lax.axis_index("gy") == 0, cells[0:4], cells[4:8])
    return cells[4:8]


class Level:
    def __init__(self, plan, level):
        self.size = tuple(n >> (level - 2) for n in plan.coarse)
        self.tile = max(8, self.size[1])
        self.shape = (self.size[0], self.tile, 128)
        self.factor = 0.25**level

    def shifts(self, v):
        z, y, x = self.size
        if z > 1:
            none = jnp.zeros((1, self.tile, 128), F32)
            yield jnp.concatenate([none, v[:-1]], axis=0)
            yield jnp.concatenate([v[1:], none], axis=0)
        else:
            yield jnp.zeros_like(v)
            yield jnp.zeros_like(v)
        row = lax.broadcasted_iota(jnp.int32, self.shape, 1)
        lane = lax.broadcasted_iota(jnp.int32, self.shape, 2)
        up, down = pltpu.roll(v, 1, 1), pltpu.roll(v, self.tile - 1, 1)
        if y == self.tile:
            up = jnp.where(row == 0, 0.0, up)
            down = jnp.where(row == self.tile - 1, 0.0, down)
        yield up
        yield down
        left, right = pltpu.roll(v, 1, 2), pltpu.roll(v, 127, 2)
        if x == 128:
            left = jnp.where(lane == 0, 0.0, left)
            right = jnp.where(lane == 127, 0.0, right)
        yield left
        yield right

    def prepare(self, mobility, source):
        z, y, x = self.size
        row = lax.broadcasted_iota(jnp.int32, self.shape, 1)
        lane = lax.broadcasted_iota(jnp.int32, self.shape, 2)
        inside = (row < y) & (lane < x)
        sums = [mobility + near for near in self.shifts(mobility)]
        self.diagonal = 0.5 * (
            ((sums[0] + sums[1]) + (sums[2] + sums[3])) + (sums[4] + sums[5])
        )
        h = jnp.where(inside, 0.4 / self.diagonal, 0.0)
        self.weights = [h * s for s in sums]
        self.first = (2.0 / self.factor) * h * source
        self.source = source

    def pull(self, v):
        t = [w * near for w, near in zip(self.weights, self.shifts(v))]
        return ((t[0] + t[1]) + (t[2] + t[3])) + (t[4] + t[5])

    def relax(self, v):
        return 0.2 * v + self.first + self.pull(v)

    def leftover(self, v):
        return self.source - self.factor * (self.diagonal * (v - 1.25 * self.pull(v)))


def lanes_2d(values, index):
    flat = values.reshape(-1, 128)
    rows = flat.shape[0]
    lane = lax.broadcasted_iota(jnp.int32, (rows, 128), 1)
    return gather(flat, index(lane)).reshape(values.shape)


def coarsen(values, fine, coarse, fine_ref, coarse_ref):
    z, y, x = coarse.size
    tile = fine.tile
    pairs = values.reshape(z, 2, tile, 128)
    fine_ref[0:z] = pairs[:, 0] + pairs[:, 1]
    rows = fine_ref[0:z, pl.ds(0, y, 2), :] + fine_ref[0:z, pl.ds(1, y, 2), :]
    coarse_ref[0:z, 0:y, :] = rows
    full = coarse_ref[0:z]
    full = full + pltpu.roll(full, 127, 2)
    full = lanes_2d(full, lambda lane: (2 * lane) & 127)
    lane = lax.broadcasted_iota(jnp.int32, full.shape, 2)
    return jnp.where(lane < x, 0.125 * full, 0.0)


def refine(values, fine, coarse, fine_ref):
    z, y, x = coarse.size
    wide = lanes_2d(values, lambda lane: lax.shift_right_logical(lane, 1))
    fine_ref[0:z, pl.ds(0, y, 2), :] = wide[:, 0:y]
    fine_ref[0:z, pl.ds(1, y, 2), :] = wide[:, 0:y]
    rows = fine_ref[0:z]
    return jnp.broadcast_to(rows[:, None], (z, 2, fine.tile, 128)).reshape(fine.shape)


def ascend(plan, n, m_ref, h_ref, e_ref, k_ref, below, v_ref, w_ref):
    for a, b, c in np.ndindex(n, n, n):
        v_ref[a, b, c] = k_ref[a, b, c] + below(a, b, c)
    for old, new in ((v_ref, w_ref), (w_ref, v_ref)):
        for a, b, c in np.ndindex(n, n, n):
            new[a, b, c] = (
                0.2 * old[a, b, c]
                + e_ref[a, b, c]
                + pull(plan, n, m_ref, old, h_ref, a, b, c)
            )


def up_kernel(plan, *refs):
    joined, m0, h0, e0, k0, m1, h1, e1, k1, out = refs[:10]
    v0, w0, v1, w1, window, r2, m2, v2 = refs[10:18]
    fine_refs = refs[18:21]
    coarse_refs = refs[21:24]
    tile = plan.tile
    gz, gy, gx = plan.counts
    iz, iy, ix = (lax.axis_index(axis) for axis in AXES)
    inside = inside_mask(plan)

    def unpack(z_block, carry):
        for z in range(4):
            for y_block in range(gy):
                value = jnp.zeros((8, 128), F32)
                for x_block in range(gx):
                    part = joined[(z_block * gy + y_block) * gx + x_block]
                    value = jnp.where(
                        between(32 * x_block, 32 * x_block + 32),
                        pltpu.roll(part, (32 * (x_block - z)) % 128, 1),
                        value,
                    )
                rows = slice(4 * y_block, 4 * y_block + 4)
                r2[4 * z_block + z, rows, :] = value[0:4]
                m2[4 * z_block + z, rows, :] = value[4:8]
        return carry

    lax.fori_loop(0, gz, unpack, 0)
    for ref in (*fine_refs, *coarse_refs):
        ref[...] = jnp.zeros(ref.shape, F32)

    levels = [Level(plan, level) for level in range(2, LEVELS + 1)]
    mobility, source = m2[...], r2[...]
    kept = []
    for i, level in enumerate(levels):
        level.prepare(mobility, source)
        if i < len(levels) - 1:
            e = level.first + level.first * 0.2 + level.pull(level.first)
            kept.append(e)
            args = (level, levels[i + 1], fine_refs[i], coarse_refs[i])
            mobility = coarsen(mobility, *args)
            source = coarsen(level.leftover(e), *args)
    level = levels[-1]
    v = level.first
    for repeat in range(COARSE - 1):
        v = level.relax(v)
    for i in range(len(levels) - 2, -1, -1):
        v = kept[i] + refine(v, levels[i], levels[i + 1], fine_refs[i])
        v = levels[i].relax(levels[i].relax(v))

    v2[...] = jnp.zeros(v2.shape, F32)
    margin = 0 if plan.near == 1 else 8
    v2[pl.ds(HALO, plan.coarse[0]), pl.ds(margin, plan.coarse[1]), :] = v
    planes = []
    for z in range(ZW):
        if plan.near == 1:
            planes.append(v2[4 * iz + z])
        else:
            planes.append(v2[4 * iz + z, pl.ds(4 * iy + 4, tile), :])
    for t in range(3):
        value = jnp.zeros((tile, 128), F32)
        for z in range(ZW):
            offset = z * XW - 128 * t
            low, high = max(offset, 0), min(offset + XW, 128)
            if low < high:
                shift = lax.rem(offset % 128 + HALO - 32 * ix + 256, 128)
                value = jnp.where(
                    between(low, high, tile), pltpu.roll(planes[z], shift, 1), value
                )
        lanes = slice(128 * t, 128 * t + 128)
        window[:, lanes] = jnp.where(inside[:, lanes], value, 0.0)

    below = window[...]

    ascend(plan, 2, m1, h1, e1, k1, lambda a, b, c: below, v1, w1)
    ascend(plan, 4, m0, h0, e0, k0, lambda a, b, c: v1[a // 2, b // 2, c // 2], v0, w0)

    lane = lane_iota(tile)
    natural = 32 * (lane & 3) + lax.shift_right_logical(lane, 2)
    starts = [(z + HALO) * XW + HALO for z in range(4)]
    places_of = [(lane - start) & 127 for start in starts]
    index = [(natural + start) & 127 for start in starts]

    def store(pz, carry):
        for py in range(4):
            parts = [
                [v0[pz, py, px, :, 128 * t : 128 * t + 128] for t in range(3)]
                for px in range(4)
            ]
            parts = [
                [part if px == 0 else pltpu.roll(part, 32 * px, 1) for part in row]
                for px, row in enumerate(parts)
            ]
            for z, start in enumerate(starts):
                low, high = start // 128, (start + 31) // 128
                value = None
                for px in range(4):
                    part = parts[px][low]
                    if low != high:
                        first = (places_of[z] & 31) < 128 - start % 128
                        part = jnp.where(first, part, parts[px][high])
                    turn = lax.shift_right_logical(places_of[z], 5) == px
                    value = part if value is None else jnp.where(turn, part, value)
                value = gather(value, index[z])
                out[4 * z + pz, pl.ds(py, 4, 4), :] = own_rows(plan, value)
        return carry

    lax.fori_loop(0, 4, store, 0, unroll=4)


def call(plan, kernel, outs, scratch, *args):
    return pl.pallas_call(
        kernel,
        out_shape=[jax.ShapeDtypeStruct(shape, F32) for shape in outs],
        scratch_shapes=[pltpu.VMEM(shape, F32) for shape in scratch],
        compiler_params=pltpu.CompilerParams(
            vmem_limit_bytes=(3 * plan.tile + plan.coarse[0] // 4) * 1024 * 1024
        ),
    )(*args)


def solution(mesh):
    plan = Plan(mesh)
    near, tile = plan.near, plan.tile
    z2, y2, x2 = plan.coarse
    full = (4, 4, 4, tile, LW)
    half = (2, 2, 2, tile, LW)
    full_rim = (6, 6, 6, tile, LW)
    half_rim = (4, 4, 4, tile, LW)

    def swap(values, *swaps):
        return lax.ppermute(values, AXES, plan.pairs(swaps))

    def on_device(residual, mobility):
        assert residual.shape == (16, 16, 128)
        cells = jnp.stack([residual, mobility])
        even, odd, *rows = call(
            plan,
            lambda *refs: first_kernel(plan, *refs),
            [(16 * (M_DEEP + R_DEEP), 128)] * 2 + [(2 * Y_ROWS, 128)] * near,
            [],
            cells,
        )
        arrived = [swap(values, None, y, None) for y, values in enumerate(rows)]
        z_own = [swap(odd, 1, None, None), swap(even, 0, None, None)][::-1]
        *beside, even, odd = call(
            plan,
            lambda *refs: edges_kernel(plan, *refs),
            [(2, 16, 16, 128)] * near + [(4, plan.rows, 128)] * 2,
            [],
            cells,
            *arrived,
        )
        edges = [swap(odd, None, None, 1), swap(even, None, None, 0)][::-1]
        sends = call(
            plan,
            lambda *refs: z_pack_kernel(plan, *refs),
            [(plan.payload, 128)] * 2,
            [],
            *beside,
            *edges[::-1],
            *z_own,
        )
        arrived = [swap(sends[1], 1, None, None), swap(sends[0], 0, None, None)][::-1]
        (own,) = call(
            plan,
            lambda *refs: own_kernel(plan, *refs),
            [(2, *full)],
            [(2, 16, plan.rows, 128), (2, 4, plan.rows, 128)],
            cells,
            *beside,
            *edges[::-1],
        )
        halo_scratch = [(2, EDGE, plan.rows, 128), (4, plan.rows, 128)]
        (other,) = call(
            plan,
            lambda *refs: place_kernel(plan, *refs),
            [(2, 4, 4, 4, tile, 128)],
            halo_scratch,
            own,
            z_own[1],
            arrived[1],
        )
        chunk, *state = call(
            plan,
            lambda *refs: down_kernel(plan, *refs),
            [(plan.devices, 8, 128)] + [full_rim] + [full] * 3 + [half_rim] + [half] * 3,
            [full] * 2
            + [half] * 2
            + halo_scratch,
            own,
            other,
            z_own[0],
            arrived[0],
        )
        joined = lax.all_to_all(chunk, AXES, 0, 0, tiled=True)
        levels = [Level(plan, level) for level in range(2, LEVELS + 1)]
        margin = 0 if near == 1 else 16
        (out,) = call(
            plan,
            lambda *refs: up_kernel(plan, *refs),
            [(16, 16, 128)],
            [full] * 2
            + [half] * 2
            + [(tile, LW)]
            + [(z2, y2, 128)] * 2
            + [(z2 + 2 * HALO, y2 + margin, 128)]
            + [level.shape for level in levels[:-1]]
            + [level.shape for level in levels[1:]],
            joined,
            *state,
        )
        return out

    spec = P(*AXES)
    return jax.shard_map(
        on_device, mesh=mesh, in_specs=(spec, spec), out_specs=spec, check_vma=False
    )
```

```python
import jax
import jax.numpy as jnp
import numpy as np
from jax import lax
from jax.experimental import pallas as pl
from jax.experimental.pallas import tpu as pltpu
from jax.sharding import PartitionSpec as P

LEVELS = 5
COARSE = 8
AXES = ("grp", "gy", "gx")
F32 = jnp.float32

HALO = 3
ZW = 4 + 2 * HALO
XW = 32 + 2 * HALO
LW = 384
EDGE = 4 * HALO
M_DEEP, M_FAR, R_DEEP, R_FAR = 11, 4, 10, 3

NEAR_TILES = (
    [[(1, d, 0)] for d in range(1, 7)]
    + [[(0, d, 0)] for d in range(1, 6)]
    + [[(1, 7, 0), (1, 11, 6)], [(1, 8, 0), (1, 10, 5)], [(0, 6, 0), (0, 10, 6)]]
    + [[(0, 7, 0), (0, 9, 5)], [(1, 9, 0), (0, 8, 4)]]
)
FAR_TILES = [[(1, 1, 0), (1, 2, 3), (0, 1, 6)], [(0, 2, 0), (1, 3, 2), (0, 3, 4), (1, 4, 5)]]
BESIDE_ROWS = 8 * (len(NEAR_TILES) + len(FAR_TILES) + 1)
M_EDGE, R_EDGE = 11, 10
Y_FAR = 3
Y_ROWS = 16 * (8 + Y_FAR)


def lane_iota(rows=8):
    return lax.broadcasted_iota(jnp.int32, (rows, 128), 1)


LANES = lax.GatherDimensionNumbers(
    offset_dims=(),
    collapsed_slice_dims=(1,),
    start_index_map=(1,),
    operand_batching_dims=(0,),
    start_indices_batching_dims=(0,),
)


def gather(source, index):
    return lax.gather(
        source, index[..., None], LANES, (1, 1), mode=lax.GatherScatterMode.PROMISE_IN_BOUNDS
    )


def every_lane(offset, px, rows):
    return (4 * lane_iota(rows) + ((px - 4 * offset) % 128)) & 127


def between(low, high, rows=8):
    lane = lane_iota(rows)
    return (lane >= low) & (lane < high)


def window_cells(t, rows):
    cell = lane_iota(rows) + 128 * t
    z = jnp.zeros((rows, 128), jnp.int32)
    for k in range(1, ZW + 1):
        z = z + (cell >= k * XW).astype(jnp.int32)
    return z, cell - z * XW


EDGE_STARTS = {(1, 0): 0, (1, 1): 33, (0, 0): 66, (0, 1): 96}


def edge_send_lanes():
    lane = lane_iota()
    mobile = lane < 66
    right = ((lane >= 33) & mobile) | (lane >= 96)
    start = jnp.where(mobile, jnp.where(right, 33, 0), jnp.where(right, 96, 66))
    width = jnp.where(mobile, M_EDGE, R_EDGE)
    t = lane - start
    z = (t >= width).astype(jnp.int32) + (t >= 2 * width).astype(jnp.int32)
    first = jnp.where(right, 0, EDGE - width)
    return jnp.minimum(jnp.where(mobile, 48, 0) + z * 12 + first + t - z * width, 95), right


def edge_own_lanes(side, t, rows):
    z, x = window_cells(t, rows)
    x = x if side == 0 else x - (XW - HALO)
    here = (z >= HALO) & (z < HALO + 4) & (x >= 0) & (x < HALO)
    return jnp.where(here, (z - HALO) * 12 + 4 * x, 0), here


def halo_start(side):
    return 0 if side == 0 else (HALO + 4) * XW - 256


def halo_cells(side, px, rows):
    p = (lane_iota(rows) - (halo_start(side) + 32 * px)) & 127
    z = (p >= XW).astype(jnp.int32) + (p >= 2 * XW).astype(jnp.int32)
    return z, p - z * XW, p < HALO * XW


def halo_turn(side, px, rows):
    z, x, _ = halo_cells(side, px, rows)
    return jnp.where((x >= HALO) & (x < XW - HALO), z, 3)


def halo_lanes(side, z, rows):
    q = (lane_iota(rows) - (halo_start(side) + z * XW + HALO)) & 127
    return 4 * (q & 31) + lax.shift_right_logical(q, 5)


def edge_far_lanes(side, a, rows):
    width = M_EDGE if a == 1 else R_EDGE
    index = jnp.zeros((rows, 128), jnp.int32)
    for px in range(4):
        z, x, here = halo_cells(side, px, rows)
        left = EDGE_STARTS[a, 0] + z * width + 4 * x + px - (EDGE - width)
        right = EDGE_STARTS[a, 1] + z * width + 4 * (x - (XW - HALO)) + px
        index = jnp.where(here & (x < HALO), left, index)
        index = jnp.where(here & (x >= XW - HALO), right, index)
    return jnp.clip(index, 0, 127)


class Plan:
    def __init__(self, mesh):
        self.counts = tuple(mesh.shape[axis] for axis in AXES)
        self.near = 1 if self.counts[1] == 2 else 2
        self.rows = 16 * (1 + self.near)
        self.cells = self.rows // 4
        self.tile = -(-self.cells // 8) * 8
        self.edge_start = BESIDE_ROWS * self.near
        self.payload = self.edge_start + 32 * (2 + self.near)
        self.devices = self.counts[0] * self.counts[1] * self.counts[2]
        self.coarse = (4 * self.counts[0], 4 * self.counts[1], 32 * self.counts[2])

    def pairs(self, swaps):
        out = []
        for index in np.ndindex(*self.counts):
            there = []
            for axis, swap in enumerate(swaps):
                i, n = index[axis], self.counts[axis]
                j = i if swap is None else (i + 1 if i % 2 == swap else i - 1)
                if axis == 2:
                    j = j % n
                there.append(j)
            if not all(0 <= j < n for j, n in zip(there, self.counts)):
                there = [index[0], index[1], index[2] ^ 1]
            out.append(
                (
                    int(np.ravel_multi_index(index, self.counts)),
                    int(np.ravel_multi_index(there, self.counts)),
                )
            )
        return out

    def y_places(self):
        iy = lax.axis_index("gy")
        if self.near == 1:
            return 16 * iy, [(1 - iy, 16 * (1 - iy))]
        odd = lax.rem(iy, 2)
        return 16, [(1 - odd, 32 * (1 - odd)), (odd, 32 * odd)]


def is_even(axis):
    return lax.rem(lax.axis_index(axis), 2) == 0


def at(start, size):
    if isinstance(start, int):
        return pl.ds(start, size)
    return pl.ds(pl.multiple_of(start, 8), size)


def x_edge(block, pz, half, to_right):
    out = jnp.zeros((8, 128), F32)
    for a in range(2):
        for z in range(4):
            cells = block[a, 4 * z + pz, 8 * half : 8 * half + 8, :]
            base = a * 48 + z * 12
            moved = jnp.where(
                to_right, pltpu.roll(cells, (base - (128 - EDGE)) % 128, 1), pltpu.roll(cells, base, 1)
            )
            out = jnp.where(between(base, base + EDGE), moved, out)
    return out


def first_kernel(plan, cells_ref, *outs):
    *outs, edge_ref = outs
    for pz in range(4):
        for half in range(2):
            rows = slice(8 * half, 8 * half + 8)
            edge_ref[pz, rows, :] = x_edge(
                cells_ref, pz, half, jnp.logical_not(is_even("gx"))
            )
    z_even = is_even("grp")
    for swap, out in enumerate(outs[:2]):
        top = z_even if swap == 0 else jnp.logical_not(z_even)
        row = 0
        for a, deep in ((1, M_DEEP), (0, R_DEEP)):
            for d in range(1, deep + 1):
                out[row : row + 16, :] = cells_ref[a, jnp.where(top, 16 - d, d - 1)]
                row += 16
    for out, (side, _) in zip(outs[2:], plan.y_places()[1]):
        last = side == 1
        for a in range(2):
            near, far = a * Y_ROWS, a * Y_ROWS + 128
            for plane in range(16):
                cells = cells_ref[a, plane]
                rows = jnp.where(last, cells[8:16], cells[0:8])
                out[near + 8 * plane : near + 8 * plane + 8, :] = rows
                rows = jnp.where(last, cells[8 - Y_FAR : 8], cells[8 : 8 + Y_FAR])
                out[far + Y_FAR * plane : far + Y_FAR * (plane + 1), :] = rows


def edges_kernel(plan, *refs):
    cells_ref = refs[0]
    near = plan.near
    arrived = refs[1 : 1 + near]
    x_arrived = refs[1 + near : 2 + 2 * near]
    beside = refs[2 + 2 * near : 2 + 3 * near]
    even_ref, odd_ref = refs[-2:]
    own_row, places = plan.y_places()
    even = is_even("gx")
    for ref, out, (side, _) in zip(arrived, beside, places):
        following = side == 1
        for a in range(2):
            near, far = a * Y_ROWS, a * Y_ROWS + 128
            for plane in range(16):
                rows = ref[near + 8 * plane : near + 8 * plane + 8, :]
                more = ref[far + Y_FAR * plane : far + Y_FAR * (plane + 1), :]
                none = jnp.zeros((8 - Y_FAR, 128), F32)
                after = jnp.concatenate([more, none], axis=0)
                before = jnp.concatenate([none, more], axis=0)
                out[a, plane, 0:8, :] = jnp.where(following, rows, before)
                out[a, plane, 8:16, :] = jnp.where(following, after, rows)
    for i, block in enumerate((cells_ref, *beside)):
        start = own_row if i == 0 else places[i - 1][1]
        odd_ref[:, at(start, 16), :] = x_arrived[i][...]
        for pz in range(4):
            for half in range(2):
                even_ref[pz, at(start + 8 * half, 8), :] = x_edge(block, pz, half, even)


def packed(pieces, following):
    row = lax.broadcasted_iota(jnp.int32, (8, 128), 0)
    row = jnp.where(following, row, 7 - row)
    out = None
    for value, first in pieces:
        if out is None:
            out = value
        else:
            moved = pltpu.roll(value, jnp.where(following, first, 8 - first), 0)
            out = jnp.where(row >= first, moved, out)
    return out


def unpacked(value, first, following):
    if first == 0:
        return value
    return pltpu.roll(value, jnp.where(following, 8 - first, first), 0)


def z_pack_kernel(plan, *refs):
    near = plan.near
    beside = refs[:near]
    x_odd_ref, x_even_ref = refs[near : near + 2]
    outs = refs[-2:]
    own_row, places = plan.y_places()
    x_even = is_even("gx")
    z_even = is_even("grp")
    lanes_0, use_right = edge_send_lanes()
    for swap, out in enumerate(outs):
        top = z_even if swap == 0 else jnp.logical_not(z_even)
        lanes = lanes_0 + jnp.where(top, 12, 0)

        def edge(pz, row):
            even, odd = x_even_ref[pz, at(row, 8), :], x_odd_ref[pz, at(row, 8), :]
            left = gather(jnp.where(x_even, odd, even), lanes)
            right = gather(jnp.where(x_even, even, odd), lanes)
            return jnp.where(use_right, right, left)

        for i, (side, base) in enumerate(places):
            following = side == 1
            to = i * BESIDE_ROWS
            for tiles, row in ((NEAR_TILES, 8 * (1 - side)), (FAR_TILES, 8 * side)):
                for pieces in tiles:
                    values = [
                        (beside[i][a, jnp.where(top, 16 - d, d - 1), at(row, 8), :], first)
                        for a, d, first in pieces
                    ]
                    out[to : to + 8, :] = packed(values, following)
                    to += 8
            values = [(edge(pz, base + 8 * side), 2 * pz) for pz in range(4)]
            out[to : to + 8, :] = packed(values, following)
        to = plan.edge_start
        rows = [own_row, own_row + 8] + [base + 8 * (1 - side) for side, base in places]
        for pz in range(4):
            for row in rows:
                out[to : to + 8, :] = edge(pz, row)
                to += 8


def padded_rows(plan, cells):
    if plan.cells == plan.tile:
        return cells
    return jnp.concatenate(
        [cells, jnp.zeros((plan.tile - plan.cells, cells.shape[1]), F32)], axis=0
    )


def every_fourth(plan, ref, lead, py):
    return padded_rows(plan, ref[(*lead, pl.ds(py, plan.cells, 4), slice(None))])


def own_kernel(plan, *refs):
    near = plan.near
    cells_ref, *beside = refs[: 1 + near]
    x_odd_ref, x_even_ref = refs[1 + near : 3 + near]
    out, planes, sides = refs[-3:]
    tile = plan.tile
    own_row, places = plan.y_places()
    x_even = is_even("gx")
    planes[:, :, at(own_row, 16), :] = cells_ref[...]
    for (_, base), block in zip(places, beside):
        planes[:, :, at(base, 16), :] = block[...]
    even, odd = x_even_ref[...], x_odd_ref[...]
    sides[0] = jnp.where(x_even, odd, even)
    sides[1] = jnp.where(x_even, even, odd)

    inside = inside_mask(plan)
    offsets = [(z + HALO) * XW + HALO for z in range(4)]
    index = [[every_lane(offset, px, tile) for px in range(4)] for offset in offsets]
    from_edge = {(s, t): edge_own_lanes(s, t, tile) for s, t in ((0, 0), (0, 1), (1, 1), (1, 2))}

    def body(pz, carry):
        for a in range(2):
            for py in range(4):
                cells = [every_fourth(plan, planes, (a, 4 * z + pz), py) for z in range(4)]
                side = [every_fourth(plan, sides, (s, pz), py) for s in range(2)]
                for px in range(4):
                    parts = [gather(cells[z], index[z][px]) for z in range(4)]
                    for t in range(3):
                        value = jnp.zeros((tile, 128), F32)
                        for z in range(4):
                            offset = offsets[z] - 128 * t
                            low, high = max(offset, 0), min(offset + 32, 128)
                            if low < high:
                                value = jnp.where(between(low, high, tile), parts[z], value)
                        for s in range(2):
                            if (s, t) in from_edge:
                                lanes, here = from_edge[s, t]
                                lanes = lanes + (48 * a + px)
                                value = jnp.where(here, gather(side[s], lanes), value)
                        lanes = slice(128 * t, 128 * t + 128)
                        out[a, pz, py, px, :, lanes] = jnp.where(inside[:, lanes], value, 0.0)
        return carry

    lax.fori_loop(0, 4, body, 0)


def inside_tile(plan, t):
    tile = plan.tile
    z, x = window_cells(t, tile)
    here = z < ZW
    z = z + (4 * lax.axis_index("grp") - HALO)
    x = x + (32 * lax.axis_index("gx") - HALO)
    here = here & (z >= 0) & (z < plan.coarse[0]) & (x >= 0) & (x < plan.coarse[2])
    if plan.near == 2:
        row = lax.broadcasted_iota(jnp.int32, (tile, 128), 0)
        y = row + (4 * lax.axis_index("gy") - 4)
        here = here & (row < plan.cells) & (y >= 0) & (y < plan.coarse[1])
    return here


def inside_mask(plan):
    masks = [jnp.where(inside_tile(plan, t), 1.0, 0.0) for t in range(3)]
    return jnp.concatenate(masks, axis=1) > 0.5


def roll_lanes(value, shift):
    return pltpu.roll(value, shift % LW, 1)


def fill_rim(plan, ref, n):
    tile = plan.tile
    row = lax.broadcasted_iota(jnp.int32, (tile, LW), 0)
    for i in range(1, n + 1):
        for j in range(1, n + 1):
            z_low, z_high = ref[n, i, j], ref[1, i, j]
            y_low, y_high = ref[i, n, j], ref[i, 1, j]
            x_low, x_high = ref[i, j, n], ref[i, j, 1]
            ref[0, i, j] = roll_lanes(z_low, XW)
            ref[n + 1, i, j] = roll_lanes(z_high, -XW)
            ref[i, 0, j] = jnp.where(row == 0, 0.0, pltpu.roll(y_low, 1, 0))
            ref[i, n + 1, j] = jnp.where(
                row == tile - 1, 0.0, pltpu.roll(y_high, tile - 1, 0)
            )
            ref[i, j, 0] = roll_lanes(x_low, 1)
            ref[i, j, n + 1] = roll_lanes(x_high, -1)


def around(ref, a, b, c):
    return (
        ref[a, b + 1, c + 1],
        ref[a + 2, b + 1, c + 1],
        ref[a + 1, b, c + 1],
        ref[a + 1, b + 2, c + 1],
        ref[a + 1, b + 1, c],
        ref[a + 1, b + 1, c + 2],
    )


def around_rimless(plan, ref, n, a, b, c):
    tile = plan.tile
    row = lax.broadcasted_iota(jnp.int32, (tile, LW), 0)
    return (
        ref[a - 1, b, c] if a > 0 else roll_lanes(ref[n - 1, b, c], XW),
        ref[a + 1, b, c] if a < n - 1 else roll_lanes(ref[0, b, c], -XW),
        ref[a, b - 1, c] if b > 0 else jnp.where(row == 0, 0.0, pltpu.roll(ref[a, n - 1, c], 1, 0)),
        ref[a, b + 1, c]
        if b < n - 1
        else jnp.where(row == tile - 1, 0.0, pltpu.roll(ref[a, 0, c], tile - 1, 0)),
        ref[a, b, c - 1] if c > 0 else roll_lanes(ref[a, b, n - 1], 1),
        ref[a, b, c + 1] if c < n - 1 else roll_lanes(ref[a, b, 0], -1),
    )


def pull(plan, n, m_ref, v_ref, h_ref, a, b, c):
    cells = around_rimless(plan, v_ref, n, a, b, c)
    mobility = around(m_ref, a, b, c)
    total = ((cells[0] + cells[1]) + (cells[2] + cells[3])) + (cells[4] + cells[5])
    products = [m * v for m, v in zip(mobility, cells)]
    other = ((products[0] + products[1]) + (products[2] + products[3])) + (
        products[4] + products[5]
    )
    return h_ref[a, b, c] * (m_ref[a + 1, b + 1, c + 1] * total + other)


def descend(plan, n, factor, inside, m_ref, r_ref, d_ref, h_ref, e_ref, k_ref):
    fill_rim(plan, m_ref, n)
    for a, b, c in np.ndindex(n, n, n):
        s = around(m_ref, a, b, c)
        d = 3.0 * m_ref[a + 1, b + 1, c + 1] + 0.5 * (
            ((s[0] + s[1]) + (s[2] + s[3])) + (s[4] + s[5])
        )
        h = jnp.where(inside, 0.4 / d, 0.0)
        d_ref[a, b, c] = d
        h_ref[a, b, c] = h
        e_ref[a, b, c] = (2.0 / factor) * h * r_ref[a, b, c]
    for a, b, c in np.ndindex(n, n, n):
        k_ref[a, b, c] = 1.2 * e_ref[a, b, c] + pull(plan, n, m_ref, e_ref, h_ref, a, b, c)


def leftover(plan, n, factor, m_ref, r_ref, d_ref, h_ref, k_ref, a, b, c):
    away = k_ref[a, b, c] - 1.25 * pull(plan, n, m_ref, k_ref, h_ref, a, b, c)
    return r_ref[a, b, c] - factor * (d_ref[a, b, c] * away)


def place_halo(plan, swap, own_ref, z_own_ref, z_ref, planes, sides, emit):
    near, tile = plan.near, plan.tile
    own_row, places = plan.y_places()
    upper = is_even("grp")
    if swap == 1:
        upper = jnp.logical_not(upper)

    def choose(make):
        return jnp.where(upper, make(1), make(0))

    def plane_of(d):
        return jnp.where(upper, d - 1, EDGE - d)

    for a, deep, far in ((1, M_DEEP, M_FAR), (0, R_DEEP, R_FAR)):
        for d in range(far + 1, EDGE + 1):
            planes[a, plane_of(d)] = jnp.zeros((plan.rows, 128), F32)
        for d in range(1, deep + 1):
            row = 16 * (d - 1) if a == 1 else 16 * (M_DEEP + d - 1)
            planes[a, plane_of(d), at(own_row, 16), :] = z_own_ref[row : row + 16, :]
    for i, (side, base) in enumerate(places):
        following = side == 1
        row = i * BESIDE_ROWS
        for tiles, to in ((NEAR_TILES, base + 8 * (1 - side)), (FAR_TILES, base + 8 * side)):
            for pieces in tiles:
                for a, d, first in pieces:
                    planes[a, plane_of(d), at(to, 8), :] = unpacked(
                        z_ref[row : row + 8, :], first, following
                    )
                row += 8
        for pz in range(4):
            sides[pz, at(base + 8 * side, 8), :] = unpacked(
                z_ref[row : row + 8, :], 2 * pz, following
            )
    row = plan.edge_start
    rows = [own_row, own_row + 8] + [base + 8 * (1 - side) for side, base in places]
    for pz in range(4):
        for to in rows:
            sides[pz, at(to, 8), :] = z_ref[row : row + 8, :]
            row += 8

    index = [choose(lambda side: halo_lanes(side, z, tile)) for z in range(HALO)]
    turns = [choose(lambda side: halo_turn(side, px, tile)) for px in range(4)]
    edge_index = [choose(lambda side: edge_far_lanes(side, a, tile)) for a in range(2)]

    def kept(side):
        z, _ = window_cells(2 * side, tile)
        z = (z < HALO) if side == 0 else (z >= HALO + 4)
        return (z & inside_tile(plan, 2 * side)).astype(jnp.int32)

    keep = choose(kept) > 0
    lanes = pl.ds(pl.multiple_of(jnp.where(upper, 256, 0), 128), 128)

    def place(pz, carry):
        for a in range(2):
            for py in range(4):
                parts = [
                    gather(every_fourth(plan, planes, (a, 4 * z + pz), py), index[z])
                    for z in range(HALO)
                ]
                edge = gather(every_fourth(plan, sides, (pz,), py), edge_index[a])
                for px in range(4):
                    turn = turns[px]
                    value = jnp.where(turn == 1, parts[1], parts[0])
                    value = jnp.where(turn == 2, parts[2], value)
                    value = jnp.where(turn == 3, edge, value)
                    if px > 0:
                        value = pltpu.roll(value, 128 - 32 * px, 1)
                    value = jnp.where(keep, value, own_ref[a, pz, py, px, :, lanes])
                    emit(a, pz, py, px, lanes, value)
        return carry

    lax.fori_loop(0, 4, place, 0)


def place_kernel(plan, own_ref, z_own_ref, z_ref, out, planes, sides):
    def emit(a, pz, py, px, lanes, value):
        out[a, pz, py, px] = value

    place_halo(plan, 1, own_ref, z_own_ref, z_ref, planes, sides, emit)


def down_kernel(plan, *refs):
    own_ref, other_ref, z_own_ref, z_ref = refs[:4]
    chunk, m0, h0, e0, k0, m1, h1, e1, k1 = refs[4:13]
    r0, d0, r1, d1, planes, sides = refs[13:]
    tile = plan.tile
    inside = inside_mask(plan)
    rest = pl.ds(pl.multiple_of(jnp.where(is_even("grp"), 0, 256), 128), 128)

    def emit(a, pz, py, px, lanes, value):
        for lanes_i, value_i in (
            (lanes, value),
            (rest, other_ref[a, pz, py, px]),
            (slice(128, 256), own_ref[a, pz, py, px, :, 128:256]),
        ):
            if a == 1:
                m0[pz + 1, py + 1, px + 1, :, lanes_i] = value_i
            else:
                r0[pz, py, px, :, lanes_i] = value_i

    place_halo(plan, 0, own_ref, z_own_ref, z_ref, planes, sides, emit)

    descend(plan, 4, 1.0, inside, m0, r0, d0, h0, e0, k0)
    for a, b, c in np.ndindex(2, 2, 2):
        rest = jnp.zeros((tile, LW), F32)
        mobility = jnp.zeros((tile, LW), F32)
        for da, db, dc in np.ndindex(2, 2, 2):
            i, j, k = 2 * a + da, 2 * b + db, 2 * c + dc
            rest = rest + leftover(plan, 4, 1.0, m0, r0, d0, h0, k0, i, j, k)
            mobility = mobility + m0[i + 1, j + 1, k + 1]
        r1[a, b, c] = 0.125 * rest
        m1[a + 1, b + 1, c + 1] = 0.125 * mobility
    descend(plan, 2, 0.25, inside, m1, r1, d1, h1, e1, k1)
    rest = jnp.zeros((tile, LW), F32)
    mobility = jnp.zeros((tile, LW), F32)
    for a, b, c in np.ndindex(2, 2, 2):
        rest = rest + leftover(plan, 2, 0.25, m1, r1, d1, h1, k1, a, b, c)
        mobility = mobility + m1[a + 1, b + 1, c + 1]
    both = []
    for total in (rest, mobility):
        packed = jnp.zeros((tile, 128), F32)
        for t in range(3):
            part = 0.125 * total[:, 128 * t : 128 * t + 128]
            for z in range(4):
                offset = (z + HALO) * XW + HALO - 128 * t
                low, high = max(offset, 0), min(offset + 32, 128)
                if low < high:
                    move = 32 * z - offset
                    packed = jnp.where(
                        between(low + move, high + move, tile),
                        pltpu.roll(part, move % 128, 1),
                        packed,
                    )
        both.append(own_rows(plan, packed))
    block = jnp.concatenate(both, axis=0)

    def put(i, carry):
        chunk[i] = block
        return carry

    lax.fori_loop(0, plan.devices, put, 0, unroll=8)


def own_rows(plan, cells):
    if plan.near == 1:
        return jnp.where(lax.axis_index("gy") == 0, cells[0:4], cells[4:8])
    return cells[4:8]


class Level:
    def __init__(self, plan, level):
        self.size = tuple(n >> (level - 2) for n in plan.coarse)
        self.tile = max(8, self.size[1])
        self.shape = (self.size[0], self.tile, 128)
        self.factor = 0.25**level

    def shifts(self, v):
        z, y, x = self.size
        if z > 1:
            none = jnp.zeros((1, self.tile, 128), F32)
            yield jnp.concatenate([none, v[:-1]], axis=0)
            yield jnp.concatenate([v[1:], none], axis=0)
        else:
            yield jnp.zeros_like(v)
            yield jnp.zeros_like(v)
        row = lax.broadcasted_iota(jnp.int32, self.shape, 1)
        lane = lax.broadcasted_iota(jnp.int32, self.shape, 2)
        up, down = pltpu.roll(v, 1, 1), pltpu.roll(v, self.tile - 1, 1)
        if y == self.tile:
            up = jnp.where(row == 0, 0.0, up)
            down = jnp.where(row == self.tile - 1, 0.0, down)
        yield up
        yield down
        left, right = pltpu.roll(v, 1, 2), pltpu.roll(v, 127, 2)
        if x == 128:
            left = jnp.where(lane == 0, 0.0, left)
            right = jnp.where(lane == 127, 0.0, right)
        yield left
        yield right

    def prepare(self, mobility, source):
        z, y, x = self.size
        row = lax.broadcasted_iota(jnp.int32, self.shape, 1)
        lane = lax.broadcasted_iota(jnp.int32, self.shape, 2)
        inside = (row < y) & (lane < x)
        sums = [mobility + near for near in self.shifts(mobility)]
        self.diagonal = 0.5 * (
            ((sums[0] + sums[1]) + (sums[2] + sums[3])) + (sums[4] + sums[5])
        )
        h = jnp.where(inside, 0.4 / self.diagonal, 0.0)
        self.weights = [h * s for s in sums]
        self.first = (2.0 / self.factor) * h * source
        self.source = source

    def pull(self, v):
        t = [w * near for w, near in zip(self.weights, self.shifts(v))]
        return ((t[0] + t[1]) + (t[2] + t[3])) + (t[4] + t[5])

    def relax(self, v):
        return 0.2 * v + self.first + self.pull(v)

    def leftover(self, v):
        return self.source - self.factor * (self.diagonal * (v - 1.25 * self.pull(v)))


def lanes_2d(values, index):
    flat = values.reshape(-1, 128)
    rows = flat.shape[0]
    lane = lax.broadcasted_iota(jnp.int32, (rows, 128), 1)
    return gather(flat, index(lane)).reshape(values.shape)


def coarsen(values, fine, coarse, fine_ref, coarse_ref):
    z, y, x = coarse.size
    tile = fine.tile
    pairs = values.reshape(z, 2, tile, 128)
    fine_ref[0:z] = pairs[:, 0] + pairs[:, 1]
    rows = fine_ref[0:z, pl.ds(0, y, 2), :] + fine_ref[0:z, pl.ds(1, y, 2), :]
    coarse_ref[0:z, 0:y, :] = rows
    full = coarse_ref[0:z]
    full = full + pltpu.roll(full, 127, 2)
    full = lanes_2d(full, lambda lane: (2 * lane) & 127)
    lane = lax.broadcasted_iota(jnp.int32, full.shape, 2)
    return jnp.where(lane < x, 0.125 * full, 0.0)


def refine(values, fine, coarse, fine_ref):
    z, y, x = coarse.size
    wide = lanes_2d(values, lambda lane: lax.shift_right_logical(lane, 1))
    fine_ref[0:z, pl.ds(0, y, 2), :] = wide[:, 0:y]
    fine_ref[0:z, pl.ds(1, y, 2), :] = wide[:, 0:y]
    rows = fine_ref[0:z]
    return jnp.broadcast_to(rows[:, None], (z, 2, fine.tile, 128)).reshape(fine.shape)


def ascend(plan, n, m_ref, h_ref, e_ref, k_ref, below, v_ref, w_ref):
    for a, b, c in np.ndindex(n, n, n):
        v_ref[a, b, c] = k_ref[a, b, c] + below(a, b, c)
    for old, new in ((v_ref, w_ref), (w_ref, v_ref)):
        for a, b, c in np.ndindex(n, n, n):
            new[a, b, c] = (
                0.2 * old[a, b, c]
                + e_ref[a, b, c]
                + pull(plan, n, m_ref, old, h_ref, a, b, c)
            )


def up_kernel(plan, *refs):
    joined, m0, h0, e0, k0, m1, h1, e1, k1, out = refs[:10]
    v0, w0, v1, w1, window, r2, m2, v2 = refs[10:18]
    fine_refs = refs[18:21]
    coarse_refs = refs[21:24]
    tile = plan.tile
    gz, gy, gx = plan.counts
    iz, iy, ix = (lax.axis_index(axis) for axis in AXES)
    inside = inside_mask(plan)

    def unpack(z_block, carry):
        for z in range(4):
            for y_block in range(gy):
                value = jnp.zeros((8, 128), F32)
                for x_block in range(gx):
                    part = joined[(z_block * gy + y_block) * gx + x_block]
                    value = jnp.where(
                        between(32 * x_block, 32 * x_block + 32),
                        pltpu.roll(part, (32 * (x_block - z)) % 128, 1),
                        value,
                    )
                rows = slice(4 * y_block, 4 * y_block + 4)
                r2[4 * z_block + z, rows, :] = value[0:4]
                m2[4 * z_block + z, rows, :] = value[4:8]
        return carry

    lax.fori_loop(0, gz, unpack, 0)
    for ref in (*fine_refs, *coarse_refs):
        ref[...] = jnp.zeros(ref.shape, F32)

    levels = [Level(plan, level) for level in range(2, LEVELS + 1)]
    mobility, source = m2[...], r2[...]
    kept = []
    for i, level in enumerate(levels):
        level.prepare(mobility, source)
        if i < len(levels) - 1:
            e = level.first + level.first * 0.2 + level.pull(level.first)
            kept.append(e)
            args = (level, levels[i + 1], fine_refs[i], coarse_refs[i])
            mobility = coarsen(mobility, *args)
            source = coarsen(level.leftover(e), *args)
    level = levels[-1]
    v = level.first
    for repeat in range(COARSE - 1):
        v = level.relax(v)
    for i in range(len(levels) - 2, -1, -1):
        v = kept[i] + refine(v, levels[i], levels[i + 1], fine_refs[i])
        v = levels[i].relax(levels[i].relax(v))

    v2[...] = jnp.zeros(v2.shape, F32)
    margin = 0 if plan.near == 1 else 8
    v2[pl.ds(HALO, plan.coarse[0]), pl.ds(margin, plan.coarse[1]), :] = v
    planes = []
    for z in range(ZW):
        if plan.near == 1:
            planes.append(v2[4 * iz + z])
        else:
            planes.append(v2[4 * iz + z, pl.ds(4 * iy + 4, tile), :])
    for t in range(3):
        value = jnp.zeros((tile, 128), F32)
        for z in range(ZW):
            offset = z * XW - 128 * t
            low, high = max(offset, 0), min(offset + XW, 128)
            if low < high:
                shift = lax.rem(offset % 128 + HALO - 32 * ix + 256, 128)
                value = jnp.where(
                    between(low, high, tile), pltpu.roll(planes[z], shift, 1), value
                )
        lanes = slice(128 * t, 128 * t + 128)
        window[:, lanes] = jnp.where(inside[:, lanes], value, 0.0)

    below = window[...]

    ascend(plan, 2, m1, h1, e1, k1, lambda a, b, c: below, v1, w1)
    ascend(plan, 4, m0, h0, e0, k0, lambda a, b, c: v1[a // 2, b // 2, c // 2], v0, w0)

    lane = lane_iota(tile)
    natural = 32 * (lane & 3) + lax.shift_right_logical(lane, 2)
    starts = [(z + HALO) * XW + HALO for z in range(4)]
    places_of = [(lane - start) & 127 for start in starts]
    index = [(natural + start) & 127 for start in starts]

    def store(pz, carry):
        for py in range(4):
            parts = [
                [v0[pz, py, px, :, 128 * t : 128 * t + 128] for t in range(3)]
                for px in range(4)
            ]
            parts = [
                [part if px == 0 else pltpu.roll(part, 32 * px, 1) for part in row]
                for px, row in enumerate(parts)
            ]
            for z, start in enumerate(starts):
                low, high = start // 128, (start + 31) // 128
                value = None
                for px in range(4):
                    part = parts[px][low]
                    if low != high:
                        first = (places_of[z] & 31) < 128 - start % 128
                        part = jnp.where(first, part, parts[px][high])
                    turn = lax.shift_right_logical(places_of[z], 5) == px
                    value = part if value is None else jnp.where(turn, part, value)
                value = gather(value, index[z])
                out[4 * z + pz, pl.ds(py, 4, 4), :] = own_rows(plan, value)
        return carry

    lax.fori_loop(0, 4, store, 0, unroll=4)


def call(plan, kernel, outs, scratch, *args):
    return pl.pallas_call(
        kernel,
        out_shape=[jax.ShapeDtypeStruct(shape, F32) for shape in outs],
        scratch_shapes=[pltpu.VMEM(shape, F32) for shape in scratch],
        compiler_params=pltpu.CompilerParams(
            vmem_limit_bytes=(3 * plan.tile + plan.coarse[0] // 4) * 1024 * 1024
        ),
    )(*args)


def solution(mesh):
    plan = Plan(mesh)
    near, tile = plan.near, plan.tile
    z2, y2, x2 = plan.coarse
    full = (4, 4, 4, tile, LW)
    half = (2, 2, 2, tile, LW)
    full_rim = (6, 6, 6, tile, LW)
    half_rim = (4, 4, 4, tile, LW)

    def swap(values, *swaps):
        return lax.ppermute(values, AXES, plan.pairs(swaps))

    def on_device(residual, mobility):
        assert residual.shape == (16, 16, 128)
        cells = jnp.stack([residual, mobility])
        even, odd, *rows, x_odd = call(
            plan,
            lambda *refs: first_kernel(plan, *refs),
            [(16 * (M_DEEP + R_DEEP), 128)] * 2 + [(2 * Y_ROWS, 128)] * near + [(4, 16, 128)],
            [],
            cells,
        )
        arrived = [swap(values, None, y, None) for y, values in enumerate(rows)]
        x_arrived = [swap(x_odd, None, y, 1) for y in (None, *range(near))]
        z_own = [swap(odd, 1, None, None), swap(even, 0, None, None)][::-1]
        *beside, even, odd = call(
            plan,
            lambda *refs: edges_kernel(plan, *refs),
            [(2, 16, 16, 128)] * near + [(4, plan.rows, 128)] * 2,
            [],
            cells,
            *arrived,
            *x_arrived,
        )
        edges = [swap(even, None, None, 0), odd]
        sends = call(
            plan,
            lambda *refs: z_pack_kernel(plan, *refs),
            [(plan.payload, 128)] * 2,
            [],
            *beside,
            *edges[::-1],
            *z_own,
        )
        arrived = [swap(sends[1], 1, None, None), swap(sends[0], 0, None, None)][::-1]
        (own,) = call(
            plan,
            lambda *refs: own_kernel(plan, *refs),
            [(2, *full)],
            [(2, 16, plan.rows, 128), (2, 4, plan.rows, 128)],
            cells,
            *beside,
            *edges[::-1],
        )
        halo_scratch = [(2, EDGE, plan.rows, 128), (4, plan.rows, 128)]
        (other,) = call(
            plan,
            lambda *refs: place_kernel(plan, *refs),
            [(2, 4, 4, 4, tile, 128)],
            halo_scratch,
            own,
            z_own[1],
            arrived[1],
        )
        chunk, *state = call(
            plan,
            lambda *refs: down_kernel(plan, *refs),
            [(plan.devices, 8, 128)] + [full_rim] + [full] * 3 + [half_rim] + [half] * 3,
            [full] * 2
            + [half] * 2
            + halo_scratch,
            own,
            other,
            z_own[0],
            arrived[0],
        )
        joined = lax.all_to_all(chunk, AXES, 0, 0, tiled=True)
        levels = [Level(plan, level) for level in range(2, LEVELS + 1)]
        margin = 0 if near == 1 else 16
        (out,) = call(
            plan,
            lambda *refs: up_kernel(plan, *refs),
            [(16, 16, 128)],
            [full] * 2
            + [half] * 2
            + [(tile, LW)]
            + [(z2, y2, 128)] * 2
            + [(z2 + 2 * HALO, y2 + margin, 128)]
            + [level.shape for level in levels[:-1]]
            + [level.shape for level in levels[1:]],
            joined,
            *state,
        )
        return out

    spec = P(*AXES)
    return jax.shard_map(
        on_device, mesh=mesh, in_specs=(spec, spec), out_specs=spec, check_vma=False
    )
```

```python
import jax
import jax.numpy as jnp
import numpy as np
from jax import lax
from jax.experimental import pallas as pl
from jax.experimental.pallas import tpu as pltpu
from jax.sharding import PartitionSpec as P

LEVELS = 5
COARSE = 8
AXES = ("grp", "gy", "gx")
F32 = jnp.float32

HALO = 3
ZW = 4 + 2 * HALO
XW = 32 + 2 * HALO
LW = 384
EDGE = 4 * HALO
M_DEEP, M_FAR, R_DEEP, R_FAR = 11, 4, 10, 3

NEAR_TILES = (
    [[(1, d, 0)] for d in range(1, 7)]
    + [[(0, d, 0)] for d in range(1, 6)]
    + [[(1, 7, 0), (1, 11, 6)], [(1, 8, 0), (1, 10, 5)], [(0, 6, 0), (0, 10, 6)]]
    + [[(0, 7, 0), (0, 9, 5)], [(1, 9, 0), (0, 8, 4)]]
)
FAR_TILES = [[(1, 1, 0), (1, 2, 3), (0, 1, 6)], [(0, 2, 0), (1, 3, 2), (0, 3, 4), (1, 4, 5)]]
BESIDE_ROWS = 8 * (len(NEAR_TILES) + len(FAR_TILES) + 1)
M_EDGE, R_EDGE = 11, 10
Y_FAR = (2, 3)
Y_STARTS = (0, 16 * (8 + Y_FAR[0]))
Y_ROWS = Y_STARTS[1] + 16 * (8 + Y_FAR[1])
DIAGONAL_ROWS = 48


def lane_iota(rows=8):
    return lax.broadcasted_iota(jnp.int32, (rows, 128), 1)


LANES = lax.GatherDimensionNumbers(
    offset_dims=(),
    collapsed_slice_dims=(1,),
    start_index_map=(1,),
    operand_batching_dims=(0,),
    start_indices_batching_dims=(0,),
)


def gather(source, index):
    return lax.gather(
        source, index[..., None], LANES, (1, 1), mode=lax.GatherScatterMode.PROMISE_IN_BOUNDS
    )


def every_lane(offset, px, rows):
    return (4 * lane_iota(rows) + ((px - 4 * offset) % 128)) & 127


def between(low, high, rows=8):
    lane = lane_iota(rows)
    return (lane >= low) & (lane < high)


def window_cells(t, rows):
    cell = lane_iota(rows) + 128 * t
    z = jnp.zeros((rows, 128), jnp.int32)
    for k in range(1, ZW + 1):
        z = z + (cell >= k * XW).astype(jnp.int32)
    return z, cell - z * XW


EDGE_STARTS = {(1, 0): 0, (1, 1): 33, (0, 0): 66, (0, 1): 96}


def edge_send_lanes():
    lane = lane_iota()
    mobile = lane < 66
    right = ((lane >= 33) & mobile) | (lane >= 96)
    start = jnp.where(mobile, jnp.where(right, 33, 0), jnp.where(right, 96, 66))
    width = jnp.where(mobile, M_EDGE, R_EDGE)
    t = lane - start
    z = (t >= width).astype(jnp.int32) + (t >= 2 * width).astype(jnp.int32)
    first = jnp.where(right, 0, EDGE - width)
    return jnp.minimum(jnp.where(mobile, 48, 0) + z * 12 + first + t - z * width, 95), right


def edge_own_lanes(side, t, rows):
    z, x = window_cells(t, rows)
    x = x if side == 0 else x - (XW - HALO)
    here = (z >= HALO) & (z < HALO + 4) & (x >= 0) & (x < HALO)
    return jnp.where(here, (z - HALO) * 12 + 4 * x, 0), here


def halo_start(side):
    return 0 if side == 0 else (HALO + 4) * XW - 256


def halo_cells(side, px, rows):
    p = (lane_iota(rows) - (halo_start(side) + 32 * px)) & 127
    z = (p >= XW).astype(jnp.int32) + (p >= 2 * XW).astype(jnp.int32)
    return z, p - z * XW, p < HALO * XW


def halo_turn(side, px, rows):
    z, x, _ = halo_cells(side, px, rows)
    return jnp.where((x >= HALO) & (x < XW - HALO), z, 3)


def halo_lanes(side, z, rows):
    q = (lane_iota(rows) - (halo_start(side) + z * XW + HALO)) & 127
    return 4 * (q & 31) + lax.shift_right_logical(q, 5)


def edge_far_lanes(side, a, rows):
    width = M_EDGE if a == 1 else R_EDGE
    index = jnp.zeros((rows, 128), jnp.int32)
    for px in range(4):
        z, x, here = halo_cells(side, px, rows)
        left = EDGE_STARTS[a, 0] + z * width + 4 * x + px - (EDGE - width)
        right = EDGE_STARTS[a, 1] + z * width + 4 * (x - (XW - HALO)) + px
        index = jnp.where(here & (x < HALO), left, index)
        index = jnp.where(here & (x >= XW - HALO), right, index)
    return jnp.clip(index, 0, 127)


class Plan:
    def __init__(self, mesh):
        self.counts = tuple(mesh.shape[axis] for axis in AXES)
        self.near = 1 if self.counts[1] == 2 else 2
        self.rows = 16 * (1 + self.near)
        self.cells = self.rows // 4
        self.tile = -(-self.cells // 8) * 8
        self.edge_start = BESIDE_ROWS * self.near
        self.payload = self.edge_start + 32 * (2 + self.near)
        self.devices = self.counts[0] * self.counts[1] * self.counts[2]
        self.coarse = (4 * self.counts[0], 4 * self.counts[1], 32 * self.counts[2])

    def pairs(self, swaps):
        out = []
        for index in np.ndindex(*self.counts):
            there = []
            for axis, swap in enumerate(swaps):
                i, n = index[axis], self.counts[axis]
                j = i if swap is None else (i + 1 if i % 2 == swap else i - 1)
                if axis == 2:
                    j = j % n
                there.append(j)
            if not all(0 <= j < n for j, n in zip(there, self.counts)):
                there = [index[0], index[1], index[2] ^ 1]
            out.append(
                (
                    int(np.ravel_multi_index(index, self.counts)),
                    int(np.ravel_multi_index(there, self.counts)),
                )
            )
        return out

    def y_places(self):
        iy = lax.axis_index("gy")
        if self.near == 1:
            return 16 * iy, [(1 - iy, 16 * (1 - iy))]
        odd = lax.rem(iy, 2)
        return 16, [(1 - odd, 32 * (1 - odd)), (odd, 32 * odd)]


def is_even(axis):
    return lax.rem(lax.axis_index(axis), 2) == 0


def at(start, size):
    if isinstance(start, int):
        return pl.ds(start, size)
    return pl.ds(pl.multiple_of(start, 8), size)


def x_edge(block, pz, half, to_right):
    out = jnp.zeros((8, 128), F32)
    for a in range(2):
        for z in range(4):
            cells = block[a, 4 * z + pz, 8 * half : 8 * half + 8, :]
            base = a * 48 + z * 12
            moved = jnp.where(
                to_right, pltpu.roll(cells, (base - (128 - EDGE)) % 128, 1), pltpu.roll(cells, base, 1)
            )
            out = jnp.where(between(base, base + EDGE), moved, out)
    return out


def first_kernel(plan, cells_ref, *outs):
    outs, edge_ref, diagonal = outs[: 2 + plan.near], outs[2 + plan.near], outs[3 + plan.near :]
    to_right = jnp.logical_not(is_even("gx"))
    edges = [[x_edge(cells_ref, pz, half, to_right) for half in range(2)] for pz in range(4)]
    for pz in range(4):
        edge_ref[pz, 0:8, :], edge_ref[pz, 8:16, :] = edges[pz]
    for out, (side, _) in zip(diagonal, plan.y_places()[1]):
        last = side == 1
        for pz in range(4):
            out[8 * pz : 8 * pz + 8, :] = jnp.where(last, edges[pz][1], edges[pz][0])
        for i in range(2):
            far = [jnp.where(last, edges[pz][0], edges[pz][1]) for pz in (2 * i, 2 * i + 1)]
            out[32 + 8 * i : 40 + 8 * i, :] = packed(
                [(far[0], 0), (far[1], 3)], jnp.logical_not(last)
            )
    z_even = is_even("grp")
    for swap, out in enumerate(outs[:2]):
        top = z_even if swap == 0 else jnp.logical_not(z_even)
        row = 0
        for a, deep in ((1, M_DEEP), (0, R_DEEP)):
            for d in range(1, deep + 1):
                out[row : row + 16, :] = cells_ref[a, jnp.where(top, 16 - d, d - 1)]
                row += 16
    for out, (side, _) in zip(outs[2:], plan.y_places()[1]):
        last = side == 1
        for a in range(2):
            near, far, deep = Y_STARTS[a], Y_STARTS[a] + 128, Y_FAR[a]
            for plane in range(16):
                cells = cells_ref[a, plane]
                rows = jnp.where(last, cells[8:16], cells[0:8])
                out[near + 8 * plane : near + 8 * plane + 8, :] = rows
                rows = jnp.where(last, cells[8 - deep : 8], cells[8 : 8 + deep])
                out[far + deep * plane : far + deep * (plane + 1), :] = rows


def edges_kernel(plan, *refs):
    cells_ref = refs[0]
    near = plan.near
    arrived = refs[1 : 1 + near]
    x_arrived = refs[1 + near : 2 + 2 * near]
    beside = refs[2 + 2 * near : 2 + 3 * near]
    even_ref, odd_ref = refs[-2:]
    own_row, places = plan.y_places()
    even = is_even("gx")
    for ref, out, (side, _) in zip(arrived, beside, places):
        following = side == 1
        for a in range(2):
            near_row, far, deep = Y_STARTS[a], Y_STARTS[a] + 128, Y_FAR[a]
            for plane in range(16):
                rows = ref[near_row + 8 * plane : near_row + 8 * plane + 8, :]
                more = ref[far + deep * plane : far + deep * (plane + 1), :]
                none = jnp.zeros((8 - deep, 128), F32)
                after = jnp.concatenate([more, none], axis=0)
                before = jnp.concatenate([none, more], axis=0)
                out[a, plane, 0:8, :] = jnp.where(following, rows, before)
                out[a, plane, 8:16, :] = jnp.where(following, after, rows)
    for i, block in enumerate((cells_ref, *beside)):
        start = own_row if i == 0 else places[i - 1][1]
        if i == 0:
            odd_ref[:, at(start, 16), :] = x_arrived[0][...]
        else:
            side = places[i - 1][0]
            ref = x_arrived[i]
            for pz in range(4):
                odd_ref[pz, at(start + 8 * (1 - side), 8), :] = ref[8 * pz : 8 * pz + 8, :]
                row = 32 + 8 * (pz // 2)
                odd_ref[pz, at(start + 8 * side, 8), :] = unpacked(
                    ref[row : row + 8, :], 3 * (pz % 2), side == 1
                )
        for pz in range(4):
            for half in range(2):
                even_ref[pz, at(start + 8 * half, 8), :] = x_edge(block, pz, half, even)


def packed(pieces, following):
    row = lax.broadcasted_iota(jnp.int32, (8, 128), 0)
    row = jnp.where(following, row, 7 - row)
    out = None
    for value, first in pieces:
        if out is None:
            out = value
        else:
            moved = pltpu.roll(value, jnp.where(following, first, 8 - first), 0)
            out = jnp.where(row >= first, moved, out)
    return out


def unpacked(value, first, following):
    if first == 0:
        return value
    return pltpu.roll(value, jnp.where(following, 8 - first, first), 0)


def z_pack_kernel(plan, *refs):
    near = plan.near
    beside = refs[:near]
    x_odd_ref, x_even_ref = refs[near : near + 2]
    outs = refs[-2:]
    own_row, places = plan.y_places()
    x_even = is_even("gx")
    z_even = is_even("grp")
    lanes_0, use_right = edge_send_lanes()
    for swap, out in enumerate(outs):
        top = z_even if swap == 0 else jnp.logical_not(z_even)
        lanes = lanes_0 + jnp.where(top, 12, 0)

        def edge(pz, row):
            even, odd = x_even_ref[pz, at(row, 8), :], x_odd_ref[pz, at(row, 8), :]
            left = gather(jnp.where(x_even, odd, even), lanes)
            right = gather(jnp.where(x_even, even, odd), lanes)
            return jnp.where(use_right, right, left)

        for i, (side, base) in enumerate(places):
            following = side == 1
            to = i * BESIDE_ROWS
            for tiles, row in ((NEAR_TILES, 8 * (1 - side)), (FAR_TILES, 8 * side)):
                for pieces in tiles:
                    values = [
                        (beside[i][a, jnp.where(top, 16 - d, d - 1), at(row, 8), :], first)
                        for a, d, first in pieces
                    ]
                    out[to : to + 8, :] = packed(values, following)
                    to += 8
            values = [(edge(pz, base + 8 * side), 2 * pz) for pz in range(4)]
            out[to : to + 8, :] = packed(values, following)
        to = plan.edge_start
        rows = [own_row, own_row + 8] + [base + 8 * (1 - side) for side, base in places]
        for pz in range(4):
            for row in rows:
                out[to : to + 8, :] = edge(pz, row)
                to += 8


def padded_rows(plan, cells):
    if plan.cells == plan.tile:
        return cells
    return jnp.concatenate(
        [cells, jnp.zeros((plan.tile - plan.cells, cells.shape[1]), F32)], axis=0
    )


def every_fourth(plan, ref, lead, py):
    return padded_rows(plan, ref[(*lead, pl.ds(py, plan.cells, 4), slice(None))])


def own_kernel(plan, *refs):
    near = plan.near
    cells_ref, *beside = refs[: 1 + near]
    x_odd_ref, x_even_ref = refs[1 + near : 3 + near]
    out, planes, sides = refs[-3:]
    tile = plan.tile
    own_row, places = plan.y_places()
    x_even = is_even("gx")
    planes[:, :, at(own_row, 16), :] = cells_ref[...]
    for (_, base), block in zip(places, beside):
        planes[:, :, at(base, 16), :] = block[...]
    even, odd = x_even_ref[...], x_odd_ref[...]
    sides[0] = jnp.where(x_even, odd, even)
    sides[1] = jnp.where(x_even, even, odd)

    inside = inside_mask(plan)
    offsets = [(z + HALO) * XW + HALO for z in range(4)]
    index = [[every_lane(offset, px, tile) for px in range(4)] for offset in offsets]
    from_edge = {(s, t): edge_own_lanes(s, t, tile) for s, t in ((0, 0), (0, 1), (1, 1), (1, 2))}

    def body(pz, carry):
        for a in range(2):
            for py in range(4):
                cells = [every_fourth(plan, planes, (a, 4 * z + pz), py) for z in range(4)]
                side = [every_fourth(plan, sides, (s, pz), py) for s in range(2)]
                for px in range(4):
                    parts = [gather(cells[z], index[z][px]) for z in range(4)]
                    for t in range(3):
                        value = jnp.zeros((tile, 128), F32)
                        for z in range(4):
                            offset = offsets[z] - 128 * t
                            low, high = max(offset, 0), min(offset + 32, 128)
                            if low < high:
                                value = jnp.where(between(low, high, tile), parts[z], value)
                        for s in range(2):
                            if (s, t) in from_edge:
                                lanes, here = from_edge[s, t]
                                lanes = lanes + (48 * a + px)
                                value = jnp.where(here, gather(side[s], lanes), value)
                        lanes = slice(128 * t, 128 * t + 128)
                        out[a, pz, py, px, :, lanes] = jnp.where(inside[:, lanes], value, 0.0)
        return carry

    lax.fori_loop(0, 4, body, 0)


def inside_tile(plan, t):
    tile = plan.tile
    z, x = window_cells(t, tile)
    here = z < ZW
    z = z + (4 * lax.axis_index("grp") - HALO)
    x = x + (32 * lax.axis_index("gx") - HALO)
    here = here & (z >= 0) & (z < plan.coarse[0]) & (x >= 0) & (x < plan.coarse[2])
    if plan.near == 2:
        row = lax.broadcasted_iota(jnp.int32, (tile, 128), 0)
        y = row + (4 * lax.axis_index("gy") - 4)
        here = here & (row < plan.cells) & (y >= 0) & (y < plan.coarse[1])
    return here


def inside_mask(plan):
    masks = [jnp.where(inside_tile(plan, t), 1.0, 0.0) for t in range(3)]
    return jnp.concatenate(masks, axis=1) > 0.5


def roll_lanes(value, shift):
    return pltpu.roll(value, shift % LW, 1)


def fill_rim(plan, ref, n):
    tile = plan.tile
    row = lax.broadcasted_iota(jnp.int32, (tile, LW), 0)
    for i in range(1, n + 1):
        for j in range(1, n + 1):
            z_low, z_high = ref[n, i, j], ref[1, i, j]
            y_low, y_high = ref[i, n, j], ref[i, 1, j]
            x_low, x_high = ref[i, j, n], ref[i, j, 1]
            ref[0, i, j] = roll_lanes(z_low, XW)
            ref[n + 1, i, j] = roll_lanes(z_high, -XW)
            ref[i, 0, j] = jnp.where(row == 0, 0.0, pltpu.roll(y_low, 1, 0))
            ref[i, n + 1, j] = jnp.where(
                row == tile - 1, 0.0, pltpu.roll(y_high, tile - 1, 0)
            )
            ref[i, j, 0] = roll_lanes(x_low, 1)
            ref[i, j, n + 1] = roll_lanes(x_high, -1)


def around(ref, a, b, c):
    return (
        ref[a, b + 1, c + 1],
        ref[a + 2, b + 1, c + 1],
        ref[a + 1, b, c + 1],
        ref[a + 1, b + 2, c + 1],
        ref[a + 1, b + 1, c],
        ref[a + 1, b + 1, c + 2],
    )


def around_rimless(plan, ref, n, a, b, c):
    tile = plan.tile
    row = lax.broadcasted_iota(jnp.int32, (tile, LW), 0)
    return (
        ref[a - 1, b, c] if a > 0 else roll_lanes(ref[n - 1, b, c], XW),
        ref[a + 1, b, c] if a < n - 1 else roll_lanes(ref[0, b, c], -XW),
        ref[a, b - 1, c] if b > 0 else jnp.where(row == 0, 0.0, pltpu.roll(ref[a, n - 1, c], 1, 0)),
        ref[a, b + 1, c]
        if b < n - 1
        else jnp.where(row == tile - 1, 0.0, pltpu.roll(ref[a, 0, c], tile - 1, 0)),
        ref[a, b, c - 1] if c > 0 else roll_lanes(ref[a, b, n - 1], 1),
        ref[a, b, c + 1] if c < n - 1 else roll_lanes(ref[a, b, 0], -1),
    )


def pull(plan, n, m_ref, v_ref, h_ref, a, b, c):
    cells = around_rimless(plan, v_ref, n, a, b, c)
    mobility = around(m_ref, a, b, c)
    total = ((cells[0] + cells[1]) + (cells[2] + cells[3])) + (cells[4] + cells[5])
    products = [m * v for m, v in zip(mobility, cells)]
    other = ((products[0] + products[1]) + (products[2] + products[3])) + (
        products[4] + products[5]
    )
    return h_ref[a, b, c] * (m_ref[a + 1, b + 1, c + 1] * total + other)


def descend(plan, n, factor, inside, m_ref, r_ref, d_ref, h_ref, e_ref, k_ref):
    fill_rim(plan, m_ref, n)
    for a, b, c in np.ndindex(n, n, n):
        s = around(m_ref, a, b, c)
        d = 3.0 * m_ref[a + 1, b + 1, c + 1] + 0.5 * (
            ((s[0] + s[1]) + (s[2] + s[3])) + (s[4] + s[5])
        )
        h = jnp.where(inside, 0.4 / d, 0.0)
        d_ref[a, b, c] = d
        h_ref[a, b, c] = h
        e_ref[a, b, c] = (2.0 / factor) * h * r_ref[a, b, c]
    for a, b, c in np.ndindex(n, n, n):
        k_ref[a, b, c] = 1.2 * e_ref[a, b, c] + pull(plan, n, m_ref, e_ref, h_ref, a, b, c)


def leftover(plan, n, factor, m_ref, r_ref, d_ref, h_ref, k_ref, a, b, c):
    away = k_ref[a, b, c] - 1.25 * pull(plan, n, m_ref, k_ref, h_ref, a, b, c)
    return r_ref[a, b, c] - factor * (d_ref[a, b, c] * away)


def place_halo(plan, swap, own_ref, z_own_ref, z_ref, planes, sides, emit):
    near, tile = plan.near, plan.tile
    own_row, places = plan.y_places()
    upper = is_even("grp")
    if swap == 1:
        upper = jnp.logical_not(upper)

    def choose(make):
        return jnp.where(upper, make(1), make(0))

    def plane_of(d):
        return jnp.where(upper, d - 1, EDGE - d)

    for a, deep, far in ((1, M_DEEP, M_FAR), (0, R_DEEP, R_FAR)):
        for d in range(far + 1, EDGE + 1):
            planes[a, plane_of(d)] = jnp.zeros((plan.rows, 128), F32)
        for d in range(1, deep + 1):
            row = 16 * (d - 1) if a == 1 else 16 * (M_DEEP + d - 1)
            planes[a, plane_of(d), at(own_row, 16), :] = z_own_ref[row : row + 16, :]
    for i, (side, base) in enumerate(places):
        following = side == 1
        row = i * BESIDE_ROWS
        for tiles, to in ((NEAR_TILES, base + 8 * (1 - side)), (FAR_TILES, base + 8 * side)):
            for pieces in tiles:
                for a, d, first in pieces:
                    planes[a, plane_of(d), at(to, 8), :] = unpacked(
                        z_ref[row : row + 8, :], first, following
                    )
                row += 8
        for pz in range(4):
            sides[pz, at(base + 8 * side, 8), :] = unpacked(
                z_ref[row : row + 8, :], 2 * pz, following
            )
    row = plan.edge_start
    rows = [own_row, own_row + 8] + [base + 8 * (1 - side) for side, base in places]
    for pz in range(4):
        for to in rows:
            sides[pz, at(to, 8), :] = z_ref[row : row + 8, :]
            row += 8

    index = [choose(lambda side: halo_lanes(side, z, tile)) for z in range(HALO)]
    turns = [choose(lambda side: halo_turn(side, px, tile)) for px in range(4)]
    edge_index = [choose(lambda side: edge_far_lanes(side, a, tile)) for a in range(2)]

    def kept(side):
        z, _ = window_cells(2 * side, tile)
        z = (z < HALO) if side == 0 else (z >= HALO + 4)
        return (z & inside_tile(plan, 2 * side)).astype(jnp.int32)

    keep = choose(kept) > 0
    lanes = pl.ds(pl.multiple_of(jnp.where(upper, 256, 0), 128), 128)

    def place(pz, carry):
        for a in range(2):
            for py in range(4):
                parts = [
                    gather(every_fourth(plan, planes, (a, 4 * z + pz), py), index[z])
                    for z in range(HALO)
                ]
                edge = gather(every_fourth(plan, sides, (pz,), py), edge_index[a])
                for px in range(4):
                    turn = turns[px]
                    value = jnp.where(turn == 1, parts[1], parts[0])
                    value = jnp.where(turn == 2, parts[2], value)
                    value = jnp.where(turn == 3, edge, value)
                    if px > 0:
                        value = pltpu.roll(value, 128 - 32 * px, 1)
                    value = jnp.where(keep, value, own_ref[a, pz, py, px, :, lanes])
                    emit(a, pz, py, px, lanes, value)
        return carry

    lax.fori_loop(0, 4, place, 0)


def place_kernel(plan, own_ref, z_own_ref, z_ref, out, planes, sides):
    def emit(a, pz, py, px, lanes, value):
        out[a, pz, py, px] = value

    place_halo(plan, 1, own_ref, z_own_ref, z_ref, planes, sides, emit)


def down_kernel(plan, *refs):
    own_ref, other_ref, z_own_ref, z_ref = refs[:4]
    chunk, m0, h0, e0, k0, m1, h1, e1, k1 = refs[4:13]
    r0, d0, r1, d1, planes, sides = refs[13:]
    tile = plan.tile
    inside = inside_mask(plan)
    rest = pl.ds(pl.multiple_of(jnp.where(is_even("grp"), 0, 256), 128), 128)

    def emit(a, pz, py, px, lanes, value):
        for lanes_i, value_i in (
            (lanes, value),
            (rest, other_ref[a, pz, py, px]),
            (slice(128, 256), own_ref[a, pz, py, px, :, 128:256]),
        ):
            if a == 1:
                m0[pz + 1, py + 1, px + 1, :, lanes_i] = value_i
            else:
                r0[pz, py, px, :, lanes_i] = value_i

    place_halo(plan, 0, own_ref, z_own_ref, z_ref, planes, sides, emit)

    descend(plan, 4, 1.0, inside, m0, r0, d0, h0, e0, k0)
    for a, b, c in np.ndindex(2, 2, 2):
        rest = jnp.zeros((tile, LW), F32)
        mobility = jnp.zeros((tile, LW), F32)
        for da, db, dc in np.ndindex(2, 2, 2):
            i, j, k = 2 * a + da, 2 * b + db, 2 * c + dc
            rest = rest + leftover(plan, 4, 1.0, m0, r0, d0, h0, k0, i, j, k)
            mobility = mobility + m0[i + 1, j + 1, k + 1]
        r1[a, b, c] = 0.125 * rest
        m1[a + 1, b + 1, c + 1] = 0.125 * mobility
    descend(plan, 2, 0.25, inside, m1, r1, d1, h1, e1, k1)
    rest = jnp.zeros((tile, LW), F32)
    mobility = jnp.zeros((tile, LW), F32)
    for a, b, c in np.ndindex(2, 2, 2):
        rest = rest + leftover(plan, 2, 0.25, m1, r1, d1, h1, k1, a, b, c)
        mobility = mobility + m1[a + 1, b + 1, c + 1]
    both = []
    for total in (rest, mobility):
        packed = jnp.zeros((tile, 128), F32)
        for t in range(3):
            part = 0.125 * total[:, 128 * t : 128 * t + 128]
            for z in range(4):
                offset = (z + HALO) * XW + HALO - 128 * t
                low, high = max(offset, 0), min(offset + 32, 128)
                if low < high:
                    move = 32 * z - offset
                    packed = jnp.where(
                        between(low + move, high + move, tile),
                        pltpu.roll(part, move % 128, 1),
                        packed,
                    )
        both.append(own_rows(plan, packed))
    block = jnp.concatenate(both, axis=0)

    def put(i, carry):
        chunk[i] = block
        return carry

    lax.fori_loop(0, plan.devices, put, 0, unroll=8)


def own_rows(plan, cells):
    if plan.near == 1:
        return jnp.where(lax.axis_index("gy") == 0, cells[0:4], cells[4:8])
    return cells[4:8]


class Level:
    def __init__(self, plan, level):
        self.size = tuple(n >> (level - 2) for n in plan.coarse)
        self.tile = max(8, self.size[1])
        self.shape = (self.size[0], self.tile, 128)
        self.factor = 0.25**level

    def shifts(self, v):
        z, y, x = self.size
        if z > 1:
            none = jnp.zeros((1, self.tile, 128), F32)
            yield jnp.concatenate([none, v[:-1]], axis=0)
            yield jnp.concatenate([v[1:], none], axis=0)
        else:
            yield jnp.zeros_like(v)
            yield jnp.zeros_like(v)
        row = lax.broadcasted_iota(jnp.int32, self.shape, 1)
        lane = lax.broadcasted_iota(jnp.int32, self.shape, 2)
        up, down = pltpu.roll(v, 1, 1), pltpu.roll(v, self.tile - 1, 1)
        if y == self.tile:
            up = jnp.where(row == 0, 0.0, up)
            down = jnp.where(row == self.tile - 1, 0.0, down)
        yield up
        yield down
        left, right = pltpu.roll(v, 1, 2), pltpu.roll(v, 127, 2)
        if x == 128:
            left = jnp.where(lane == 0, 0.0, left)
            right = jnp.where(lane == 127, 0.0, right)
        yield left
        yield right

    def prepare(self, mobility, source):
        z, y, x = self.size
        row = lax.broadcasted_iota(jnp.int32, self.shape, 1)
        lane = lax.broadcasted_iota(jnp.int32, self.shape, 2)
        inside = (row < y) & (lane < x)
        sums = [mobility + near for near in self.shifts(mobility)]
        self.diagonal = 0.5 * (
            ((sums[0] + sums[1]) + (sums[2] + sums[3])) + (sums[4] + sums[5])
        )
        h = jnp.where(inside, 0.4 / self.diagonal, 0.0)
        self.weights = [h * s for s in sums]
        self.first = (2.0 / self.factor) * h * source
        self.source = source

    def pull(self, v):
        t = [w * near for w, near in zip(self.weights, self.shifts(v))]
        return ((t[0] + t[1]) + (t[2] + t[3])) + (t[4] + t[5])

    def relax(self, v):
        return 0.2 * v + self.first + self.pull(v)

    def leftover(self, v):
        return self.source - self.factor * (self.diagonal * (v - 1.25 * self.pull(v)))


def lanes_2d(values, index):
    flat = values.reshape(-1, 128)
    rows = flat.shape[0]
    lane = lax.broadcasted_iota(jnp.int32, (rows, 128), 1)
    return gather(flat, index(lane)).reshape(values.shape)


def coarsen(values, coarse, fine_ref):
    z, y, x = coarse.size
    pairs = values.reshape(z, 2, values.shape[1], 128)
    fine_ref[0:z, 0 : values.shape[1], :] = pairs[:, 0] + pairs[:, 1]
    tile = coarse.tile
    full = fine_ref[0:z, pl.ds(0, tile, 2), :] + fine_ref[0:z, pl.ds(1, tile, 2), :]
    full = lanes_2d(full, lambda lane: (2 * lane) & 127) + lanes_2d(
        full, lambda lane: (2 * lane + 1) & 127
    )
    lane = lax.broadcasted_iota(jnp.int32, full.shape, 2)
    return jnp.where(lane < x, 0.125 * full, 0.0)


def refine(values, fine, coarse, fine_ref):
    z, y, x = coarse.size
    wide = lanes_2d(values, lambda lane: lax.shift_right_logical(lane, 1))
    fine_ref[0:z, pl.ds(0, y, 2), :] = wide[:, 0:y]
    fine_ref[0:z, pl.ds(1, y, 2), :] = wide[:, 0:y]
    rows = fine_ref[0:z, 0 : fine.tile, :]
    return jnp.broadcast_to(rows[:, None], (z, 2, fine.tile, 128)).reshape(fine.shape)


def ascend(plan, n, m_ref, h_ref, e_ref, k_ref, below, v_ref, w_ref):
    for a, b, c in np.ndindex(n, n, n):
        v_ref[a, b, c] = k_ref[a, b, c] + below(a, b, c)
    for old, new in ((v_ref, w_ref), (w_ref, v_ref)):
        for a, b, c in np.ndindex(n, n, n):
            new[a, b, c] = (
                0.2 * old[a, b, c]
                + e_ref[a, b, c]
                + pull(plan, n, m_ref, old, h_ref, a, b, c)
            )


def up_kernel(plan, *refs):
    joined, m0, h0, e0, k0, m1, h1, e1, k1, out = refs[:10]
    v0, w0, v1, w1, window, r2, m2, v2 = refs[10:18]
    fine_refs = refs[18:21]
    tile = plan.tile
    gz, gy, gx = plan.counts
    iz, iy, ix = (lax.axis_index(axis) for axis in AXES)
    inside = inside_mask(plan)

    def unpack(z_block, carry):
        for z in range(4):
            for y_block in range(gy):
                value = jnp.zeros((8, 128), F32)
                for x_block in range(gx):
                    part = joined[(z_block * gy + y_block) * gx + x_block]
                    value = jnp.where(
                        between(32 * x_block, 32 * x_block + 32),
                        pltpu.roll(part, (32 * (x_block - z)) % 128, 1),
                        value,
                    )
                rows = slice(4 * y_block, 4 * y_block + 4)
                r2[4 * z_block + z, rows, :] = value[0:4]
                m2[4 * z_block + z, rows, :] = value[4:8]
        return carry

    lax.fori_loop(0, gz, unpack, 0, unroll=4)
    for ref in fine_refs:
        ref[...] = jnp.zeros(ref.shape, F32)

    levels = [Level(plan, level) for level in range(2, LEVELS + 1)]
    mobility, source = m2[...], r2[...]
    kept = []
    for i, level in enumerate(levels):
        level.prepare(mobility, source)
        if i < len(levels) - 1:
            e = level.first + level.first * 0.2 + level.pull(level.first)
            kept.append(e)
            args = (levels[i + 1], fine_refs[i])
            mobility = coarsen(mobility, *args)
            source = coarsen(level.leftover(e), *args)
    level = levels[-1]
    v = level.first
    for repeat in range(COARSE - 1):
        v = level.relax(v)
    for i in range(len(levels) - 2, -1, -1):
        v = kept[i] + refine(v, levels[i], levels[i + 1], fine_refs[i])
        v = levels[i].relax(levels[i].relax(v))

    v2[...] = jnp.zeros(v2.shape, F32)
    margin = 0 if plan.near == 1 else 8
    v2[pl.ds(HALO, plan.coarse[0]), pl.ds(margin, plan.coarse[1]), :] = v
    planes = []
    for z in range(ZW):
        if plan.near == 1:
            planes.append(v2[4 * iz + z])
        else:
            planes.append(v2[4 * iz + z, pl.ds(4 * iy + 4, tile), :])
    for t in range(3):
        value = jnp.zeros((tile, 128), F32)
        for z in range(ZW):
            offset = z * XW - 128 * t
            low, high = max(offset, 0), min(offset + XW, 128)
            if low < high:
                shift = lax.rem(offset % 128 + HALO - 32 * ix + 256, 128)
                value = jnp.where(
                    between(low, high, tile), pltpu.roll(planes[z], shift, 1), value
                )
        lanes = slice(128 * t, 128 * t + 128)
        window[:, lanes] = jnp.where(inside[:, lanes], value, 0.0)

    below = window[...]

    ascend(plan, 2, m1, h1, e1, k1, lambda a, b, c: below, v1, w1)
    ascend(plan, 4, m0, h0, e0, k0, lambda a, b, c: v1[a // 2, b // 2, c // 2], v0, w0)

    lane = lane_iota(tile)
    natural = 32 * (lane & 3) + lax.shift_right_logical(lane, 2)
    starts = [(z + HALO) * XW + HALO for z in range(4)]
    places_of = [(lane - start) & 127 for start in starts]
    index = [(natural + start) & 127 for start in starts]

    def store(pz, carry):
        for py in range(4):
            parts = [
                [v0[pz, py, px, :, 128 * t : 128 * t + 128] for t in range(3)]
                for px in range(4)
            ]
            parts = [
                [part if px == 0 else pltpu.roll(part, 32 * px, 1) for part in row]
                for px, row in enumerate(parts)
            ]
            for z, start in enumerate(starts):
                low, high = start // 128, (start + 31) // 128
                value = None
                for px in range(4):
                    part = parts[px][low]
                    if low != high:
                        first = (places_of[z] & 31) < 128 - start % 128
                        part = jnp.where(first, part, parts[px][high])
                    turn = lax.shift_right_logical(places_of[z], 5) == px
                    value = part if value is None else jnp.where(turn, part, value)
                value = gather(value, index[z])
                out[4 * z + pz, pl.ds(py, 4, 4), :] = own_rows(plan, value)
        return carry

    lax.fori_loop(0, 4, store, 0, unroll=4)


def call(plan, kernel, outs, scratch, *args):
    return pl.pallas_call(
        kernel,
        out_shape=[jax.ShapeDtypeStruct(shape, F32) for shape in outs],
        scratch_shapes=[pltpu.VMEM(shape, F32) for shape in scratch],
        compiler_params=pltpu.CompilerParams(
            vmem_limit_bytes=(3 * plan.tile + plan.coarse[0] // 4) * 1024 * 1024
        ),
    )(*args)


def solution(mesh):
    plan = Plan(mesh)
    near, tile = plan.near, plan.tile
    z2, y2, x2 = plan.coarse
    full = (4, 4, 4, tile, LW)
    half = (2, 2, 2, tile, LW)
    full_rim = (6, 6, 6, tile, LW)
    half_rim = (4, 4, 4, tile, LW)

    def swap(values, *swaps):
        return lax.ppermute(values, AXES, plan.pairs(swaps))

    def on_device(residual, mobility):
        assert residual.shape == (16, 16, 128)
        cells = jnp.stack([residual, mobility])
        even, odd, *sent = call(
            plan,
            lambda *refs: first_kernel(plan, *refs),
            [(16 * (M_DEEP + R_DEEP), 128)] * 2 + [(Y_ROWS, 128)] * near
            + [(4, 16, 128)]
            + [(DIAGONAL_ROWS, 128)] * near,
            [],
            cells,
        )
        arrived = [swap(sent[y], None, y, None) for y in range(near)]
        x_arrived = [swap(sent[near], None, None, 1)]
        x_arrived += [swap(sent[1 + near + y], None, y, 1) for y in range(near)]
        z_own = [swap(odd, 1, None, None), swap(even, 0, None, None)][::-1]
        *beside, even, odd = call(
            plan,
            lambda *refs: edges_kernel(plan, *refs),
            [(2, 16, 16, 128)] * near + [(4, plan.rows, 128)] * 2,
            [],
            cells,
            *arrived,
            *x_arrived,
        )
        edges = [swap(even, None, None, 0), odd]
        sends = call(
            plan,
            lambda *refs: z_pack_kernel(plan, *refs),
            [(plan.payload, 128)] * 2,
            [],
            *beside,
            *edges[::-1],
            *z_own,
        )
        arrived = [swap(sends[1], 1, None, None), swap(sends[0], 0, None, None)][::-1]
        (own,) = call(
            plan,
            lambda *refs: own_kernel(plan, *refs),
            [(2, *full)],
            [(2, 16, plan.rows, 128), (2, 4, plan.rows, 128)],
            cells,
            *beside,
            *edges[::-1],
        )
        halo_scratch = [(2, EDGE, plan.rows, 128), (4, plan.rows, 128)]
        (other,) = call(
            plan,
            lambda *refs: place_kernel(plan, *refs),
            [(2, 4, 4, 4, tile, 128)],
            halo_scratch,
            own,
            z_own[1],
            arrived[1],
        )
        chunk, *state = call(
            plan,
            lambda *refs: down_kernel(plan, *refs),
            [(plan.devices, 8, 128)] + [full_rim] + [full] * 3 + [half_rim] + [half] * 3,
            [full] * 2
            + [half] * 2
            + halo_scratch,
            own,
            other,
            z_own[0],
            arrived[0],
        )
        joined = lax.all_to_all(chunk, AXES, 0, 0, tiled=True)
        levels = [Level(plan, level) for level in range(2, LEVELS + 1)]
        margin = 0 if near == 1 else 16
        (out,) = call(
            plan,
            lambda *refs: up_kernel(plan, *refs),
            [(16, 16, 128)],
            [full] * 2
            + [half] * 2
            + [(tile, LW)]
            + [(z2, y2, 128)] * 2
            + [(z2 + 2 * HALO, y2 + margin, 128)]
            + [
                (fine.size[0], max(fine.tile, 2 * coarse.tile), 128)
                for fine, coarse in zip(levels[:-1], levels[1:])
            ],
            joined,
            *state,
        )
        return out

    spec = P(*AXES)
    return jax.shard_map(
        on_device, mesh=mesh, in_specs=(spec, spec), out_specs=spec, check_vma=False
    )
```

```python
import jax
import jax.numpy as jnp
import numpy as np
from jax import lax
from jax.experimental import pallas as pl
from jax.experimental.pallas import tpu as pltpu
from jax.sharding import PartitionSpec as P

LEVELS = 5
COARSE = 8
AXES = ("grp", "gy", "gx")
F32 = jnp.float32

HALO = 3
ZW = 4 + 2 * HALO
XW = 32 + 2 * HALO
LW = 384
NARROW = 256
EDGE = 4 * HALO
M_DEEP, M_FAR, R_DEEP, R_FAR = 11, 4, 10, 3

NEAR_TILES = (
    [[(1, d, 0)] for d in range(1, 7)]
    + [[(0, d, 0)] for d in range(1, 6)]
    + [[(1, 7, 0), (1, 11, 6)], [(1, 8, 0), (1, 10, 5)], [(0, 6, 0), (0, 10, 6)]]
    + [[(0, 7, 0), (0, 9, 5)], [(1, 9, 0), (0, 8, 4)]]
)
FAR_TILES = [[(1, 1, 0), (1, 2, 3), (0, 1, 6)], [(0, 2, 0), (1, 3, 2), (0, 3, 4), (1, 4, 5)]]
BESIDE_ROWS = 8 * (len(NEAR_TILES) + len(FAR_TILES) + 1)
M_EDGE, R_EDGE = 11, 10
Y_FAR = (2, 3)
Y_STARTS = (0, 16 * (8 + Y_FAR[0]))
Y_ROWS = Y_STARTS[1] + 16 * (8 + Y_FAR[1])
DIAGONAL_ROWS = 48


def lane_of(z):
    return ((z - 2) * XW) % LW


def lane_iota(rows=8):
    return lax.broadcasted_iota(jnp.int32, (rows, 128), 1)


LANES = lax.GatherDimensionNumbers(
    offset_dims=(),
    collapsed_slice_dims=(1,),
    start_index_map=(1,),
    operand_batching_dims=(0,),
    start_indices_batching_dims=(0,),
)


def gather(source, index):
    return lax.gather(
        source, index[..., None], LANES, (1, 1), mode=lax.GatherScatterMode.PROMISE_IN_BOUNDS
    )


def every_lane(offset, px, rows):
    return (4 * lane_iota(rows) + ((px - 4 * offset) % 128)) & 127


def between(low, high, rows=8):
    lane = lane_iota(rows)
    return (lane >= low) & (lane < high)


def window_cells(t, rows):
    cell = lane_iota(rows) + 128 * t
    cell = jnp.where(cell >= lane_of(0), cell - lane_of(0), cell + 2 * XW)
    z = jnp.zeros((rows, 128), jnp.int32)
    for k in range(1, ZW + 1):
        z = z + (cell >= k * XW).astype(jnp.int32)
    return z, cell - z * XW


EDGE_STARTS = {(1, 0): 0, (1, 1): 33, (0, 0): 66, (0, 1): 96}


def edge_send_lanes():
    lane = lane_iota()
    mobile = lane < 66
    right = ((lane >= 33) & mobile) | (lane >= 96)
    start = jnp.where(mobile, jnp.where(right, 33, 0), jnp.where(right, 96, 66))
    width = jnp.where(mobile, M_EDGE, R_EDGE)
    t = lane - start
    z = (t >= width).astype(jnp.int32) + (t >= 2 * width).astype(jnp.int32)
    first = jnp.where(right, 0, EDGE - width)
    return jnp.minimum(jnp.where(mobile, 48, 0) + z * 12 + first + t - z * width, 95), right


def edge_own_lanes(side, t, rows):
    z, x = window_cells(t, rows)
    x = x if side == 0 else x - (XW - HALO)
    here = (z >= HALO) & (z < HALO + 4) & (x >= 0) & (x < HALO)
    return jnp.where(here, (z - HALO) * 12 + 4 * x, 0), here


def halo_start(side):
    return lane_of(0 if side == 0 else HALO + 4) % 128


def halo_cells(side, px, rows):
    p = (lane_iota(rows) - (halo_start(side) + 32 * px)) & 127
    z = (p >= XW).astype(jnp.int32) + (p >= 2 * XW).astype(jnp.int32)
    return z, p - z * XW, p < HALO * XW


def halo_turn(side, px, rows):
    z, x, _ = halo_cells(side, px, rows)
    return jnp.where((x >= HALO) & (x < XW - HALO), z, 3)


def halo_lanes(side, z, rows):
    q = (lane_iota(rows) - (halo_start(side) + z * XW + HALO)) & 127
    return 4 * (q & 31) + lax.shift_right_logical(q, 5)


def edge_far_lanes(side, a, rows):
    width = M_EDGE if a == 1 else R_EDGE
    index = jnp.zeros((rows, 128), jnp.int32)
    for px in range(4):
        z, x, here = halo_cells(side, px, rows)
        left = EDGE_STARTS[a, 0] + z * width + 4 * x + px - (EDGE - width)
        right = EDGE_STARTS[a, 1] + z * width + 4 * (x - (XW - HALO)) + px
        index = jnp.where(here & (x < HALO), left, index)
        index = jnp.where(here & (x >= XW - HALO), right, index)
    return jnp.clip(index, 0, 127)


class Plan:
    def __init__(self, mesh):
        self.counts = tuple(mesh.shape[axis] for axis in AXES)
        self.near = 1 if self.counts[1] == 2 else 2
        self.rows = 16 * (1 + self.near)
        self.cells = self.rows // 4
        self.tile = -(-self.cells // 8) * 8
        self.edge_start = BESIDE_ROWS * self.near
        self.payload = self.edge_start + 32 * (2 + self.near)
        self.devices = self.counts[0] * self.counts[1] * self.counts[2]
        self.coarse = (4 * self.counts[0], 4 * self.counts[1], 32 * self.counts[2])

    def pairs(self, swaps):
        out = []
        for index in np.ndindex(*self.counts):
            there = []
            for axis, swap in enumerate(swaps):
                i, n = index[axis], self.counts[axis]
                j = i if swap is None else (i + 1 if i % 2 == swap else i - 1)
                if axis == 2:
                    j = j % n
                there.append(j)
            if not all(0 <= j < n for j, n in zip(there, self.counts)):
                there = [index[0], index[1], index[2] ^ 1]
            out.append(
                (
                    int(np.ravel_multi_index(index, self.counts)),
                    int(np.ravel_multi_index(there, self.counts)),
                )
            )
        return out

    def y_places(self):
        iy = lax.axis_index("gy")
        if self.near == 1:
            return 16 * iy, [(1 - iy, 16 * (1 - iy))]
        odd = lax.rem(iy, 2)
        return 16, [(1 - odd, 32 * (1 - odd)), (odd, 32 * odd)]


def is_even(axis):
    return lax.rem(lax.axis_index(axis), 2) == 0


def at(start, size):
    if isinstance(start, int):
        return pl.ds(start, size)
    return pl.ds(pl.multiple_of(start, 8), size)


def x_edge(block, pz, half, to_right):
    out = jnp.zeros((8, 128), F32)
    for a in range(2):
        for z in range(4):
            cells = block[a, 4 * z + pz, 8 * half : 8 * half + 8, :]
            base = a * 48 + z * 12
            moved = jnp.where(
                to_right, pltpu.roll(cells, (base - (128 - EDGE)) % 128, 1), pltpu.roll(cells, base, 1)
            )
            out = jnp.where(between(base, base + EDGE), moved, out)
    return out


def first_kernel(plan, cells_ref, *outs):
    outs, edge_ref, diagonal = outs[: 2 + plan.near], outs[2 + plan.near], outs[3 + plan.near :]
    to_right = jnp.logical_not(is_even("gx"))
    edges = [[x_edge(cells_ref, pz, half, to_right) for half in range(2)] for pz in range(4)]
    for pz in range(4):
        edge_ref[pz, 0:8, :], edge_ref[pz, 8:16, :] = edges[pz]
    for out, (side, _) in zip(diagonal, plan.y_places()[1]):
        last = side == 1
        for pz in range(4):
            out[8 * pz : 8 * pz + 8, :] = jnp.where(last, edges[pz][1], edges[pz][0])
        for i in range(2):
            far = [jnp.where(last, edges[pz][0], edges[pz][1]) for pz in (2 * i, 2 * i + 1)]
            out[32 + 8 * i : 40 + 8 * i, :] = packed(
                [(far[0], 0), (far[1], 3)], jnp.logical_not(last)
            )
    z_even = is_even("grp")
    for swap, out in enumerate(outs[:2]):
        top = z_even if swap == 0 else jnp.logical_not(z_even)
        row = 0
        for a, deep in ((1, M_DEEP), (0, R_DEEP)):
            for d in range(1, deep + 1):
                out[row : row + 16, :] = cells_ref[a, jnp.where(top, 16 - d, d - 1)]
                row += 16
    for out, (side, _) in zip(outs[2:], plan.y_places()[1]):
        last = side == 1
        for a in range(2):
            near, far, deep = Y_STARTS[a], Y_STARTS[a] + 128, Y_FAR[a]
            for plane in range(16):
                cells = cells_ref[a, plane]
                rows = jnp.where(last, cells[8:16], cells[0:8])
                out[near + 8 * plane : near + 8 * plane + 8, :] = rows
                rows = jnp.where(last, cells[8 - deep : 8], cells[8 : 8 + deep])
                out[far + deep * plane : far + deep * (plane + 1), :] = rows


def edges_kernel(plan, *refs):
    cells_ref = refs[0]
    near = plan.near
    arrived = refs[1 : 1 + near]
    x_arrived = refs[1 + near : 2 + 2 * near]
    beside = refs[2 + 2 * near : 2 + 3 * near]
    even_ref, odd_ref = refs[-2:]
    own_row, places = plan.y_places()
    even = is_even("gx")
    for ref, out, (side, _) in zip(arrived, beside, places):
        following = side == 1
        for a in range(2):
            near_row, far, deep = Y_STARTS[a], Y_STARTS[a] + 128, Y_FAR[a]
            for plane in range(16):
                rows = ref[near_row + 8 * plane : near_row + 8 * plane + 8, :]
                more = ref[far + deep * plane : far + deep * (plane + 1), :]
                none = jnp.zeros((8 - deep, 128), F32)
                after = jnp.concatenate([more, none], axis=0)
                before = jnp.concatenate([none, more], axis=0)
                out[a, plane, 0:8, :] = jnp.where(following, rows, before)
                out[a, plane, 8:16, :] = jnp.where(following, after, rows)
    for i, block in enumerate((cells_ref, *beside)):
        start = own_row if i == 0 else places[i - 1][1]
        if i == 0:
            odd_ref[:, at(start, 16), :] = x_arrived[0][...]
        else:
            side = places[i - 1][0]
            ref = x_arrived[i]
            for pz in range(4):
                odd_ref[pz, at(start + 8 * (1 - side), 8), :] = ref[8 * pz : 8 * pz + 8, :]
                row = 32 + 8 * (pz // 2)
                odd_ref[pz, at(start + 8 * side, 8), :] = unpacked(
                    ref[row : row + 8, :], 3 * (pz % 2), side == 1
                )
        for pz in range(4):
            for half in range(2):
                even_ref[pz, at(start + 8 * half, 8), :] = x_edge(block, pz, half, even)


def packed(pieces, following):
    row = lax.broadcasted_iota(jnp.int32, (8, 128), 0)
    row = jnp.where(following, row, 7 - row)
    out = None
    for value, first in pieces:
        if out is None:
            out = value
        else:
            moved = pltpu.roll(value, jnp.where(following, first, 8 - first), 0)
            out = jnp.where(row >= first, moved, out)
    return out


def unpacked(value, first, following):
    if first == 0:
        return value
    return pltpu.roll(value, jnp.where(following, 8 - first, first), 0)


def z_pack_kernel(plan, *refs):
    near = plan.near
    beside = refs[:near]
    x_odd_ref, x_even_ref = refs[near : near + 2]
    outs = refs[-2:]
    own_row, places = plan.y_places()
    x_even = is_even("gx")
    z_even = is_even("grp")
    lanes_0, use_right = edge_send_lanes()
    for swap, out in enumerate(outs):
        top = z_even if swap == 0 else jnp.logical_not(z_even)
        lanes = lanes_0 + jnp.where(top, 12, 0)

        def edge(pz, row):
            even, odd = x_even_ref[pz, at(row, 8), :], x_odd_ref[pz, at(row, 8), :]
            left = gather(jnp.where(x_even, odd, even), lanes)
            right = gather(jnp.where(x_even, even, odd), lanes)
            return jnp.where(use_right, right, left)

        for i, (side, base) in enumerate(places):
            following = side == 1
            to = i * BESIDE_ROWS
            for tiles, row in ((NEAR_TILES, 8 * (1 - side)), (FAR_TILES, 8 * side)):
                for pieces in tiles:
                    values = [
                        (beside[i][a, jnp.where(top, 16 - d, d - 1), at(row, 8), :], first)
                        for a, d, first in pieces
                    ]
                    out[to : to + 8, :] = packed(values, following)
                    to += 8
            values = [(edge(pz, base + 8 * side), 2 * pz) for pz in range(4)]
            out[to : to + 8, :] = packed(values, following)
        to = plan.edge_start
        rows = [own_row, own_row + 8] + [base + 8 * (1 - side) for side, base in places]
        for pz in range(4):
            for row in rows:
                out[to : to + 8, :] = edge(pz, row)
                to += 8


def padded_rows(plan, cells):
    if plan.cells == plan.tile:
        return cells
    return jnp.concatenate(
        [cells, jnp.zeros((plan.tile - plan.cells, cells.shape[1]), F32)], axis=0
    )


def every_fourth(plan, ref, lead, py):
    return padded_rows(plan, ref[(*lead, pl.ds(py, plan.cells, 4), slice(None))])


def own_kernel(plan, *refs):
    near = plan.near
    cells_ref, *beside = refs[: 1 + near]
    x_odd_ref, x_even_ref = refs[1 + near : 3 + near]
    out, planes, sides = refs[-3:]
    tile = plan.tile
    own_row, places = plan.y_places()
    x_even = is_even("gx")
    planes[:, :, at(own_row, 16), :] = cells_ref[...]
    for (_, base), block in zip(places, beside):
        planes[:, :, at(base, 16), :] = block[...]
    even, odd = x_even_ref[...], x_odd_ref[...]
    sides[0] = jnp.where(x_even, odd, even)
    sides[1] = jnp.where(x_even, even, odd)

    inside = inside_mask(plan)
    offsets = [lane_of(z + HALO) + HALO for z in range(4)]
    index = [[every_lane(offset, px, tile) for px in range(4)] for offset in offsets]
    from_edge = {(s, t): edge_own_lanes(s, t, tile) for s in range(2) for t in range(2)}

    def body(pz, carry):
        for a in range(2):
            for py in range(4):
                cells = [every_fourth(plan, planes, (a, 4 * z + pz), py) for z in range(4)]
                side = [every_fourth(plan, sides, (s, pz), py) for s in range(2)]
                for px in range(4):
                    parts = [gather(cells[z], index[z][px]) for z in range(4)]
                    for t in range(2):
                        value = jnp.zeros((tile, 128), F32)
                        for z in range(4):
                            offset = offsets[z] - 128 * t
                            low, high = max(offset, 0), min(offset + 32, 128)
                            if low < high:
                                value = jnp.where(between(low, high, tile), parts[z], value)
                        for s in range(2):
                            if (s, t) in from_edge:
                                lanes, here = from_edge[s, t]
                                lanes = lanes + (48 * a + px)
                                value = jnp.where(here, gather(side[s], lanes), value)
                        lanes = slice(128 * t, 128 * t + 128)
                        out[a, pz, py, px, :, lanes] = jnp.where(inside[:, lanes], value, 0.0)
        return carry

    lax.fori_loop(0, 4, body, 0)


def inside_tile(plan, t):
    tile = plan.tile
    z, x = window_cells(t, tile)
    here = z < ZW
    z = z + (4 * lax.axis_index("grp") - HALO)
    x = x + (32 * lax.axis_index("gx") - HALO)
    here = here & (z >= 0) & (z < plan.coarse[0]) & (x >= 0) & (x < plan.coarse[2])
    if plan.near == 2:
        row = lax.broadcasted_iota(jnp.int32, (tile, 128), 0)
        y = row + (4 * lax.axis_index("gy") - 4)
        here = here & (row < plan.cells) & (y >= 0) & (y < plan.coarse[1])
    return here


def inside_mask(plan):
    masks = [jnp.where(inside_tile(plan, t), 1.0, 0.0) for t in range(3)]
    return jnp.concatenate(masks, axis=1) > 0.5


def roll_lanes(value, shift):
    return pltpu.roll(value, shift % value.shape[1], 1)


def fill_rim(plan, ref, n):
    tile = plan.tile
    row = lax.broadcasted_iota(jnp.int32, (tile, LW), 0)
    for i in range(1, n + 1):
        for j in range(1, n + 1):
            z_low, z_high = ref[n, i, j], ref[1, i, j]
            y_low, y_high = ref[i, n, j], ref[i, 1, j]
            x_low, x_high = ref[i, j, n], ref[i, j, 1]
            ref[0, i, j] = roll_lanes(z_low, XW)
            ref[n + 1, i, j] = roll_lanes(z_high, -XW)
            ref[i, 0, j] = jnp.where(row == 0, 0.0, pltpu.roll(y_low, 1, 0))
            ref[i, n + 1, j] = jnp.where(
                row == tile - 1, 0.0, pltpu.roll(y_high, tile - 1, 0)
            )
            ref[i, j, 0] = roll_lanes(x_low, 1)
            ref[i, j, n + 1] = roll_lanes(x_high, -1)


def around(ref, a, b, c, width=LW):
    lanes = slice(0, width)
    return (
        ref[a, b + 1, c + 1, :, lanes],
        ref[a + 2, b + 1, c + 1, :, lanes],
        ref[a + 1, b, c + 1, :, lanes],
        ref[a + 1, b + 2, c + 1, :, lanes],
        ref[a + 1, b + 1, c, :, lanes],
        ref[a + 1, b + 1, c + 2, :, lanes],
    )


def around_rimless(plan, ref, n, a, b, c, width):
    tile = plan.tile
    row = lax.broadcasted_iota(jnp.int32, (tile, width), 0)

    def cells(i, j, k):
        return ref[i, j, k, :, 0:width]

    def first_row(value):
        return jnp.where(row == 0, 0.0, pltpu.roll(value, 1, 0))

    def last_row(value):
        return jnp.where(row == tile - 1, 0.0, pltpu.roll(value, tile - 1, 0))

    return (
        cells(a - 1, b, c) if a > 0 else roll_lanes(cells(n - 1, b, c), XW),
        cells(a + 1, b, c) if a < n - 1 else roll_lanes(cells(0, b, c), -XW),
        cells(a, b - 1, c) if b > 0 else first_row(cells(a, n - 1, c)),
        cells(a, b + 1, c) if b < n - 1 else last_row(cells(a, 0, c)),
        cells(a, b, c - 1) if c > 0 else roll_lanes(cells(a, b, n - 1), 1),
        cells(a, b, c + 1) if c < n - 1 else roll_lanes(cells(a, b, 0), -1),
    )


def pull(plan, n, m_ref, v_ref, h_ref, a, b, c, width=LW):
    cells = around_rimless(plan, v_ref, n, a, b, c, width)
    mobility = around(m_ref, a, b, c, width)
    total = ((cells[0] + cells[1]) + (cells[2] + cells[3])) + (cells[4] + cells[5])
    products = [m * v for m, v in zip(mobility, cells)]
    other = ((products[0] + products[1]) + (products[2] + products[3])) + (
        products[4] + products[5]
    )
    centre = m_ref[a + 1, b + 1, c + 1, :, 0:width]
    return h_ref[a, b, c, :, 0:width] * (centre * total + other)


def descend(plan, n, factor, inside, m_ref, r_ref, d_ref, h_ref, e_ref, k_ref):
    fill_rim(plan, m_ref, n)
    for a, b, c in np.ndindex(n, n, n):
        s = around(m_ref, a, b, c)
        d = 3.0 * m_ref[a + 1, b + 1, c + 1] + 0.5 * (
            ((s[0] + s[1]) + (s[2] + s[3])) + (s[4] + s[5])
        )
        h = jnp.where(inside, 0.4 / d, 0.0)
        d_ref[a, b, c] = d
        h_ref[a, b, c] = h
        e_ref[a, b, c] = (2.0 / factor) * h * r_ref[a, b, c]
    for a, b, c in np.ndindex(n, n, n):
        k_ref[a, b, c] = 1.2 * e_ref[a, b, c] + pull(plan, n, m_ref, e_ref, h_ref, a, b, c)


def leftover(plan, n, factor, m_ref, r_ref, d_ref, h_ref, k_ref, a, b, c):
    away = k_ref[a, b, c] - 1.25 * pull(plan, n, m_ref, k_ref, h_ref, a, b, c)
    return r_ref[a, b, c] - factor * (d_ref[a, b, c] * away)


def place_halo(plan, swap, z_own_ref, z_ref, planes, sides, emit):
    near, tile = plan.near, plan.tile
    own_row, places = plan.y_places()
    upper = is_even("grp")
    if swap == 1:
        upper = jnp.logical_not(upper)

    def choose(make):
        return jnp.where(upper, make(1), make(0))

    def plane_of(d):
        return jnp.where(upper, d - 1, EDGE - d)

    for a, deep, far in ((1, M_DEEP, M_FAR), (0, R_DEEP, R_FAR)):
        for d in range(far + 1, EDGE + 1):
            planes[a, plane_of(d)] = jnp.zeros((plan.rows, 128), F32)
        for d in range(1, deep + 1):
            row = 16 * (d - 1) if a == 1 else 16 * (M_DEEP + d - 1)
            planes[a, plane_of(d), at(own_row, 16), :] = z_own_ref[row : row + 16, :]
    for i, (side, base) in enumerate(places):
        following = side == 1
        row = i * BESIDE_ROWS
        for tiles, to in ((NEAR_TILES, base + 8 * (1 - side)), (FAR_TILES, base + 8 * side)):
            for pieces in tiles:
                for a, d, first in pieces:
                    planes[a, plane_of(d), at(to, 8), :] = unpacked(
                        z_ref[row : row + 8, :], first, following
                    )
                row += 8
        for pz in range(4):
            sides[pz, at(base + 8 * side, 8), :] = unpacked(
                z_ref[row : row + 8, :], 2 * pz, following
            )
    row = plan.edge_start
    rows = [own_row, own_row + 8] + [base + 8 * (1 - side) for side, base in places]
    for pz in range(4):
        for to in rows:
            sides[pz, at(to, 8), :] = z_ref[row : row + 8, :]
            row += 8

    index = [choose(lambda side: halo_lanes(side, z, tile)) for z in range(HALO)]
    turns = [choose(lambda side: halo_turn(side, px, tile)) for px in range(4)]
    edge_index = [choose(lambda side: edge_far_lanes(side, a, tile)) for a in range(2)]

    def place(pz, carry):
        for a in range(2):
            for py in range(4):
                parts = [
                    gather(every_fourth(plan, planes, (a, 4 * z + pz), py), index[z])
                    for z in range(HALO)
                ]
                edge = gather(every_fourth(plan, sides, (pz,), py), edge_index[a])
                for px in range(4):
                    turn = turns[px]
                    value = jnp.where(turn == 1, parts[1], parts[0])
                    value = jnp.where(turn == 2, parts[2], value)
                    value = jnp.where(turn == 3, edge, value)
                    if px > 0:
                        value = pltpu.roll(value, 128 - 32 * px, 1)
                    emit(a, pz, py, px, value)
        return carry

    lax.fori_loop(0, 4, place, 0)


def place_kernel(plan, z_own_ref, z_ref, out, planes, sides):
    def emit(a, pz, py, px, value):
        out[a, pz, py, px] = value

    place_halo(plan, 1, z_own_ref, z_ref, planes, sides, emit)


def down_kernel(plan, *refs):
    own_ref, other_ref, z_own_ref, z_ref = refs[:4]
    chunk, m0, h0, e0, k0, m1, h1, e1, k1 = refs[4:13]
    r0, d0, r1, d1, planes, sides = refs[13:]
    tile = plan.tile
    inside = inside_mask(plan)
    z_even = is_even("grp")
    z = [window_cells(t, tile)[0] for t in range(3)]
    here = [inside_tile(plan, t) for t in range(3)]
    lower_0, upper_1 = (z[0] < HALO) & here[0], (z[1] >= HALO + 4) & here[1]
    lower_2, upper_2 = (z[2] < HALO) & here[2], (z[2] >= HALO + 4) & here[2]

    def emit(a, pz, py, px, value):
        other = other_ref[a, pz, py, px]
        lower = jnp.where(z_even, other, value)
        upper = jnp.where(z_even, value, other)
        tiles = (
            jnp.where(lower_0, lower, own_ref[a, pz, py, px, :, 0:128]),
            jnp.where(upper_1, upper, own_ref[a, pz, py, px, :, 128:256]),
            jnp.where(lower_2, lower, jnp.where(upper_2, upper, 0.0)),
        )
        for t, cells in enumerate(tiles):
            lanes = slice(128 * t, 128 * t + 128)
            if a == 1:
                m0[pz + 1, py + 1, px + 1, :, lanes] = cells
            else:
                r0[pz, py, px, :, lanes] = cells

    place_halo(plan, 0, z_own_ref, z_ref, planes, sides, emit)

    descend(plan, 4, 1.0, inside, m0, r0, d0, h0, e0, k0)
    for a, b, c in np.ndindex(2, 2, 2):
        rest = jnp.zeros((tile, LW), F32)
        mobility = jnp.zeros((tile, LW), F32)
        for da, db, dc in np.ndindex(2, 2, 2):
            i, j, k = 2 * a + da, 2 * b + db, 2 * c + dc
            rest = rest + leftover(plan, 4, 1.0, m0, r0, d0, h0, k0, i, j, k)
            mobility = mobility + m0[i + 1, j + 1, k + 1]
        r1[a, b, c] = 0.125 * rest
        m1[a + 1, b + 1, c + 1] = 0.125 * mobility
    descend(plan, 2, 0.25, inside, m1, r1, d1, h1, e1, k1)
    rest = jnp.zeros((tile, LW), F32)
    mobility = jnp.zeros((tile, LW), F32)
    for a, b, c in np.ndindex(2, 2, 2):
        rest = rest + leftover(plan, 2, 0.25, m1, r1, d1, h1, k1, a, b, c)
        mobility = mobility + m1[a + 1, b + 1, c + 1]
    both = []
    for total in (rest, mobility):
        packed = jnp.zeros((tile, 128), F32)
        for t in range(3):
            part = 0.125 * total[:, 128 * t : 128 * t + 128]
            for z in range(4):
                offset = lane_of(z + HALO) + HALO - 128 * t
                low, high = max(offset, 0), min(offset + 32, 128)
                if low < high:
                    move = 32 * z - offset
                    packed = jnp.where(
                        between(low + move, high + move, tile),
                        pltpu.roll(part, move % 128, 1),
                        packed,
                    )
        both.append(own_rows(plan, packed))
    block = jnp.concatenate(both, axis=0)

    def put(i, carry):
        chunk[i] = block
        return carry

    lax.fori_loop(0, plan.devices, put, 0, unroll=8)


def own_rows(plan, cells):
    if plan.near == 1:
        return jnp.where(lax.axis_index("gy") == 0, cells[0:4], cells[4:8])
    return cells[4:8]


class Level:
    def __init__(self, plan, level):
        self.size = tuple(n >> (level - 2) for n in plan.coarse)
        self.tile = max(8, self.size[1])
        self.shape = (self.size[0], self.tile, 128)
        self.factor = 0.25**level

    def shifts(self, v):
        z, y, x = self.size
        if z > 1:
            none = jnp.zeros((1, self.tile, 128), F32)
            yield jnp.concatenate([none, v[:-1]], axis=0)
            yield jnp.concatenate([v[1:], none], axis=0)
        else:
            yield jnp.zeros_like(v)
            yield jnp.zeros_like(v)
        row = lax.broadcasted_iota(jnp.int32, self.shape, 1)
        lane = lax.broadcasted_iota(jnp.int32, self.shape, 2)
        up, down = pltpu.roll(v, 1, 1), pltpu.roll(v, self.tile - 1, 1)
        if y == self.tile:
            up = jnp.where(row == 0, 0.0, up)
            down = jnp.where(row == self.tile - 1, 0.0, down)
        yield up
        yield down
        left, right = pltpu.roll(v, 1, 2), pltpu.roll(v, 127, 2)
        if x == 128:
            left = jnp.where(lane == 0, 0.0, left)
            right = jnp.where(lane == 127, 0.0, right)
        yield left
        yield right

    def prepare(self, mobility, source):
        z, y, x = self.size
        row = lax.broadcasted_iota(jnp.int32, self.shape, 1)
        lane = lax.broadcasted_iota(jnp.int32, self.shape, 2)
        inside = (row < y) & (lane < x)
        sums = [mobility + near for near in self.shifts(mobility)]
        self.diagonal = 0.5 * (
            ((sums[0] + sums[1]) + (sums[2] + sums[3])) + (sums[4] + sums[5])
        )
        h = jnp.where(inside, 0.4 / self.diagonal, 0.0)
        self.weights = [h * s for s in sums]
        self.first = (2.0 / self.factor) * h * source
        self.source = source

    def pull(self, v):
        t = [w * near for w, near in zip(self.weights, self.shifts(v))]
        return ((t[0] + t[1]) + (t[2] + t[3])) + (t[4] + t[5])

    def relax(self, v):
        return 0.2 * v + self.first + self.pull(v)

    def leftover(self, v):
        return self.source - self.factor * (self.diagonal * (v - 1.25 * self.pull(v)))


def lanes_2d(values, index):
    flat = values.reshape(-1, 128)
    rows = flat.shape[0]
    lane = lax.broadcasted_iota(jnp.int32, (rows, 128), 1)
    return gather(flat, index(lane)).reshape(values.shape)


def coarsen(values, coarse, fine_ref):
    z, y, x = coarse.size
    pairs = values.reshape(z, 2, values.shape[1], 128)
    fine_ref[0:z, 0 : values.shape[1], :] = pairs[:, 0] + pairs[:, 1]
    tile = coarse.tile
    full = fine_ref[0:z, pl.ds(0, tile, 2), :] + fine_ref[0:z, pl.ds(1, tile, 2), :]
    full = lanes_2d(full, lambda lane: (2 * lane) & 127) + lanes_2d(
        full, lambda lane: (2 * lane + 1) & 127
    )
    lane = lax.broadcasted_iota(jnp.int32, full.shape, 2)
    return jnp.where(lane < x, 0.125 * full, 0.0)


def refine(values, fine, coarse, fine_ref):
    z, y, x = coarse.size
    wide = lanes_2d(values, lambda lane: lax.shift_right_logical(lane, 1))
    fine_ref[0:z, pl.ds(0, y, 2), :] = wide[:, 0:y]
    fine_ref[0:z, pl.ds(1, y, 2), :] = wide[:, 0:y]
    rows = fine_ref[0:z, 0 : fine.tile, :]
    return jnp.broadcast_to(rows[:, None], (z, 2, fine.tile, 128)).reshape(fine.shape)


def ascend(plan, n, width, m_ref, h_ref, e_ref, k_ref, below, v_ref, w_ref):
    lanes = slice(0, width)
    for a, b, c in np.ndindex(n, n, n):
        v_ref[a, b, c] = k_ref[a, b, c, :, lanes] + below(a, b, c)
    for old, new in ((v_ref, w_ref), (w_ref, v_ref)):
        for a, b, c in np.ndindex(n, n, n):
            new[a, b, c] = (
                0.2 * old[a, b, c]
                + e_ref[a, b, c, :, lanes]
                + pull(plan, n, m_ref, old, h_ref, a, b, c, width)
            )


def up_kernel(plan, *refs):
    joined, m0, h0, e0, k0, m1, h1, e1, k1, out = refs[:10]
    v0, w0, v1, w1, window, r2, m2, v2 = refs[10:18]
    fine_refs = refs[18:21]
    tile = plan.tile
    gz, gy, gx = plan.counts
    iz, iy, ix = (lax.axis_index(axis) for axis in AXES)
    inside = inside_mask(plan)

    def unpack(z_block, carry):
        for z in range(4):
            for y_block in range(gy):
                value = jnp.zeros((8, 128), F32)
                for x_block in range(gx):
                    part = joined[(z_block * gy + y_block) * gx + x_block]
                    value = jnp.where(
                        between(32 * x_block, 32 * x_block + 32),
                        pltpu.roll(part, (32 * (x_block - z)) % 128, 1),
                        value,
                    )
                rows = slice(4 * y_block, 4 * y_block + 4)
                r2[4 * z_block + z, rows, :] = value[0:4]
                m2[4 * z_block + z, rows, :] = value[4:8]
        return carry

    lax.fori_loop(0, gz, unpack, 0, unroll=4)
    for ref in fine_refs:
        ref[...] = jnp.zeros(ref.shape, F32)

    levels = [Level(plan, level) for level in range(2, LEVELS + 1)]
    mobility, source = m2[...], r2[...]
    kept = []
    for i, level in enumerate(levels):
        level.prepare(mobility, source)
        if i < len(levels) - 1:
            e = level.first + level.first * 0.2 + level.pull(level.first)
            kept.append(e)
            args = (levels[i + 1], fine_refs[i])
            mobility = coarsen(mobility, *args)
            source = coarsen(level.leftover(e), *args)
    level = levels[-1]
    v = level.first
    for repeat in range(COARSE - 1):
        v = level.relax(v)
    for i in range(len(levels) - 2, -1, -1):
        v = kept[i] + refine(v, levels[i], levels[i + 1], fine_refs[i])
        v = levels[i].relax(levels[i].relax(v))

    v2[...] = jnp.zeros(v2.shape, F32)
    margin = 0 if plan.near == 1 else 8
    v2[pl.ds(HALO, plan.coarse[0]), pl.ds(margin, plan.coarse[1]), :] = v
    planes = []
    for z in range(ZW):
        if plan.near == 1:
            planes.append(v2[4 * iz + z])
        else:
            planes.append(v2[4 * iz + z, pl.ds(4 * iy + 4, tile), :])
    for t in range(3):
        value = jnp.zeros((tile, 128), F32)
        for z in range(ZW):
            offset = lane_of(z) - 128 * t
            low, high = max(offset, 0), min(offset + XW, 128)
            if low < high:
                shift = lax.rem(offset % 128 + HALO - 32 * ix + 256, 128)
                value = jnp.where(
                    between(low, high, tile), pltpu.roll(planes[z], shift, 1), value
                )
        lanes = slice(128 * t, 128 * t + 128)
        window[:, lanes] = jnp.where(inside[:, lanes], value, 0.0)

    below = window[...]

    ascend(plan, 2, LW, m1, h1, e1, k1, lambda a, b, c: below, v1, w1)

    def from_half(a, b, c):
        return v1[a // 2, b // 2, c // 2, :, 0:NARROW]

    ascend(plan, 4, NARROW, m0, h0, e0, k0, from_half, v0, w0)

    lane = lane_iota(tile)
    natural = 32 * (lane & 3) + lax.shift_right_logical(lane, 2)
    starts = [lane_of(z + HALO) + HALO for z in range(4)]
    places_of = [(lane - start) & 127 for start in starts]
    index = [(natural + start) & 127 for start in starts]

    def store(pz, carry):
        for py in range(4):
            parts = [
                [v0[pz, py, px, :, 128 * t : 128 * t + 128] for t in range(2)]
                for px in range(4)
            ]
            parts = [
                [part if px == 0 else pltpu.roll(part, 32 * px, 1) for part in row]
                for px, row in enumerate(parts)
            ]
            for z, start in enumerate(starts):
                low, high = start // 128, (start + 31) // 128
                value = None
                for px in range(4):
                    part = parts[px][low]
                    if low != high:
                        first = (places_of[z] & 31) < 128 - start % 128
                        part = jnp.where(first, part, parts[px][high])
                    turn = lax.shift_right_logical(places_of[z], 5) == px
                    value = part if value is None else jnp.where(turn, part, value)
                value = gather(value, index[z])
                out[4 * z + pz, pl.ds(py, 4, 4), :] = own_rows(plan, value)
        return carry

    lax.fori_loop(0, 4, store, 0, unroll=4)


def call(plan, kernel, outs, scratch, *args):
    return pl.pallas_call(
        kernel,
        out_shape=[jax.ShapeDtypeStruct(shape, F32) for shape in outs],
        scratch_shapes=[pltpu.VMEM(shape, F32) for shape in scratch],
        compiler_params=pltpu.CompilerParams(
            vmem_limit_bytes=(3 * plan.tile + plan.coarse[0] // 4) * 1024 * 1024
        ),
    )(*args)


def solution(mesh):
    plan = Plan(mesh)
    near, tile = plan.near, plan.tile
    z2, y2, x2 = plan.coarse
    full = (4, 4, 4, tile, LW)
    narrow = (4, 4, 4, tile, NARROW)
    half = (2, 2, 2, tile, LW)
    full_rim = (6, 6, 6, tile, LW)
    half_rim = (4, 4, 4, tile, LW)

    def swap(values, *swaps):
        return lax.ppermute(values, AXES, plan.pairs(swaps))

    def on_device(residual, mobility):
        assert residual.shape == (16, 16, 128)
        cells = jnp.stack([residual, mobility])
        even, odd, *sent = call(
            plan,
            lambda *refs: first_kernel(plan, *refs),
            [(16 * (M_DEEP + R_DEEP), 128)] * 2 + [(Y_ROWS, 128)] * near
            + [(4, 16, 128)]
            + [(DIAGONAL_ROWS, 128)] * near,
            [],
            cells,
        )
        arrived = [swap(sent[y], None, y, None) for y in range(near)]
        x_arrived = [swap(sent[near], None, None, 1)]
        x_arrived += [swap(sent[1 + near + y], None, y, 1) for y in range(near)]
        z_own = [swap(odd, 1, None, None), swap(even, 0, None, None)][::-1]
        *beside, even, odd = call(
            plan,
            lambda *refs: edges_kernel(plan, *refs),
            [(2, 16, 16, 128)] * near + [(4, plan.rows, 128)] * 2,
            [],
            cells,
            *arrived,
            *x_arrived,
        )
        edges = [swap(even, None, None, 0), odd]
        sends = call(
            plan,
            lambda *refs: z_pack_kernel(plan, *refs),
            [(plan.payload, 128)] * 2,
            [],
            *beside,
            *edges[::-1],
            *z_own,
        )
        arrived = [swap(sends[1], 1, None, None), swap(sends[0], 0, None, None)][::-1]
        (own,) = call(
            plan,
            lambda *refs: own_kernel(plan, *refs),
            [(2, *narrow)],
            [(2, 16, plan.rows, 128), (2, 4, plan.rows, 128)],
            cells,
            *beside,
            *edges[::-1],
        )
        halo_scratch = [(2, EDGE, plan.rows, 128), (4, plan.rows, 128)]
        (other,) = call(
            plan,
            lambda *refs: place_kernel(plan, *refs),
            [(2, 4, 4, 4, tile, 128)],
            halo_scratch,
            z_own[1],
            arrived[1],
        )
        chunk, *state = call(
            plan,
            lambda *refs: down_kernel(plan, *refs),
            [(plan.devices, 8, 128)] + [full_rim] + [full] * 3 + [half_rim] + [half] * 3,
            [full] * 2
            + [half] * 2
            + halo_scratch,
            own,
            other,
            z_own[0],
            arrived[0],
        )
        joined = lax.all_to_all(chunk, AXES, 0, 0, tiled=True)
        levels = [Level(plan, level) for level in range(2, LEVELS + 1)]
        margin = 0 if near == 1 else 16
        (out,) = call(
            plan,
            lambda *refs: up_kernel(plan, *refs),
            [(16, 16, 128)],
            [narrow] * 2
            + [half] * 2
            + [(tile, LW)]
            + [(z2, y2, 128)] * 2
            + [(z2 + 2 * HALO, y2 + margin, 128)]
            + [
                (fine.size[0], max(fine.tile, 2 * coarse.tile), 128)
                for fine, coarse in zip(levels[:-1], levels[1:])
            ],
            joined,
            *state,
        )
        return out

    spec = P(*AXES)
    return jax.shard_map(
        on_device, mesh=mesh, in_specs=(spec, spec), out_specs=spec, check_vma=False
    )
```

```python
import jax
import jax.numpy as jnp
import numpy as np
from jax import lax
from jax.experimental import pallas as pl
from jax.experimental.pallas import tpu as pltpu
from jax.sharding import PartitionSpec as P

LEVELS = 5
COARSE = 8
AXES = ("grp", "gy", "gx")
F32 = jnp.float32

HALO = 3
ZW = 4 + 2 * HALO
XW = 32 + 2 * HALO
LW = 384
NARROW = 256
EDGE = 4 * HALO
M_DEEP, M_FAR, R_DEEP, R_FAR = 11, 4, 10, 3

NEAR_TILES = (
    [[(1, d, 0)] for d in range(1, 7)]
    + [[(0, d, 0)] for d in range(1, 6)]
    + [[(1, 7, 0), (1, 11, 6)], [(1, 8, 0), (1, 10, 5)], [(0, 6, 0), (0, 10, 6)]]
    + [[(0, 7, 0), (0, 9, 5)], [(1, 9, 0), (0, 8, 4)]]
)
FAR_TILES = [[(1, 1, 0), (1, 2, 3), (0, 1, 6)], [(0, 2, 0), (1, 3, 2), (0, 3, 4), (1, 4, 5)]]
BESIDE_ROWS = 8 * (len(NEAR_TILES) + len(FAR_TILES) + 1)
M_EDGE, R_EDGE = 11, 10
Y_FAR = (2, 3)
Y_STARTS = (0, 16 * (8 + Y_FAR[0]))
Y_ROWS = Y_STARTS[1] + 16 * (8 + Y_FAR[1])
DIAGONAL_ROWS = 48


def lane_of(z):
    return ((z - 2) * XW) % LW


def lane_iota(rows=8):
    return lax.broadcasted_iota(jnp.int32, (rows, 128), 1)


LANES = lax.GatherDimensionNumbers(
    offset_dims=(),
    collapsed_slice_dims=(1,),
    start_index_map=(1,),
    operand_batching_dims=(0,),
    start_indices_batching_dims=(0,),
)


def gather(source, index):
    return lax.gather(
        source, index[..., None], LANES, (1, 1), mode=lax.GatherScatterMode.PROMISE_IN_BOUNDS
    )


def every_lane(offset, px, rows):
    return (4 * lane_iota(rows) + ((px - 4 * offset) % 128)) & 127


def between(low, high, rows=8):
    lane = lane_iota(rows)
    return (lane >= low) & (lane < high)


def window_cells(t, rows):
    cell = lane_iota(rows) + 128 * t
    cell = jnp.where(cell >= lane_of(0), cell - lane_of(0), cell + 2 * XW)
    z = jnp.zeros((rows, 128), jnp.int32)
    for k in range(1, ZW + 1):
        z = z + (cell >= k * XW).astype(jnp.int32)
    return z, cell - z * XW


EDGE_STARTS = {(1, 0): 0, (1, 1): 33, (0, 0): 66, (0, 1): 96}


def edge_send_lanes():
    lane = lane_iota()
    mobile = lane < 66
    right = ((lane >= 33) & mobile) | (lane >= 96)
    start = jnp.where(mobile, jnp.where(right, 33, 0), jnp.where(right, 96, 66))
    width = jnp.where(mobile, M_EDGE, R_EDGE)
    t = lane - start
    z = (t >= width).astype(jnp.int32) + (t >= 2 * width).astype(jnp.int32)
    first = jnp.where(right, 0, EDGE - width)
    return jnp.minimum(jnp.where(mobile, 48, 0) + z * 12 + first + t - z * width, 95), right


def edge_own_lanes(side, t, rows):
    z, x = window_cells(t, rows)
    x = x if side == 0 else x - (XW - HALO)
    here = (z >= HALO) & (z < HALO + 4) & (x >= 0) & (x < HALO)
    return jnp.where(here, (z - HALO) * 12 + 4 * x, 0), here


def halo_start(side):
    return lane_of(0 if side == 0 else HALO + 4) % 128


def halo_cells(side, px, rows):
    p = (lane_iota(rows) - (halo_start(side) + 32 * px)) & 127
    z = (p >= XW).astype(jnp.int32) + (p >= 2 * XW).astype(jnp.int32)
    return z, p - z * XW, p < HALO * XW


def halo_turn(side, px, rows):
    z, x, _ = halo_cells(side, px, rows)
    return jnp.where((x >= HALO) & (x < XW - HALO), z, 3)


def halo_lanes(side, z, rows):
    q = (lane_iota(rows) - (halo_start(side) + z * XW + HALO)) & 127
    return 4 * (q & 31) + lax.shift_right_logical(q, 5)


def edge_far_lanes(side, a, rows):
    width = M_EDGE if a == 1 else R_EDGE
    index = jnp.zeros((rows, 128), jnp.int32)
    for px in range(4):
        z, x, here = halo_cells(side, px, rows)
        left = EDGE_STARTS[a, 0] + z * width + 4 * x + px - (EDGE - width)
        right = EDGE_STARTS[a, 1] + z * width + 4 * (x - (XW - HALO)) + px
        index = jnp.where(here & (x < HALO), left, index)
        index = jnp.where(here & (x >= XW - HALO), right, index)
    return jnp.clip(index, 0, 127)


class Plan:
    def __init__(self, mesh):
        self.counts = tuple(mesh.shape[axis] for axis in AXES)
        self.near = 1 if self.counts[1] == 2 else 2
        self.rows = 16 * (1 + self.near)
        self.cells = self.rows // 4
        self.tile = -(-self.cells // 8) * 8
        self.edge_start = BESIDE_ROWS * self.near
        self.payload = self.edge_start + 32 * (2 + self.near)
        self.devices = self.counts[0] * self.counts[1] * self.counts[2]
        self.coarse = (4 * self.counts[0], 4 * self.counts[1], 32 * self.counts[2])

    def pairs(self, swaps):
        out = []
        for index in np.ndindex(*self.counts):
            there = []
            for axis, swap in enumerate(swaps):
                i, n = index[axis], self.counts[axis]
                j = i if swap is None else (i + 1 if i % 2 == swap else i - 1)
                if axis == 2:
                    j = j % n
                there.append(j)
            if not all(0 <= j < n for j, n in zip(there, self.counts)):
                there = [index[0], index[1], index[2] ^ 1]
            out.append(
                (
                    int(np.ravel_multi_index(index, self.counts)),
                    int(np.ravel_multi_index(there, self.counts)),
                )
            )
        return out

    def y_places(self):
        iy = lax.axis_index("gy")
        if self.near == 1:
            return 16 * iy, [(1 - iy, 16 * (1 - iy))]
        odd = lax.rem(iy, 2)
        return 16, [(1 - odd, 32 * (1 - odd)), (odd, 32 * odd)]


def is_even(axis):
    return lax.rem(lax.axis_index(axis), 2) == 0


def at(start, size):
    if isinstance(start, int):
        return pl.ds(start, size)
    return pl.ds(pl.multiple_of(start, 8), size)


def x_edge(block, pz, half, to_right):
    out = jnp.zeros((8, 128), F32)
    for a in range(2):
        for z in range(4):
            cells = block[a, 4 * z + pz, 8 * half : 8 * half + 8, :]
            base = a * 48 + z * 12
            shift = jnp.where(to_right, (base - (128 - EDGE)) % 128, base)
            out = jnp.where(between(base, base + EDGE), pltpu.roll(cells, shift, 1), out)
    return out


def first_kernel(plan, cells_ref, *outs):
    outs, edge_ref, diagonal = outs[: 2 + plan.near], outs[2 + plan.near], outs[3 + plan.near :]
    to_right = jnp.logical_not(is_even("gx"))
    edges = [[x_edge(cells_ref, pz, half, to_right) for half in range(2)] for pz in range(4)]
    for pz in range(4):
        edge_ref[pz, 0:8, :], edge_ref[pz, 8:16, :] = edges[pz]
    for out, (side, _) in zip(diagonal, plan.y_places()[1]):
        last = side == 1
        for pz in range(4):
            out[8 * pz : 8 * pz + 8, :] = jnp.where(last, edges[pz][1], edges[pz][0])
        for i in range(2):
            far = [jnp.where(last, edges[pz][0], edges[pz][1]) for pz in (2 * i, 2 * i + 1)]
            out[32 + 8 * i : 40 + 8 * i, :] = packed(
                [(far[0], 0), (far[1], 3)], jnp.logical_not(last)
            )
    z_even = is_even("grp")
    for swap, out in enumerate(outs[:2]):
        top = z_even if swap == 0 else jnp.logical_not(z_even)
        row = 0
        for a, deep in ((1, M_DEEP), (0, R_DEEP)):
            for d in range(1, deep + 1):
                out[row : row + 16, :] = cells_ref[a, jnp.where(top, 16 - d, d - 1)]
                row += 16
    for out, (side, _) in zip(outs[2:], plan.y_places()[1]):
        last = side == 1
        for a in range(2):
            near, far, deep = Y_STARTS[a], Y_STARTS[a] + 128, Y_FAR[a]
            for plane in range(16):
                cells = cells_ref[a, plane]
                rows = jnp.where(last, cells[8:16], cells[0:8])
                out[near + 8 * plane : near + 8 * plane + 8, :] = rows
                rows = jnp.where(last, cells[8 - deep : 8], cells[8 : 8 + deep])
                out[far + deep * plane : far + deep * (plane + 1), :] = rows


def edges_kernel(plan, *refs):
    cells_ref = refs[0]
    near = plan.near
    arrived = refs[1 : 1 + near]
    x_arrived = refs[1 + near : 2 + 2 * near]
    beside = refs[2 + 2 * near : 2 + 3 * near]
    even_ref, odd_ref = refs[-2:]
    own_row, places = plan.y_places()
    even = is_even("gx")
    for ref, out, (side, _) in zip(arrived, beside, places):
        following = side == 1
        for a in range(2):
            near_row, far, deep = Y_STARTS[a], Y_STARTS[a] + 128, Y_FAR[a]
            for plane in range(16):
                rows = ref[near_row + 8 * plane : near_row + 8 * plane + 8, :]
                more = ref[far + deep * plane : far + deep * (plane + 1), :]
                none = jnp.zeros((8 - deep, 128), F32)
                more = jnp.concatenate([more, none], axis=0)
                more = pltpu.roll(more, jnp.where(following, 0, 8 - deep), 0)
                out[a, plane, at(8 * (1 - side), 8), :] = rows
                out[a, plane, at(8 * side, 8), :] = more
    for i, block in enumerate((cells_ref, *beside)):
        start = own_row if i == 0 else places[i - 1][1]
        if i == 0:
            odd_ref[:, at(start, 16), :] = x_arrived[0][...]
        else:
            side = places[i - 1][0]
            ref = x_arrived[i]
            for pz in range(4):
                odd_ref[pz, at(start + 8 * (1 - side), 8), :] = ref[8 * pz : 8 * pz + 8, :]
                row = 32 + 8 * (pz // 2)
                odd_ref[pz, at(start + 8 * side, 8), :] = unpacked(
                    ref[row : row + 8, :], 3 * (pz % 2), side == 1
                )
        for pz in range(4):
            for half in range(2):
                even_ref[pz, at(start + 8 * half, 8), :] = x_edge(block, pz, half, even)


def packed(pieces, following):
    row = lax.broadcasted_iota(jnp.int32, (8, 128), 0)
    row = jnp.where(following, row, 7 - row)
    out = None
    for value, first in pieces:
        if out is None:
            out = value
        else:
            moved = pltpu.roll(value, jnp.where(following, first, 8 - first), 0)
            out = jnp.where(row >= first, moved, out)
    return out


def unpacked(value, first, following):
    if first == 0:
        return value
    return pltpu.roll(value, jnp.where(following, 8 - first, first), 0)


def z_pack_kernel(plan, *refs):
    near = plan.near
    beside = refs[:near]
    x_odd_ref, x_even_ref = refs[near : near + 2]
    outs = refs[-2:]
    own_row, places = plan.y_places()
    x_even = is_even("gx")
    z_even = is_even("grp")
    lanes_0, use_right = edge_send_lanes()
    for swap, out in enumerate(outs):
        top = z_even if swap == 0 else jnp.logical_not(z_even)
        lanes = lanes_0 + jnp.where(top, 12, 0)

        def edge(pz, row):
            even, odd = x_even_ref[pz, at(row, 8), :], x_odd_ref[pz, at(row, 8), :]
            left = gather(jnp.where(x_even, odd, even), lanes)
            right = gather(jnp.where(x_even, even, odd), lanes)
            return jnp.where(use_right, right, left)

        for i, (side, base) in enumerate(places):
            following = side == 1
            to = i * BESIDE_ROWS
            for tiles, row in ((NEAR_TILES, 8 * (1 - side)), (FAR_TILES, 8 * side)):
                for pieces in tiles:
                    values = [
                        (beside[i][a, jnp.where(top, 16 - d, d - 1), at(row, 8), :], first)
                        for a, d, first in pieces
                    ]
                    out[to : to + 8, :] = packed(values, following)
                    to += 8
            values = [(edge(pz, base + 8 * side), 2 * pz) for pz in range(4)]
            out[to : to + 8, :] = packed(values, following)
        to = plan.edge_start
        rows = [own_row, own_row + 8] + [base + 8 * (1 - side) for side, base in places]
        for pz in range(4):
            for row in rows:
                out[to : to + 8, :] = edge(pz, row)
                to += 8


def padded_rows(plan, cells):
    if plan.cells == plan.tile:
        return cells
    return jnp.concatenate(
        [cells, jnp.zeros((plan.tile - plan.cells, cells.shape[1]), F32)], axis=0
    )


def every_fourth(plan, ref, lead, py):
    return padded_rows(plan, ref[(*lead, pl.ds(py, plan.cells, 4), slice(None))])


def own_kernel(plan, *refs):
    near = plan.near
    cells_ref, *beside = refs[: 1 + near]
    x_odd_ref, x_even_ref = refs[1 + near : 3 + near]
    out, planes, sides = refs[-3:]
    tile = plan.tile
    own_row, places = plan.y_places()
    x_even = is_even("gx")
    planes[:, :, at(own_row, 16), :] = cells_ref[...]
    for (_, base), block in zip(places, beside):
        planes[:, :, at(base, 16), :] = block[...]
    even, odd = x_even_ref[...], x_odd_ref[...]
    sides[0] = jnp.where(x_even, odd, even)
    sides[1] = jnp.where(x_even, even, odd)

    inside = inside_mask(plan)
    offsets = [lane_of(z + HALO) + HALO for z in range(4)]
    index = [[every_lane(offset, px, tile) for px in range(4)] for offset in offsets]
    from_edge = {(s, t): edge_own_lanes(s, t, tile) for s in range(2) for t in range(2)}

    def body(pz, carry):
        for a in range(2):
            for py in range(4):
                cells = [every_fourth(plan, planes, (a, 4 * z + pz), py) for z in range(4)]
                side = [every_fourth(plan, sides, (s, pz), py) for s in range(2)]
                for px in range(4):
                    parts = [gather(cells[z], index[z][px]) for z in range(4)]
                    for t in range(2):
                        value = jnp.zeros((tile, 128), F32)
                        for z in range(4):
                            offset = offsets[z] - 128 * t
                            low, high = max(offset, 0), min(offset + 32, 128)
                            if low < high:
                                value = jnp.where(between(low, high, tile), parts[z], value)
                        for s in range(2):
                            if (s, t) in from_edge:
                                lanes, here = from_edge[s, t]
                                lanes = lanes + (48 * a + px)
                                value = jnp.where(here, gather(side[s], lanes), value)
                        lanes = slice(128 * t, 128 * t + 128)
                        out[a, pz, py, px, :, lanes] = jnp.where(inside[:, lanes], value, 0.0)
        return carry

    lax.fori_loop(0, 4, body, 0)


def inside_tile(plan, t):
    tile = plan.tile
    z, x = window_cells(t, tile)
    here = z < ZW
    z = z + (4 * lax.axis_index("grp") - HALO)
    x = x + (32 * lax.axis_index("gx") - HALO)
    here = here & (z >= 0) & (z < plan.coarse[0]) & (x >= 0) & (x < plan.coarse[2])
    if plan.near == 2:
        row = lax.broadcasted_iota(jnp.int32, (tile, 128), 0)
        y = row + (4 * lax.axis_index("gy") - 4)
        here = here & (row < plan.cells) & (y >= 0) & (y < plan.coarse[1])
    return here


def inside_mask(plan):
    masks = [jnp.where(inside_tile(plan, t), 1.0, 0.0) for t in range(3)]
    return jnp.concatenate(masks, axis=1) > 0.5


def roll_lanes(value, shift):
    return pltpu.roll(value, shift % value.shape[1], 1)


def fill_rim(plan, ref, n):
    tile = plan.tile
    row = lax.broadcasted_iota(jnp.int32, (tile, LW), 0)
    for i in range(1, n + 1):
        for j in range(1, n + 1):
            z_low, z_high = ref[n, i, j], ref[1, i, j]
            y_low, y_high = ref[i, n, j], ref[i, 1, j]
            x_low, x_high = ref[i, j, n], ref[i, j, 1]
            ref[0, i, j] = roll_lanes(z_low, XW)
            ref[n + 1, i, j] = roll_lanes(z_high, -XW)
            ref[i, 0, j] = jnp.where(row == 0, 0.0, pltpu.roll(y_low, 1, 0))
            ref[i, n + 1, j] = jnp.where(
                row == tile - 1, 0.0, pltpu.roll(y_high, tile - 1, 0)
            )
            ref[i, j, 0] = roll_lanes(x_low, 1)
            ref[i, j, n + 1] = roll_lanes(x_high, -1)


def around(ref, a, b, c, width=LW):
    lanes = slice(0, width)
    return (
        ref[a, b + 1, c + 1, :, lanes],
        ref[a + 2, b + 1, c + 1, :, lanes],
        ref[a + 1, b, c + 1, :, lanes],
        ref[a + 1, b + 2, c + 1, :, lanes],
        ref[a + 1, b + 1, c, :, lanes],
        ref[a + 1, b + 1, c + 2, :, lanes],
    )


def around_rimless(plan, ref, n, a, b, c, width):
    tile = plan.tile
    row = lax.broadcasted_iota(jnp.int32, (tile, width), 0)

    def cells(i, j, k):
        return ref[i, j, k, :, 0:width]

    def first_row(value):
        return jnp.where(row == 0, 0.0, pltpu.roll(value, 1, 0))

    def last_row(value):
        return jnp.where(row == tile - 1, 0.0, pltpu.roll(value, tile - 1, 0))

    return (
        cells(a - 1, b, c) if a > 0 else roll_lanes(cells(n - 1, b, c), XW),
        cells(a + 1, b, c) if a < n - 1 else roll_lanes(cells(0, b, c), -XW),
        cells(a, b - 1, c) if b > 0 else first_row(cells(a, n - 1, c)),
        cells(a, b + 1, c) if b < n - 1 else last_row(cells(a, 0, c)),
        cells(a, b, c - 1) if c > 0 else roll_lanes(cells(a, b, n - 1), 1),
        cells(a, b, c + 1) if c < n - 1 else roll_lanes(cells(a, b, 0), -1),
    )


def pull(plan, n, m_ref, v_ref, h_ref, a, b, c, width=LW):
    cells = around_rimless(plan, v_ref, n, a, b, c, width)
    mobility = around(m_ref, a, b, c, width)
    total = ((cells[0] + cells[1]) + (cells[2] + cells[3])) + (cells[4] + cells[5])
    products = [m * v for m, v in zip(mobility, cells)]
    other = ((products[0] + products[1]) + (products[2] + products[3])) + (
        products[4] + products[5]
    )
    centre = m_ref[a + 1, b + 1, c + 1, :, 0:width]
    return h_ref[a, b, c, :, 0:width] * (centre * total + other)


def descend(plan, n, factor, inside, m_ref, r_ref, d_ref, h_ref, e_ref, k_ref):
    fill_rim(plan, m_ref, n)
    for a, b, c in np.ndindex(n, n, n):
        s = around(m_ref, a, b, c)
        d = 3.0 * m_ref[a + 1, b + 1, c + 1] + 0.5 * (
            ((s[0] + s[1]) + (s[2] + s[3])) + (s[4] + s[5])
        )
        h = jnp.where(inside, 0.4 / d, 0.0)
        d_ref[a, b, c] = d
        h_ref[a, b, c] = h
        e_ref[a, b, c] = (2.0 / factor) * h * r_ref[a, b, c]
    for a, b, c in np.ndindex(n, n, n):
        k_ref[a, b, c] = 1.2 * e_ref[a, b, c] + pull(plan, n, m_ref, e_ref, h_ref, a, b, c)


def leftover(plan, n, factor, m_ref, r_ref, d_ref, h_ref, k_ref, a, b, c):
    away = k_ref[a, b, c] - 1.25 * pull(plan, n, m_ref, k_ref, h_ref, a, b, c)
    return r_ref[a, b, c] - factor * (d_ref[a, b, c] * away)


def place_halo(plan, swap, z_own_ref, z_ref, planes, sides, emit):
    near, tile = plan.near, plan.tile
    own_row, places = plan.y_places()
    upper = is_even("grp")
    if swap == 1:
        upper = jnp.logical_not(upper)

    def choose(make):
        return jnp.where(upper, make(1), make(0))

    def plane_of(d):
        return jnp.where(upper, d - 1, EDGE - d)

    for a, deep, far in ((1, M_DEEP, M_FAR), (0, R_DEEP, R_FAR)):
        for d in range(far + 1, EDGE + 1):
            planes[a, plane_of(d)] = jnp.zeros((plan.rows, 128), F32)
        for d in range(1, deep + 1):
            row = 16 * (d - 1) if a == 1 else 16 * (M_DEEP + d - 1)
            planes[a, plane_of(d), at(own_row, 16), :] = z_own_ref[row : row + 16, :]
    for i, (side, base) in enumerate(places):
        following = side == 1
        row = i * BESIDE_ROWS
        for tiles, to in ((NEAR_TILES, base + 8 * (1 - side)), (FAR_TILES, base + 8 * side)):
            for pieces in tiles:
                for a, d, first in pieces:
                    planes[a, plane_of(d), at(to, 8), :] = unpacked(
                        z_ref[row : row + 8, :], first, following
                    )
                row += 8
        for pz in range(4):
            sides[pz, at(base + 8 * side, 8), :] = unpacked(
                z_ref[row : row + 8, :], 2 * pz, following
            )
    row = plan.edge_start
    rows = [own_row, own_row + 8] + [base + 8 * (1 - side) for side, base in places]
    for pz in range(4):
        for to in rows:
            sides[pz, at(to, 8), :] = z_ref[row : row + 8, :]
            row += 8

    index = [choose(lambda side: halo_lanes(side, z, tile)) for z in range(HALO)]
    turns = [choose(lambda side: halo_turn(side, px, tile)) for px in range(4)]
    edge_index = [choose(lambda side: edge_far_lanes(side, a, tile)) for a in range(2)]

    def place(pz, carry):
        for a in range(2):
            for py in range(4):
                parts = [
                    gather(every_fourth(plan, planes, (a, 4 * z + pz), py), index[z])
                    for z in range(HALO)
                ]
                edge = gather(every_fourth(plan, sides, (pz,), py), edge_index[a])
                for px in range(4):
                    turn = turns[px]
                    value = jnp.where(turn == 1, parts[1], parts[0])
                    value = jnp.where(turn == 2, parts[2], value)
                    value = jnp.where(turn == 3, edge, value)
                    if px > 0:
                        value = pltpu.roll(value, 128 - 32 * px, 1)
                    emit(a, pz, py, px, value)
        return carry

    lax.fori_loop(0, 4, place, 0)


def place_kernel(plan, z_own_ref, z_ref, out, planes, sides):
    def emit(a, pz, py, px, value):
        out[a, pz, py, px] = value

    place_halo(plan, 1, z_own_ref, z_ref, planes, sides, emit)


def down_kernel(plan, *refs):
    own_ref, other_ref, z_own_ref, z_ref = refs[:4]
    chunk, m0, h0, e0, k0, m1, h1, e1, k1 = refs[4:13]
    r0, d0, r1, d1, planes, sides = refs[13:]
    tile = plan.tile
    inside = inside_mask(plan)
    z_even = is_even("grp")
    z = [window_cells(t, tile)[0] for t in range(3)]
    here = [inside_tile(plan, t) for t in range(3)]
    lower_0, upper_1 = (z[0] < HALO) & here[0], (z[1] >= HALO + 4) & here[1]
    lower_2, upper_2 = (z[2] < HALO) & here[2], (z[2] >= HALO + 4) & here[2]

    def emit(a, pz, py, px, value):
        other = other_ref[a, pz, py, px]
        lower = jnp.where(z_even, other, value)
        upper = jnp.where(z_even, value, other)
        tiles = (
            jnp.where(lower_0, lower, own_ref[a, pz, py, px, :, 0:128]),
            jnp.where(upper_1, upper, own_ref[a, pz, py, px, :, 128:256]),
            jnp.where(lower_2, lower, jnp.where(upper_2, upper, 0.0)),
        )
        for t, cells in enumerate(tiles):
            lanes = slice(128 * t, 128 * t + 128)
            if a == 1:
                m0[pz + 1, py + 1, px + 1, :, lanes] = cells
            else:
                r0[pz, py, px, :, lanes] = cells

    place_halo(plan, 0, z_own_ref, z_ref, planes, sides, emit)

    descend(plan, 4, 1.0, inside, m0, r0, d0, h0, e0, k0)
    for a, b, c in np.ndindex(2, 2, 2):
        rest = jnp.zeros((tile, LW), F32)
        mobility = jnp.zeros((tile, LW), F32)
        for da, db, dc in np.ndindex(2, 2, 2):
            i, j, k = 2 * a + da, 2 * b + db, 2 * c + dc
            rest = rest + leftover(plan, 4, 1.0, m0, r0, d0, h0, k0, i, j, k)
            mobility = mobility + m0[i + 1, j + 1, k + 1]
        r1[a, b, c] = 0.125 * rest
        m1[a + 1, b + 1, c + 1] = 0.125 * mobility
    descend(plan, 2, 0.25, inside, m1, r1, d1, h1, e1, k1)
    rest = jnp.zeros((tile, LW), F32)
    mobility = jnp.zeros((tile, LW), F32)
    for a, b, c in np.ndindex(2, 2, 2):
        rest = rest + leftover(plan, 2, 0.25, m1, r1, d1, h1, k1, a, b, c)
        mobility = mobility + m1[a + 1, b + 1, c + 1]
    both = []
    for total in (rest, mobility):
        packed = jnp.zeros((tile, 128), F32)
        for t in range(3):
            part = 0.125 * total[:, 128 * t : 128 * t + 128]
            for z in range(4):
                offset = lane_of(z + HALO) + HALO - 128 * t
                low, high = max(offset, 0), min(offset + 32, 128)
                if low < high:
                    move = 32 * z - offset
                    packed = jnp.where(
                        between(low + move, high + move, tile),
                        pltpu.roll(part, move % 128, 1),
                        packed,
                    )
        both.append(own_rows(plan, packed))
    block = jnp.concatenate(both, axis=0)

    def put(i, carry):
        chunk[i] = block
        return carry

    lax.fori_loop(0, plan.devices, put, 0, unroll=8)


def own_rows(plan, cells):
    if plan.near == 1:
        return jnp.where(lax.axis_index("gy") == 0, cells[0:4], cells[4:8])
    return cells[4:8]


class Level:
    def __init__(self, plan, level):
        self.size = tuple(n >> (level - 2) for n in plan.coarse)
        self.tile = max(8, self.size[1])
        self.shape = (self.size[0], self.tile, 128)
        self.factor = 0.25**level

    def shifts(self, v):
        z, y, x = self.size
        if z > 1:
            none = jnp.zeros((1, self.tile, 128), F32)
            yield jnp.concatenate([none, v[:-1]], axis=0)
            yield jnp.concatenate([v[1:], none], axis=0)
        else:
            yield jnp.zeros_like(v)
            yield jnp.zeros_like(v)
        row = lax.broadcasted_iota(jnp.int32, self.shape, 1)
        lane = lax.broadcasted_iota(jnp.int32, self.shape, 2)
        up, down = pltpu.roll(v, 1, 1), pltpu.roll(v, self.tile - 1, 1)
        if y == self.tile:
            up = jnp.where(row == 0, 0.0, up)
            down = jnp.where(row == self.tile - 1, 0.0, down)
        yield up
        yield down
        left, right = pltpu.roll(v, 1, 2), pltpu.roll(v, 127, 2)
        if x == 128:
            left = jnp.where(lane == 0, 0.0, left)
            right = jnp.where(lane == 127, 0.0, right)
        yield left
        yield right

    def prepare(self, mobility, source):
        z, y, x = self.size
        row = lax.broadcasted_iota(jnp.int32, self.shape, 1)
        lane = lax.broadcasted_iota(jnp.int32, self.shape, 2)
        inside = (row < y) & (lane < x)
        sums = [mobility + near for near in self.shifts(mobility)]
        self.diagonal = 0.5 * (
            ((sums[0] + sums[1]) + (sums[2] + sums[3])) + (sums[4] + sums[5])
        )
        h = jnp.where(inside, 0.4 / self.diagonal, 0.0)
        self.weights = [h * s for s in sums]
        self.first = (2.0 / self.factor) * h * source
        self.source = source

    def pull(self, v):
        shifts = list(self.shifts(v))
        if self.size[1] == 1:
            t = [self.weights[i] * shifts[i] for i in (0, 1, 4, 5)]
            return (t[0] + t[1]) + (t[2] + t[3])
        t = [w * near for w, near in zip(self.weights, shifts)]
        return ((t[0] + t[1]) + (t[2] + t[3])) + (t[4] + t[5])

    def relax(self, v):
        return 0.2 * v + self.first + self.pull(v)

    def leftover(self, v):
        return self.source - self.factor * (self.diagonal * (v - 1.25 * self.pull(v)))


def lanes_2d(values, index):
    flat = values.reshape(-1, 128)
    rows = flat.shape[0]
    lane = lax.broadcasted_iota(jnp.int32, (rows, 128), 1)
    return gather(flat, index(lane)).reshape(values.shape)


def coarsen(values, coarse, fine_ref):
    z, y, x = coarse.size
    pairs = values.reshape(z, 2, values.shape[1], 128)
    fine_ref[0:z, 0 : values.shape[1], :] = pairs[:, 0] + pairs[:, 1]
    tile = coarse.tile
    full = fine_ref[0:z, pl.ds(0, tile, 2), :] + fine_ref[0:z, pl.ds(1, tile, 2), :]
    full = lanes_2d(full, lambda lane: (2 * lane) & 127) + lanes_2d(
        full, lambda lane: (2 * lane + 1) & 127
    )
    lane = lax.broadcasted_iota(jnp.int32, full.shape, 2)
    return jnp.where(lane < x, 0.125 * full, 0.0)


def refine(values, fine, coarse, fine_ref):
    z, y, x = coarse.size
    wide = lanes_2d(values, lambda lane: lax.shift_right_logical(lane, 1))
    fine_ref[0:z, pl.ds(0, y, 2), :] = wide[:, 0:y]
    fine_ref[0:z, pl.ds(1, y, 2), :] = wide[:, 0:y]
    rows = fine_ref[0:z, 0 : fine.tile, :]
    return jnp.broadcast_to(rows[:, None], (z, 2, fine.tile, 128)).reshape(fine.shape)


def ascend(plan, n, width, m_ref, h_ref, e_ref, k_ref, below, v_ref, w_ref):
    lanes = slice(0, width)
    for a, b, c in np.ndindex(n, n, n):
        v_ref[a, b, c] = k_ref[a, b, c, :, lanes] + below(a, b, c)
    for old, new in ((v_ref, w_ref), (w_ref, v_ref)):
        for a, b, c in np.ndindex(n, n, n):
            new[a, b, c] = (
                0.2 * old[a, b, c]
                + e_ref[a, b, c, :, lanes]
                + pull(plan, n, m_ref, old, h_ref, a, b, c, width)
            )


def up_kernel(plan, *refs):
    joined, m0, h0, e0, k0, m1, h1, e1, k1, out = refs[:10]
    v0, w0, v1, w1, window, r2, m2, v2 = refs[10:18]
    fine_refs = refs[18:21]
    tile = plan.tile
    gz, gy, gx = plan.counts
    iz, iy, ix = (lax.axis_index(axis) for axis in AXES)
    inside = inside_mask(plan)

    def unpack(z_block, carry):
        for z in range(4):
            for y_block in range(gy):
                value = jnp.zeros((8, 128), F32)
                for x_block in range(gx):
                    part = joined[(z_block * gy + y_block) * gx + x_block]
                    value = jnp.where(
                        between(32 * x_block, 32 * x_block + 32),
                        pltpu.roll(part, (32 * (x_block - z)) % 128, 1),
                        value,
                    )
                rows = slice(4 * y_block, 4 * y_block + 4)
                r2[4 * z_block + z, rows, :] = value[0:4]
                m2[4 * z_block + z, rows, :] = value[4:8]
        return carry

    lax.fori_loop(0, gz, unpack, 0, unroll=4)
    for ref in fine_refs:
        ref[...] = jnp.zeros(ref.shape, F32)

    levels = [Level(plan, level) for level in range(2, LEVELS + 1)]
    mobility, source = m2[...], r2[...]
    kept = []
    for i, level in enumerate(levels):
        level.prepare(mobility, source)
        if i < len(levels) - 1:
            e = level.first + level.first * 0.2 + level.pull(level.first)
            kept.append(e)
            args = (levels[i + 1], fine_refs[i])
            mobility = coarsen(mobility, *args)
            source = coarsen(level.leftover(e), *args)
    level = levels[-1]
    v = level.first
    for repeat in range(COARSE - 1):
        v = level.relax(v)
    for i in range(len(levels) - 2, -1, -1):
        v = kept[i] + refine(v, levels[i], levels[i + 1], fine_refs[i])
        v = levels[i].relax(levels[i].relax(v))

    v2[...] = jnp.zeros(v2.shape, F32)
    margin = 0 if plan.near == 1 else 8
    v2[pl.ds(HALO, plan.coarse[0]), pl.ds(margin, plan.coarse[1]), :] = v
    planes = []
    for z in range(ZW):
        if plan.near == 1:
            planes.append(v2[4 * iz + z])
        else:
            planes.append(v2[4 * iz + z, pl.ds(4 * iy + 4, tile), :])
    for t in range(3):
        value = jnp.zeros((tile, 128), F32)
        for z in range(ZW):
            offset = lane_of(z) - 128 * t
            low, high = max(offset, 0), min(offset + XW, 128)
            if low < high:
                shift = lax.rem(offset % 128 + HALO - 32 * ix + 256, 128)
                value = jnp.where(
                    between(low, high, tile), pltpu.roll(planes[z], shift, 1), value
                )
        lanes = slice(128 * t, 128 * t + 128)
        window[:, lanes] = jnp.where(inside[:, lanes], value, 0.0)

    below = window[...]

    ascend(plan, 2, LW, m1, h1, e1, k1, lambda a, b, c: below, v1, w1)

    def from_half(a, b, c):
        return v1[a // 2, b // 2, c // 2, :, 0:NARROW]

    ascend(plan, 4, NARROW, m0, h0, e0, k0, from_half, v0, w0)

    lane = lane_iota(tile)
    natural = 32 * (lane & 3) + lax.shift_right_logical(lane, 2)
    starts = [lane_of(z + HALO) + HALO for z in range(4)]
    places_of = [(lane - start) & 127 for start in starts]
    index = [(natural + start) & 127 for start in starts]

    def store(pz, carry):
        for py in range(4):
            parts = [
                [v0[pz, py, px, :, 128 * t : 128 * t + 128] for t in range(2)]
                for px in range(4)
            ]
            parts = [
                [part if px == 0 else pltpu.roll(part, 32 * px, 1) for part in row]
                for px, row in enumerate(parts)
            ]
            for z, start in enumerate(starts):
                low, high = start // 128, (start + 31) // 128
                value = None
                for px in range(4):
                    part = parts[px][low]
                    if low != high:
                        first = (places_of[z] & 31) < 128 - start % 128
                        part = jnp.where(first, part, parts[px][high])
                    turn = lax.shift_right_logical(places_of[z], 5) == px
                    value = part if value is None else jnp.where(turn, part, value)
                value = gather(value, index[z])
                out[4 * z + pz, pl.ds(py, 4, 4), :] = own_rows(plan, value)
        return carry

    lax.fori_loop(0, 4, store, 0, unroll=4)


def call(plan, kernel, outs, scratch, *args):
    return pl.pallas_call(
        kernel,
        out_shape=[jax.ShapeDtypeStruct(shape, F32) for shape in outs],
        scratch_shapes=[pltpu.VMEM(shape, F32) for shape in scratch],
        compiler_params=pltpu.CompilerParams(
            vmem_limit_bytes=(3 * plan.tile + plan.coarse[0] // 4) * 1024 * 1024
        ),
    )(*args)


def solution(mesh):
    plan = Plan(mesh)
    near, tile = plan.near, plan.tile
    z2, y2, x2 = plan.coarse
    full = (4, 4, 4, tile, LW)
    narrow = (4, 4, 4, tile, NARROW)
    half = (2, 2, 2, tile, LW)
    full_rim = (6, 6, 6, tile, LW)
    half_rim = (4, 4, 4, tile, LW)

    def swap(values, *swaps):
        return lax.ppermute(values, AXES, plan.pairs(swaps))

    def on_device(residual, mobility):
        assert residual.shape == (16, 16, 128)
        cells = jnp.stack([residual, mobility])
        even, odd, *sent = call(
            plan,
            lambda *refs: first_kernel(plan, *refs),
            [(16 * (M_DEEP + R_DEEP), 128)] * 2 + [(Y_ROWS, 128)] * near
            + [(4, 16, 128)]
            + [(DIAGONAL_ROWS, 128)] * near,
            [],
            cells,
        )
        arrived = [swap(sent[y], None, y, None) for y in range(near)]
        x_arrived = [swap(sent[near], None, None, 1)]
        x_arrived += [swap(sent[1 + near + y], None, y, 1) for y in range(near)]
        z_own = [swap(odd, 1, None, None), swap(even, 0, None, None)][::-1]
        *beside, even, odd = call(
            plan,
            lambda *refs: edges_kernel(plan, *refs),
            [(2, 16, 16, 128)] * near + [(4, plan.rows, 128)] * 2,
            [],
            cells,
            *arrived,
            *x_arrived,
        )
        edges = [swap(even, None, None, 0), odd]
        sends = call(
            plan,
            lambda *refs: z_pack_kernel(plan, *refs),
            [(plan.payload, 128)] * 2,
            [],
            *beside,
            *edges[::-1],
            *z_own,
        )
        arrived = [swap(sends[1], 1, None, None), swap(sends[0], 0, None, None)][::-1]
        (own,) = call(
            plan,
            lambda *refs: own_kernel(plan, *refs),
            [(2, *narrow)],
            [(2, 16, plan.rows, 128), (2, 4, plan.rows, 128)],
            cells,
            *beside,
            *edges[::-1],
        )
        halo_scratch = [(2, EDGE, plan.rows, 128), (4, plan.rows, 128)]
        (other,) = call(
            plan,
            lambda *refs: place_kernel(plan, *refs),
            [(2, 4, 4, 4, tile, 128)],
            halo_scratch,
            z_own[1],
            arrived[1],
        )
        chunk, *state = call(
            plan,
            lambda *refs: down_kernel(plan, *refs),
            [(plan.devices, 8, 128)] + [full_rim] + [full] * 3 + [half_rim] + [half] * 3,
            [full] * 2
            + [half] * 2
            + halo_scratch,
            own,
            other,
            z_own[0],
            arrived[0],
        )
        joined = lax.all_to_all(chunk, AXES, 0, 0, tiled=True)
        levels = [Level(plan, level) for level in range(2, LEVELS + 1)]
        margin = 0 if near == 1 else 16
        (out,) = call(
            plan,
            lambda *refs: up_kernel(plan, *refs),
            [(16, 16, 128)],
            [narrow] * 2
            + [half] * 2
            + [(tile, LW)]
            + [(z2, y2, 128)] * 2
            + [(z2 + 2 * HALO, y2 + margin, 128)]
            + [
                (fine.size[0], max(fine.tile, 2 * coarse.tile), 128)
                for fine, coarse in zip(levels[:-1], levels[1:])
            ],
            joined,
            *state,
        )
        return out

    spec = P(*AXES)
    return jax.shard_map(
        on_device, mesh=mesh, in_specs=(spec, spec), out_specs=spec, check_vma=False
    )
```
